32 devices in a mesh: seq: 4 (over y, x), chan: 8 (over z, core).
Axes of the slice: x: 2, y: 2, z: 4, core: 2. Of those that a mesh axis runs over, the one named last changes fastest.
Arguments:
- tokens: bfloat16 [14336, 2048], P('seq', 'chan'), may hold values from -6 to 6
- w_query: bfloat16 [2048, 256], replicated, may hold values from -0.125 to 0.125
- w_key: bfloat16 [2048, 256], replicated, may hold values from -0.125 to 0.125
- w_value: bfloat16 [2048, 2048], P(None, 'chan'), may hold values from -0.125 to 0.125
- w_out: bfloat16 [2048, 2048], replicated, may hold values from -0.125 to 0.125
- gain: float32 [2048], replicated, may hold values from 0.1 to 1.9
Outputs:
- mixed: bfloat16 [14336, 2048], P('seq', 'chan')
The draws below stay inside these ranges and needn't reach their ends.
All inputs are finite; a program needn't handle non-finite values.
Results may differ from the reference program's by a relative error of at most 0.019.
Values may be sent and summed in bfloat16 or wider, within the bound.
No kernel may reach another device: no remote copies, remote signals or barrier semaphores. Data moves between devices by JAX's collectives and lax.ppermute only.
A program may use at most 128 MiB of HBM per device.

```python
import jax
import jax.numpy as jnp
from jax import lax

D = 2048
HEADS = 16
FEAT = 16
HEAD_DIM = 128
BLOCK = 896
LENGTH = 14336
HEAD_GROUPS = 8


def steps_of(own_key, extent, cuts, smallest, high):
    def one(position, shards_of):
        draws = jax.random.uniform(jax.random.fold_in(jax.random.fold_in(own_key, 6), position), (shards_of,), jnp.float32, smallest / len(cuts), high / len(cuts))
        return jnp.repeat(jnp.exp(draws), extent[position] // shards_of).reshape((-1,) + (1,) * (len(extent) - position - 1))

    level = one(*cuts[0])
    for cut in cuts[1:]:
        level = level * one(*cut)
    return level


def normal_values(key, extent, width, most, pieces=(), kind=jnp.bfloat16):
    result = jax.random.normal(key, extent, jnp.float32) * width
    if len(pieces) > 0:
        result = steps_of(key, extent, pieces, -0.22, 0.18) * result
    return jnp.clip(result, min=-most, max=most).astype(kind)


def setup_inputs(seed: int = 0) -> dict:
    key_list = jax.random.split(jax.random.key(seed), 7)
    return {
        "tokens": normal_values(key_list[0], (LENGTH, D), 1.0, 6.0, ((0, 4), (1, 8))),
        "w_query": normal_values(key_list[1], (D, HEADS * FEAT), D ** -0.5, 0.125),
        "w_key": normal_values(key_list[2], (D, HEADS * FEAT), D ** -0.5, 0.125),
        "w_value": normal_values(key_list[3], (D, HEADS * HEAD_DIM), D ** -0.5, 0.125, ((1, 8),)),
        "w_out": normal_values(key_list[4], (HEADS * HEAD_DIM, D), (HEADS * HEAD_DIM) ** -0.5, 0.125),
        "gain": jnp.clip(1.0 + 0.18 * jax.random.normal(key_list[5], (HEADS * HEAD_DIM,), jnp.float32), 0.1, 1.9),
    }


def feature_map(rows):
    first = jnp.ones(rows.shape[:-1] + (1,), jnp.float32)
    linear = rows * FEAT ** (-0.25)
    square = (rows[..., :, None] * rows[..., None, :]).reshape(rows.shape[:-1] + (FEAT * FEAT,)) * (2.0 * FEAT) ** (-0.5)
    return jnp.concatenate([first, linear, square], axis=-1)

def reference(tokens, w_query, w_key, w_value, w_out, gain):
    highest = lax.Precision.HIGHEST
    query = jnp.dot(tokens, w_query, preferred_element_type=jnp.float32).astype(jnp.bfloat16)
    key = jnp.dot(tokens, w_key, preferred_element_type=jnp.float32).astype(jnp.bfloat16)
    value = jnp.dot(tokens, w_value, preferred_element_type=jnp.float32).astype(jnp.bfloat16)
    count = LENGTH // BLOCK
    query_blocks = query.reshape(count, BLOCK, HEADS, FEAT)
    key_blocks = key.reshape(count, BLOCK, HEADS, FEAT)
    value_blocks = value.reshape(count, BLOCK, HEADS, HEAD_DIM)
    causal = jnp.arange(BLOCK)[:, None] >= jnp.arange(BLOCK)[None, :]

    def advance(state, block):
        query_now, key_now, value_now = block
        query_f = query_now.astype(jnp.float32)
        key_f = key_now.astype(jnp.float32)
        value_f = value_now.astype(jnp.float32)
        scores = jnp.einsum('thf,shf->hts', query_f, key_f) / jnp.sqrt(jnp.float32(FEAT))
        kernel = 1.0 + scores + 0.5 * scores * scores
        weights = lax.optimization_barrier(jnp.where(causal[None], kernel, 0.0).astype(jnp.bfloat16))
        intra = jnp.einsum('hts,she->the', weights.astype(jnp.float32), value_f)
        inter = jnp.einsum('thp,hpe->the', feature_map(query_f), state, precision=highest)
        grown = state + jnp.einsum('thp,the->hpe', feature_map(key_f), value_f, precision=highest)
        return (grown, intra + inter)
    start = jnp.zeros((HEADS, 1 + FEAT + FEAT * FEAT, HEAD_DIM), jnp.float32)
    final_state, numerator = lax.scan(advance, start, (query_blocks, key_blocks, value_blocks))
    numerator = numerator.reshape(LENGTH, HEADS, HEAD_DIM)
    mean_square = lax.optimization_barrier(jnp.mean(numerator * numerator, axis=-1, keepdims=True))
    hidden = (numerator * lax.rsqrt(mean_square + 1e-05) * gain.reshape(HEADS, HEAD_DIM)).astype(jnp.bfloat16)
    hidden = hidden.reshape(LENGTH, HEADS * HEAD_DIM)
    columns = HEADS * HEAD_DIM // HEAD_GROUPS
    total = jnp.zeros((LENGTH, D), jnp.float32)
    for group in range(HEAD_GROUPS):
        part = jnp.dot(hidden[:, group * columns:(group + 1) * columns], w_out[group * columns:(group + 1) * columns], preferred_element_type=jnp.float32)
        total = total + lax.optimization_barrier(part.astype(jnp.bfloat16)).astype(jnp.float32)
    return total.astype(jnp.bfloat16)
```

```python
import jax
import jax.numpy as jnp
import numpy as np
from jax import lax
from jax.sharding import PartitionSpec as P

HEADS = 16
FEAT = 16
HEAD_DIM = 128
PACKED = 160


def feature_tables():
    first = np.zeros((FEAT, PACKED), np.float32)
    second = np.zeros((FEAT, PACKED), np.float32)
    first_bias = np.zeros((PACKED,), np.float32)
    second_bias = np.zeros((PACKED,), np.float32)
    scale = np.zeros((PACKED,), np.float32)
    first_bias[0] = second_bias[0] = scale[0] = 1.0
    place = 1
    for i in range(FEAT):
        first[i, place] = 1.0
        second_bias[place] = 1.0
        scale[place] = 1.0 / 4.0
        place += 1
    for i in range(FEAT):
        for j in range(i, FEAT):
            first[i, place] = 1.0
            second[j, place] = 1.0
            scale[place] = 1.0 / 32.0 if i == j else 1.0 / 16.0
            place += 1
    return first, second, first_bias, second_bias, scale


def features(rows, scaled):
    first, second, first_bias, second_bias, scale = feature_tables()
    dot = lambda table: jnp.einsum(
        "htf,fp->htp", rows, jnp.asarray(table, jnp.bfloat16), preferred_element_type=jnp.float32
    )
    phi = (dot(first) + first_bias) * (dot(second) + second_bias)
    if scaled:
        phi = phi * scale
    return phi.astype(jnp.bfloat16)


def per_device(tokens, w_query, w_key, w_value, w_out, gain):
    groups = lax.axis_size("chan")
    slabs = lax.axis_size("seq")
    my_slab = lax.axis_index("seq")
    width = tokens.shape[1]
    rows = tokens.shape[0] // groups
    model = w_value.shape[0]
    part = model // slabs
    per_group = HEADS // groups

    value_part = lax.dynamic_slice_in_dim(w_value, my_slab * part, part, 0)
    value_all = lax.all_gather(value_part, ("seq", "chan"), axis=0, tiled=False)
    value_all = value_all.reshape(slabs, groups, part, w_value.shape[1])

    mine = lax.all_to_all(
        tokens.reshape(groups, rows, width), "chan", split_axis=0, concat_axis=0, tiled=True
    )
    x = mine.transpose(1, 0, 2).reshape(rows, model)
    f32 = jnp.float32
    query = jnp.dot(x, w_query, preferred_element_type=f32).astype(jnp.bfloat16)
    key = jnp.dot(x, w_key, preferred_element_type=f32).astype(jnp.bfloat16)
    w_value_full = value_all.transpose(0, 2, 1, 3).reshape(model, model)
    value = jnp.dot(x, w_value_full, preferred_element_type=f32).astype(jnp.bfloat16)
    query = query.reshape(rows, HEADS, FEAT).transpose(1, 0, 2)
    key = key.reshape(rows, HEADS, FEAT).transpose(1, 0, 2)
    value = value.reshape(rows, HEADS, HEAD_DIM).transpose(1, 0, 2)
    phi_key = features(key, False)
    phi_query = features(query, True)
    own = jnp.einsum("htp,hte->hpe", phi_key, value, preferred_element_type=f32)

    own = own.astype(jnp.bfloat16).reshape(groups, per_group, PACKED, HEAD_DIM)
    line = lax.all_to_all(own, "chan", split_axis=0, concat_axis=0, tiled=True).astype(f32)
    total = jnp.sum(line, axis=0)
    before = jnp.concatenate([jnp.zeros_like(line[:1]), jnp.cumsum(line, axis=0)[:-1]], axis=0)
    totals = lax.all_gather(total.astype(jnp.bfloat16), "seq", axis=0, tiled=False).astype(f32)
    earlier = (jnp.arange(slabs) < my_slab).reshape(slabs, 1, 1, 1)
    base = jnp.sum(jnp.where(earlier, totals, 0.0), axis=0)
    prefix = (before + base[None]).astype(jnp.bfloat16)
    prefix = lax.all_to_all(prefix, "chan", split_axis=0, concat_axis=0, tiled=True)
    prefix = prefix.reshape(HEADS, PACKED, HEAD_DIM)

    scores = jnp.einsum("htf,hsf->hts", query, key, preferred_element_type=f32) * FEAT ** (-0.5)
    kernel = 1.0 + scores + 0.5 * scores * scores
    causal = jnp.arange(rows)[:, None] >= jnp.arange(rows)[None, :]
    weights = jnp.where(causal, kernel, 0.0).astype(jnp.bfloat16)
    intra = jnp.einsum("hts,hse->hte", weights, value, preferred_element_type=f32)
    inter = jnp.einsum("htp,hpe->hte", phi_query, prefix, preferred_element_type=f32)
    numerator = intra + inter
    mean_square = jnp.mean(numerator * numerator, axis=-1, keepdims=True)
    hidden = numerator * lax.rsqrt(mean_square + 1e-05) * gain.reshape(HEADS, 1, HEAD_DIM)
    hidden = hidden.astype(jnp.bfloat16).transpose(1, 0, 2).reshape(rows, HEADS * HEAD_DIM)
    out = jnp.dot(hidden, w_out, preferred_element_type=f32).astype(jnp.bfloat16)
    out = out.reshape(rows, groups, width).transpose(1, 0, 2)
    out = lax.all_to_all(out, "chan", split_axis=0, concat_axis=0, tiled=True)
    return out.reshape(groups * rows, width)


def solution(mesh):
    return jax.shard_map(
        per_device,
        mesh=mesh,
        in_specs=(P("seq", "chan"), P(), P(), P(None, "chan"), P(), P()),
        out_specs=P("seq", "chan"),
        check_vma=False,
    )
```

```python
import functools

import jax
import jax.numpy as jnp
import numpy as np
from jax import lax
from jax.experimental import pallas as pl
from jax.experimental.pallas import tpu as pltpu
from jax.sharding import PartitionSpec as P

HEADS = 16
FEAT = 16
HEAD_DIM = 128
PACKED = 160
LANES = 128
HELD = LANES // FEAT
MIB = 1024 * 1024

F32 = jnp.float32
BF16 = jnp.bfloat16
NN = (((1,), (0,)), ((), ()))
NT = (((1,), (1,)), ((), ()))


def dot(a, b, dims=NN):
    return lax.dot_general(a, b, dims, preferred_element_type=F32)


def feature_tables():
    first = np.zeros((FEAT, PACKED), np.float32)
    second = np.zeros((FEAT, PACKED), np.float32)
    first_bias = np.zeros((PACKED,), np.float32)
    second_bias = np.zeros((PACKED,), np.float32)
    scale = np.zeros((PACKED,), np.float32)
    first_bias[0] = second_bias[0] = scale[0] = 1.0
    place = 1
    for i in range(FEAT):
        first[i, place] = 1.0
        second_bias[place] = 1.0
        scale[place] = 1.0 / 4.0
        place += 1
    for i in range(FEAT):
        for j in range(i, FEAT):
            first[i, place] = 1.0
            second[j, place] = 1.0
            scale[place] = 1.0 / 32.0 if i == j else 1.0 / 16.0
            place += 1
    return first, second, first_bias, second_bias, scale


def placed(table):
    out = np.zeros((HELD, LANES, PACKED), np.float32)
    for place in range(HELD):
        out[place, place * FEAT : (place + 1) * FEAT] = table
    return out


def project_kernel(
    per_group, x_ref, wq_ref, wk_ref, wv_ref, ta_ref, tb_ref, bias_ref, q_ref, k_ref, v_ref, s_ref, row_ref
):
    step = pl.program_id(0)
    groups, _, width = x_ref.shape

    @pl.when(step == 0)
    def _():
        for c in range(groups):
            row_ref[:, c * width : (c + 1) * width] = x_ref[c]
        q_ref[...] = dot(row_ref[...], wq_ref[...]).astype(BF16)
        k_ref[...] = dot(row_ref[...], wk_ref[...]).astype(BF16)

    wv = wv_ref[...].reshape(row_ref.shape[1], wv_ref.shape[-1])
    value = dot(row_ref[...], wv).astype(BF16)
    v_ref[...] = value
    for i in range(per_group):
        head = step * per_group + i
        lanes = pl.multiple_of((head // HELD) * LANES, LANES)
        key = k_ref[:, pl.ds(lanes, LANES)]
        place = lax.rem(head, HELD)
        left = dot(ta_ref[place], key, NT) + bias_ref[:, 0:1]
        right = dot(tb_ref[place], key, NT) + bias_ref[:, 1:2]
        phi = (left * right).astype(BF16)
        s_ref[i] = dot(phi, value[:, i * HEAD_DIM : (i + 1) * HEAD_DIM]).astype(BF16)


def local_kernel(per_group, q_ref, k_ref, v_ref, ta_ref, tb_ref, bias_ref, num_ref, phi_ref):
    step = pl.program_id(0)
    rows = q_ref.shape[0]
    half = rows // 2
    for i in range(per_group):
        head = step * per_group + i
        lanes = pl.multiple_of((head // HELD) * LANES, LANES)
        place = lax.rem(head, HELD)
        query = q_ref[:, pl.ds(lanes, LANES)]
        key = k_ref[:, pl.ds(lanes, LANES)]
        left = dot(query, ta_ref[place]) + bias_ref[0:1]
        right = dot(query, tb_ref[place]) + bias_ref[1:2]
        phi_ref[i] = (left * right).astype(BF16)
        lane = lax.broadcasted_iota(jnp.int32, (rows, LANES), 1)
        mine = jnp.where(lane // FEAT == place, query * jnp.asarray(0.25, BF16), jnp.zeros_like(query))
        columns = slice(i * HEAD_DIM, (i + 1) * HEAD_DIM)
        for low in (0, half):
            seen = low + half
            s = dot(mine[low:seen], key[:seen], NT)
            weight = 1.0 + s + 0.5 * s * s
            t_at = lax.broadcasted_iota(jnp.int32, (half, seen), 0) + low
            j_at = lax.broadcasted_iota(jnp.int32, (half, seen), 1)
            weight = jnp.where(t_at >= j_at, weight, 0.0).astype(BF16)
            num_ref[low:seen, columns] = dot(weight, v_ref[:seen, columns])


def prefix_kernel(slab_ref, line_ref, totals_ref, out_ref):
    run = jnp.zeros(line_ref.shape[1:], F32)
    for s in range(totals_ref.shape[0]):
        keep = jnp.where(s < slab_ref[0], 1.0, 0.0)
        run = run + totals_ref[s].astype(F32) * keep
    for c in range(line_ref.shape[0]):
        out_ref[c] = run.astype(BF16)
        run = run + line_ref[c].astype(F32)


def output_kernel(head_steps, out_steps, num_ref, phi_ref, state_ref, gain_ref, w_ref, out_ref, hidden_ref):
    step = pl.program_id(0)
    per_step = HEADS // head_steps

    @pl.when(step < head_steps)
    def _():
        for i in range(per_step):
            columns = slice(i * HEAD_DIM, (i + 1) * HEAD_DIM)
            num = num_ref[:, columns] + dot(phi_ref[i], state_ref[i])
            mean_square = jnp.mean(num * num, axis=1, keepdims=True)
            hidden = num * lax.rsqrt(mean_square + 1e-05) * gain_ref[:, columns]
            at = pl.multiple_of((step * per_step + i) * HEAD_DIM, HEAD_DIM)
            hidden_ref[:, pl.ds(at, HEAD_DIM)] = hidden.astype(BF16)

    @pl.when(step >= head_steps)
    def _():
        width = out_ref.shape[2]
        for c in range(out_ref.shape[0]):
            part = dot(hidden_ref[...], w_ref[:, c * width : (c + 1) * width])
            out_ref[c] = part.astype(BF16)


def whole(shape):
    return pl.BlockSpec(shape, lambda i: (0,) * len(shape))


def params(mib):
    return pltpu.CompilerParams(vmem_limit_bytes=mib * MIB)


def per_device(tokens, w_query, w_key, w_value, w_out, gain):
    groups = lax.axis_size("chan")
    slabs = lax.axis_size("seq")
    my_slab = lax.axis_index("seq")
    width = tokens.shape[1]
    rows = tokens.shape[0] // groups
    model = w_value.shape[0]
    value_width = w_value.shape[1]
    part = model // slabs
    per_group = HEADS // groups
    narrow = w_query.shape[1]

    first, second, first_bias, second_bias, scale = feature_tables()
    key_a = jnp.asarray(placed(first).transpose(0, 2, 1), BF16)
    key_b = jnp.asarray(placed(second).transpose(0, 2, 1), BF16)
    key_bias = jnp.asarray(np.stack([first_bias, second_bias], axis=1))
    query_a = jnp.asarray(placed(first * scale), BF16)
    query_b = jnp.asarray(placed(second), BF16)
    query_bias = jnp.asarray(np.stack([first_bias * scale, second_bias]))

    value_part = lax.dynamic_slice_in_dim(w_value, my_slab * part, part, 0)
    value_all = lax.all_gather(value_part, "chan", axis=0, tiled=False)
    value_all = lax.all_gather(value_all, "seq", axis=0, tiled=False)

    x = lax.all_to_all(
        tokens.reshape(groups, rows, width), "chan", split_axis=0, concat_axis=0, tiled=True
    )
    query, key, value, own = pl.pallas_call(
        functools.partial(project_kernel, per_group),
        grid=(groups,),
        in_specs=[
            whole((groups, rows, width)),
            whole((model, narrow)),
            whole((model, narrow)),
            pl.BlockSpec((slabs, 1, part, value_width), lambda i: (0, i, 0, 0)),
            whole((HELD, PACKED, LANES)),
            whole((HELD, PACKED, LANES)),
            whole((PACKED, 2)),
        ],
        out_specs=[
            whole((rows, narrow)),
            whole((rows, narrow)),
            pl.BlockSpec((rows, value_width), lambda i: (0, i)),
            pl.BlockSpec((per_group, PACKED, HEAD_DIM), lambda i: (i, 0, 0)),
        ],
        out_shape=[
            jax.ShapeDtypeStruct((rows, narrow), BF16),
            jax.ShapeDtypeStruct((rows, narrow), BF16),
            jax.ShapeDtypeStruct((rows, model), BF16),
            jax.ShapeDtypeStruct((HEADS, PACKED, HEAD_DIM), BF16),
        ],
        scratch_shapes=[pltpu.VMEM((rows, model), BF16)],
        compiler_params=params(32),
        cost_estimate=pl.CostEstimate(
            flops=2 * rows * model * (model + 2 * narrow), bytes_accessed=14 * MIB, transcendentals=0
        ),
    )(x, w_query, w_key, value_all, key_a, key_b, key_bias)

    line = lax.all_to_all(
        own.reshape(groups, per_group, PACKED, HEAD_DIM), "chan", split_axis=0, concat_axis=0, tiled=True
    )
    total = jnp.sum(line.astype(F32), axis=0).astype(BF16)
    totals = lax.all_gather(total, "seq", axis=0, tiled=False)
    vmem = pl.BlockSpec(memory_space=pltpu.VMEM)
    prefix = pl.pallas_call(
        prefix_kernel,
        in_specs=[pl.BlockSpec(memory_space=pltpu.SMEM), vmem, vmem],
        out_specs=vmem,
        out_shape=jax.ShapeDtypeStruct(line.shape, BF16),
    )(my_slab.reshape(1), line, totals)
    prefix = lax.all_to_all(prefix, "chan", split_axis=0, concat_axis=0, tiled=True)
    prefix = prefix.reshape(HEADS, PACKED, HEAD_DIM)

    local, phi = pl.pallas_call(
        functools.partial(local_kernel, per_group),
        grid=(groups,),
        in_specs=[
            whole((rows, narrow)),
            whole((rows, narrow)),
            pl.BlockSpec((rows, value_width), lambda i: (0, i)),
            whole((HELD, LANES, PACKED)),
            whole((HELD, LANES, PACKED)),
            whole((2, PACKED)),
        ],
        out_specs=[
            pl.BlockSpec((rows, value_width), lambda i: (0, i)),
            pl.BlockSpec((per_group, rows, PACKED), lambda i: (i, 0, 0)),
        ],
        out_shape=[
            jax.ShapeDtypeStruct((rows, model), F32),
            jax.ShapeDtypeStruct((HEADS, rows, PACKED), BF16),
        ],
        compiler_params=params(32),
        cost_estimate=pl.CostEstimate(
            flops=HEADS * rows * rows * 600, bytes_accessed=8 * MIB, transcendentals=0
        ),
    )(query, key, value, query_a, query_b, query_bias)

    head_steps = 4
    out_steps = 4
    per_step = HEADS // head_steps
    per_out = groups // out_steps
    out = pl.pallas_call(
        functools.partial(output_kernel, head_steps, out_steps),
        grid=(head_steps + out_steps,),
        in_specs=[
            pl.BlockSpec((rows, per_step * HEAD_DIM), lambda i: (0, jnp.minimum(i, head_steps - 1))),
            pl.BlockSpec((per_step, rows, PACKED), lambda i: (jnp.minimum(i, head_steps - 1), 0, 0)),
            pl.BlockSpec((per_step, PACKED, HEAD_DIM), lambda i: (jnp.minimum(i, head_steps - 1), 0, 0)),
            pl.BlockSpec((1, per_step * HEAD_DIM), lambda i: (0, jnp.minimum(i, head_steps - 1))),
            pl.BlockSpec((model, per_out * width), lambda i: (0, jnp.maximum(i - head_steps, 0))),
        ],
        out_specs=pl.BlockSpec((per_out, rows, width), lambda i: (jnp.maximum(i - head_steps, 0), 0, 0)),
        out_shape=jax.ShapeDtypeStruct((groups, rows, width), BF16),
        scratch_shapes=[pltpu.VMEM((rows, model), BF16)],
        compiler_params=params(32),
        cost_estimate=pl.CostEstimate(
            flops=2 * rows * model * model, bytes_accessed=16 * MIB, transcendentals=0
        ),
    )(local, phi, prefix, gain.reshape(1, HEADS * HEAD_DIM), w_out)
    out = lax.all_to_all(out, "chan", split_axis=0, concat_axis=0, tiled=True)
    return out.reshape(groups * rows, width)


def solution(mesh):
    return jax.shard_map(
        per_device,
        mesh=mesh,
        in_specs=(P("seq", "chan"), P(), P(), P(None, "chan"), P(), P()),
        out_specs=P("seq", "chan"),
        check_vma=False,
    )
```

```python
import jax
import jax.numpy as jnp
import numpy as np
from jax import lax
from jax.experimental import pallas as pl
from jax.experimental.pallas import tpu as pltpu
from jax.sharding import PartitionSpec as P

HEADS = 16
FEAT = 16
HEAD_DIM = 128
PACKED = 160
LANES = 128
HELD = LANES // FEAT
MIB = 1024 * 1024

F32 = jnp.float32
BF16 = jnp.bfloat16
NN = (((1,), (0,)), ((), ()))
NT = (((1,), (1,)), ((), ()))


def dot(a, b, dims=NN):
    return lax.dot_general(a, b, dims, preferred_element_type=F32)


def feature_tables():
    first = np.zeros((FEAT, PACKED), np.float32)
    second = np.zeros((FEAT, PACKED), np.float32)
    first_bias = np.zeros((PACKED,), np.float32)
    second_bias = np.zeros((PACKED,), np.float32)
    scale = np.zeros((PACKED,), np.float32)
    first_bias[0] = second_bias[0] = scale[0] = 1.0
    place = 1
    for i in range(FEAT):
        first[i, place] = 1.0
        second_bias[place] = 1.0
        scale[place] = 1.0 / 4.0
        place += 1
    for i in range(FEAT):
        for j in range(i, FEAT):
            first[i, place] = 1.0
            second[j, place] = 1.0
            scale[place] = 1.0 / 32.0 if i == j else 1.0 / 16.0
            place += 1
    return first, second, first_bias, second_bias, scale


def placed(table):
    out = np.zeros((HELD, LANES, PACKED), np.float32)
    for place in range(HELD):
        out[place, place * FEAT : (place + 1) * FEAT] = table
    return out


def project_kernel(
    core_ref,
    per_group,
    first_mine,
    second_mine,
    first_other,
    second_other,
    wq_ref,
    wk_ref,
    wv_ref,
    ta_ref,
    tb_ref,
    bias_ref,
    q_ref,
    k_ref,
    v_ref,
    early_ref,
    total_ref,
    row_ref,
):
    step = pl.program_id(0)
    core = core_ref[0]
    layers, rows, width = first_mine.shape

    @pl.when(step == 0)
    def _():
        for chunk, (mine, other) in enumerate(
            ((first_mine, first_other), (second_mine, second_other))
        ):
            at = slice(chunk * rows, (chunk + 1) * rows)
            for z in range(layers):
                here = pl.multiple_of((2 * z + core) * width, width)
                there = pl.multiple_of((2 * z + 1 - core) * width, width)
                row_ref[at, pl.ds(here, width)] = mine[z]
                row_ref[at, pl.ds(there, width)] = other[z]
            q_ref[chunk] = dot(row_ref[at, :], wq_ref[...]).astype(BF16)
            k_ref[chunk] = dot(row_ref[at, :], wk_ref[...]).astype(BF16)

    wv = wv_ref[...].reshape(row_ref.shape[1], wv_ref.shape[-1])
    for chunk in range(2):
        value = dot(row_ref[chunk * rows : (chunk + 1) * rows, :], wv).astype(BF16)
        v_ref[chunk] = value
        for i in range(per_group):
            head = (2 * step + core) * per_group + i
            lanes = pl.multiple_of((head // HELD) * LANES, LANES)
            key = k_ref[chunk, :, pl.ds(lanes, LANES)]
            place = lax.rem(head, HELD)
            left = dot(ta_ref[place], key, NT) + bias_ref[:, 0:1]
            right = dot(tb_ref[place], key, NT) + bias_ref[:, 1:2]
            phi = (left * right).astype(BF16)
            state = dot(phi, value[:, i * HEAD_DIM : (i + 1) * HEAD_DIM])
            if chunk == 0:
                early_ref[i] = state.astype(BF16)
                total_ref[i] = state
            else:
                total_ref[i] = total_ref[i] + state


def local_kernel(
    core_ref, per_group, q_ref, k_ref, v_ref, early_ref, ta_ref, tb_ref, bias_ref, num_ref, phi_ref
):
    chunk = pl.program_id(0)
    step = pl.program_id(1)
    rows = q_ref.shape[1]
    half = rows // 2
    for i in range(per_group):
        head = (2 * step + core_ref[0]) * per_group + i
        lanes = pl.multiple_of((head // HELD) * LANES, LANES)
        place = lax.rem(head, HELD)
        query = q_ref[0, :, pl.ds(lanes, LANES)]
        key = k_ref[0, :, pl.ds(lanes, LANES)]
        left = dot(query, ta_ref[place]) + bias_ref[0:1]
        right = dot(query, tb_ref[place]) + bias_ref[1:2]
        phi_ref[0, i] = (left * right).astype(BF16)
        lane = lax.broadcasted_iota(jnp.int32, (rows, LANES), 1)
        mine = jnp.where(lane // FEAT == place, query * jnp.asarray(0.25, BF16), jnp.zeros_like(query))
        columns = slice(i * HEAD_DIM, (i + 1) * HEAD_DIM)
        for low in (0, half):
            seen = low + half
            s = dot(mine[low:seen], key[:seen], NT)
            weight = 1.0 + s + 0.5 * s * s
            t_at = lax.broadcasted_iota(jnp.int32, (half, seen), 0) + low
            j_at = lax.broadcasted_iota(jnp.int32, (half, seen), 1)
            weight = jnp.where(t_at >= j_at, weight, 0.0).astype(BF16)
            num_ref[0, low:seen, columns] = dot(weight, v_ref[0, :seen, columns])

        @pl.when(chunk == 1)
        def _():
            num_ref[0, :, columns] += dot(phi_ref[0, i], early_ref[i])


def prefix_kernel(slab_ref, line_ref, totals_ref, out_ref):
    run = jnp.zeros(line_ref.shape[1:], F32)
    for s in range(totals_ref.shape[0]):
        keep = jnp.where(s < slab_ref[0], 1.0, 0.0)
        run = run + totals_ref[s].astype(F32) * keep
    for c in range(line_ref.shape[0]):
        out_ref[c] = run.astype(BF16)
        run = run + line_ref[c].astype(F32)


def hidden_kernel(chunk_ref, num_ref, phi_ref, state_ref, gain_ref, out_ref):
    for i in range(phi_ref.shape[1]):
        columns = slice(i * HEAD_DIM, (i + 1) * HEAD_DIM)
        num = num_ref[0, :, columns] + dot(phi_ref[0, i], state_ref[i])
        mean_square = jnp.mean(num * num, axis=1, keepdims=True)
        hidden = num * lax.rsqrt(mean_square + 1e-05) * gain_ref[:, columns]
        out_ref[:, columns] = hidden.astype(BF16)


def output_kernel(core_ref, layers, mine_ref, other_ref, w_ref, out_ref, hidden_ref):
    core = core_ref[0]

    @pl.when(pl.program_id(0) == 0)
    def _():
        block = mine_ref.shape[1] // layers
        for z in range(layers):
            columns = slice(z * block, (z + 1) * block)
            here = pl.multiple_of((2 * z + core) * block, block)
            there = pl.multiple_of((2 * z + 1 - core) * block, block)
            hidden_ref[:, pl.ds(here, block)] = mine_ref[:, columns]
            hidden_ref[:, pl.ds(there, block)] = other_ref[:, columns]

    width = out_ref.shape[2]
    for c in range(out_ref.shape[0]):
        part = dot(hidden_ref[...], w_ref[:, c * width : (c + 1) * width])
        out_ref[c] = part.astype(BF16)


def whole(shape):
    return pl.BlockSpec(shape, lambda *_: (0,) * len(shape))


def params(mib):
    return pltpu.CompilerParams(vmem_limit_bytes=mib * MIB)


def call(kernel, scalar, grid, in_specs, out_specs, out_shape, args, flops, scratch=(), mib=60):
    return pl.pallas_call(
        kernel,
        grid_spec=pltpu.PrefetchScalarGridSpec(
            num_scalar_prefetch=1,
            grid=grid,
            in_specs=in_specs,
            out_specs=out_specs,
            scratch_shapes=list(scratch),
        ),
        out_shape=out_shape,
        compiler_params=params(mib),
        cost_estimate=pl.CostEstimate(flops=flops, bytes_accessed=12 * MIB, transcendentals=0),
    )(scalar, *args)


def per_device(tokens, w_query, w_key, w_value, w_out, gain):
    slabs = lax.axis_size("seq")
    layers = lax.axis_size("z")
    groups = 2 * layers
    my_slab = lax.axis_index("seq")
    core = lax.axis_index("core").astype(jnp.int32)
    which = core.reshape(1)
    width = tokens.shape[1]
    rows = tokens.shape[0] // groups
    model, value_width = w_value.shape
    part = model // slabs
    per_group = HEADS // groups
    heads = HEADS // 2
    narrow = w_query.shape[1]
    swap = [(0, 1), (1, 0)]

    first, second, first_bias, second_bias, scale = feature_tables()
    key_a = jnp.asarray(placed(first).transpose(0, 2, 1), BF16)
    key_b = jnp.asarray(placed(second).transpose(0, 2, 1), BF16)
    key_bias = jnp.asarray(np.stack([first_bias, second_bias], axis=1))
    query_a = jnp.asarray(placed(first * scale), BF16)
    query_b = jnp.asarray(placed(second), BF16)
    query_bias = jnp.asarray(np.stack([first_bias * scale, second_bias]))
    gain_mine = lax.dynamic_index_in_dim(gain.reshape(layers, 2, value_width), core, 1, False)
    gain_mine = gain_mine.reshape(1, layers * value_width)

    value_part = lax.dynamic_slice_in_dim(w_value, my_slab * part, part, 0)
    value_all = lax.all_gather(value_part, "z", axis=0, tiled=False)
    value_all = lax.all_gather(value_all, "seq", axis=0, tiled=False)

    blocks = tokens.reshape(layers, 2, rows, width)
    mine = [
        lax.all_to_all(blocks[:, chunk], "z", split_axis=0, concat_axis=0, tiled=True)
        for chunk in range(2)
    ]
    other = [lax.ppermute(half, "core", swap) for half in mine]

    query, key, value, early, total = call(
        lambda core_ref, *refs: project_kernel(core_ref, per_group, *refs),
        which,
        (layers,),
        [whole((layers, rows, width))] * 4
        + [
            whole((model, narrow)),
            whole((model, narrow)),
            pl.BlockSpec((slabs, 1, part, value_width), lambda i, _: (0, i, 0, 0)),
            whole((HELD, PACKED, LANES)),
            whole((HELD, PACKED, LANES)),
            whole((PACKED, 2)),
        ],
        [
            whole((2, rows, narrow)),
            whole((2, rows, narrow)),
            pl.BlockSpec((2, rows, value_width), lambda i, _: (0, 0, i)),
            pl.BlockSpec((per_group, PACKED, HEAD_DIM), lambda i, _: (i, 0, 0)),
            pl.BlockSpec((per_group, PACKED, HEAD_DIM), lambda i, _: (i, 0, 0)),
        ],
        [
            jax.ShapeDtypeStruct((2, rows, narrow), BF16),
            jax.ShapeDtypeStruct((2, rows, narrow), BF16),
            jax.ShapeDtypeStruct((2, rows, layers * value_width), BF16),
            jax.ShapeDtypeStruct((heads, PACKED, HEAD_DIM), BF16),
            jax.ShapeDtypeStruct((heads, PACKED, HEAD_DIM), F32),
        ],
        (mine[0], mine[1], other[0], other[1], w_query, w_key, value_all, key_a, key_b, key_bias),
        4 * rows * model * (model // 2 + 2 * narrow),
        [pltpu.VMEM((2 * rows, model), BF16)],
    )

    own = total.astype(BF16).reshape(layers, per_group, PACKED, HEAD_DIM)
    line = lax.all_to_all(own, "z", split_axis=0, concat_axis=0, tiled=True)
    slab_total = jnp.sum(line.astype(F32), axis=0).astype(BF16)
    totals = lax.all_gather(slab_total, "seq", axis=0, tiled=False)
    vmem = pl.BlockSpec(memory_space=pltpu.VMEM)
    prefix = pl.pallas_call(
        prefix_kernel,
        in_specs=[pl.BlockSpec(memory_space=pltpu.SMEM), vmem, vmem],
        out_specs=vmem,
        out_shape=jax.ShapeDtypeStruct(line.shape, BF16),
    )(my_slab.reshape(1), line, totals)
    prefix = lax.all_to_all(prefix, "z", split_axis=0, concat_axis=0, tiled=True)
    prefix = prefix.reshape(heads, PACKED, HEAD_DIM)

    local, phi = call(
        lambda core_ref, *refs: local_kernel(core_ref, per_group, *refs),
        which,
        (2, layers),
        [
            pl.BlockSpec((1, rows, narrow), lambda c, i, _: (c, 0, 0)),
            pl.BlockSpec((1, rows, narrow), lambda c, i, _: (c, 0, 0)),
            pl.BlockSpec((1, rows, value_width), lambda c, i, _: (c, 0, i)),
            pl.BlockSpec((per_group, PACKED, HEAD_DIM), lambda c, i, _: (i, 0, 0)),
            whole((HELD, LANES, PACKED)),
            whole((HELD, LANES, PACKED)),
            whole((2, PACKED)),
        ],
        [
            pl.BlockSpec((1, rows, value_width), lambda c, i, _: (c, 0, i)),
            pl.BlockSpec((1, per_group, rows, PACKED), lambda c, i, _: (c, i, 0, 0)),
        ],
        [
            jax.ShapeDtypeStruct((2, rows, layers * value_width), F32),
            jax.ShapeDtypeStruct((2, heads, rows, PACKED), BF16),
        ],
        (query, key, value, early, query_a, query_b, query_bias),
        heads * rows * rows * 1200,
    )

    per_step = heads // 2

    def hidden(chunk):
        return call(
            hidden_kernel,
            chunk.reshape(1),
            (2,),
            [
                pl.BlockSpec((1, rows, per_step * HEAD_DIM), lambda i, c: (c[0], 0, i)),
                pl.BlockSpec((1, per_step, rows, PACKED), lambda i, c: (c[0], i, 0, 0)),
                pl.BlockSpec((per_step, PACKED, HEAD_DIM), lambda i, c: (i, 0, 0)),
                pl.BlockSpec((1, per_step * HEAD_DIM), lambda i, c: (0, i)),
            ],
            pl.BlockSpec((rows, per_step * HEAD_DIM), lambda i, c: (0, i)),
            jax.ShapeDtypeStruct((rows, heads * HEAD_DIM), BF16),
            (local, phi, prefix, gain_mine),
            rows * heads * HEAD_DIM * 600,
        )

    received = lax.ppermute(hidden(1 - core), "core", swap)
    kept = hidden(core)
    steps = 4
    per_out = groups // steps
    out = call(
        lambda core_ref, *refs: output_kernel(core_ref, layers, *refs),
        which,
        (steps,),
        [
            whole((rows, heads * HEAD_DIM)),
            whole((rows, heads * HEAD_DIM)),
            pl.BlockSpec((model, per_out * width), lambda i, _: (0, i)),
        ],
        pl.BlockSpec((per_out, rows, width), lambda i, _: (i, 0, 0)),
        jax.ShapeDtypeStruct((groups, rows, width), BF16),
        (kept, received, w_out),
        2 * rows * model * model,
        [pltpu.VMEM((rows, model), BF16)],
    )
    out = lax.all_to_all(out, ("z", "core"), split_axis=0, concat_axis=0, tiled=True)
    return out.reshape(groups * rows, width)


def solution(mesh):
    slabs, groups = mesh.shape["seq"], mesh.shape["chan"]
    split = jax.sharding.Mesh(mesh.devices.reshape(slabs, groups // 2, 2), ("seq", "z", "core"))
    chan = ("z", "core")
    return jax.shard_map(
        per_device,
        mesh=split,
        in_specs=(P("seq", chan), P(), P(), P(None, chan), P(), P()),
        out_specs=P("seq", chan),
        check_vma=False,
    )
```

```python
import jax
import jax.numpy as jnp
import numpy as np
from jax import lax
from jax.experimental import pallas as pl
from jax.experimental.pallas import tpu as pltpu
from jax.sharding import PartitionSpec as P

HEADS = 16
FEAT = 16
HEAD_DIM = 128
PACKED = 160
LANES = 128
HELD = LANES // FEAT
MIB = 1024 * 1024

F32 = jnp.float32
BF16 = jnp.bfloat16
NN = (((1,), (0,)), ((), ()))
NT = (((1,), (1,)), ((), ()))


def dot(a, b, dims=NN):
    return lax.dot_general(a, b, dims, preferred_element_type=F32)


def feature_tables():
    first = np.zeros((FEAT, PACKED), np.float32)
    second = np.zeros((FEAT, PACKED), np.float32)
    first_bias = np.zeros((PACKED,), np.float32)
    second_bias = np.zeros((PACKED,), np.float32)
    scale = np.zeros((PACKED,), np.float32)
    first_bias[0] = second_bias[0] = scale[0] = 1.0
    place = 1
    for i in range(FEAT):
        first[i, place] = 1.0
        second_bias[place] = 1.0
        scale[place] = 1.0 / 4.0
        place += 1
    for i in range(FEAT):
        for j in range(i, FEAT):
            first[i, place] = 1.0
            second[j, place] = 1.0
            scale[place] = 1.0 / 32.0 if i == j else 1.0 / 16.0
            place += 1
    return first, second, first_bias, second_bias, scale


def placed(table):
    out = np.zeros((HELD, LANES, PACKED), np.float32)
    for place in range(HELD):
        out[place, place * FEAT : (place + 1) * FEAT] = table
    return out


def stacked(table, per_group):
    every = placed(table).transpose(0, 2, 1)
    own = [[p for p in range(HELD) if (p // per_group) % 2 == core] for core in range(2)]
    return np.stack([every[places].reshape(-1, LANES) for places in own])


def project_kernel(
    at_ref,
    per_group,
    counts,
    mine_ref,
    other_ref,
    wq_ref,
    wk_ref,
    table_ref,
    bias_ref,
    *rest,
):
    n_weights = sum(counts)
    weights = rest[:n_weights]
    q_ref, k_ref, v_ref, early_ref, total_ref, row_ref, w_ref, phi_ref, sems = rest[n_weights:]
    core, layer, slab = at_ref[0], at_ref[1], at_ref[2]
    layers, both, width = mine_ref.shape
    rows = both // 2
    copies = []
    place = 0
    for d, count in enumerate(counts):
        for m in range(count):
            source = weights[place]
            part = source.shape[0]
            start = 0 if count == 1 else pl.multiple_of((slab ^ m) * part, part)
            copy = pltpu.make_async_copy(source, w_ref.at[d, pl.ds(start, part)], sems.at[place])
            copy.start()
            copies.append((d, copy))
            place += 1

    for z in range(layers):
        here = pl.multiple_of((2 * z + core) * width, width)
        there = pl.multiple_of((2 * z + 1 - core) * width, width)
        row_ref[:, pl.ds(here, width)] = mine_ref[z]
        row_ref[:, pl.ds(there, width)] = other_ref[z]
    q = dot(row_ref[...], wq_ref[...]).astype(BF16)
    k = dot(row_ref[...], wk_ref[...]).astype(BF16)
    half = table_ref.shape[1] // 2
    for chunk in range(2):
        at = slice(chunk * rows, (chunk + 1) * rows)
        q_ref[chunk] = q[at]
        k_ref[chunk] = k[at]
        for lanes in range(0, k.shape[1], LANES):
            product = dot(table_ref[0], k[at, lanes : lanes + LANES], NT)
            left = product[:half] + bias_ref[:, 0:1]
            right = product[half:] + bias_ref[:, 1:2]
            to = (lanes // LANES) * half
            phi_ref[chunk, to : to + half, :] = (left * right).astype(BF16)

    block = v_ref.shape[2] // layers
    for d in range(layers):
        for slot, copy in copies:
            if slot == d:
                copy.wait()
        z = lax.rem(layer + d, layers)
        for chunk in range(2):
            value = dot(row_ref[chunk * rows : (chunk + 1) * rows, :], w_ref[d]).astype(BF16)
            v_ref[chunk, :, pl.ds(pl.multiple_of(z * block, block), block)] = value
            for i in range(per_group):
                head = z * per_group + i
                phi = phi_ref[chunk, pl.ds(pl.multiple_of(head * PACKED, PACKED), PACKED), :]
                state = dot(phi, value[:, i * HEAD_DIM : (i + 1) * HEAD_DIM])
                if chunk == 0:
                    early_ref[head] = state.astype(BF16)
                    first = state if i == 0 else jnp.concatenate([first, state], axis=0)
                else:
                    total = first[i * PACKED : (i + 1) * PACKED] + state
                    total_ref[head] = total.astype(BF16)


def local_kernel(
    core_ref, per_group, offset, q_ref, k_ref, v_ref, early_ref, ta_ref, tb_ref, bias_ref, num_ref, phi_ref
):
    chunk = pl.program_id(0)
    step = pl.program_id(1) + offset
    rows = q_ref.shape[1]
    half = rows // 2
    for i in range(per_group):
        head = (2 * step + core_ref[0]) * per_group + i
        lanes = pl.multiple_of((head // HELD) * LANES, LANES)
        place = lax.rem(head, HELD)
        query = q_ref[0, :, pl.ds(lanes, LANES)]
        key = k_ref[0, :, pl.ds(lanes, LANES)]
        left = dot(query, ta_ref[place]) + bias_ref[0:1]
        right = dot(query, tb_ref[place]) + bias_ref[1:2]
        phi_ref[0, i] = (left * right).astype(BF16)
        lane = lax.broadcasted_iota(jnp.int32, (rows, LANES), 1)
        mine = jnp.where(lane // FEAT == place, query * jnp.asarray(0.25, BF16), jnp.zeros_like(query))
        columns = slice(i * HEAD_DIM, (i + 1) * HEAD_DIM)
        for low in (0, half):
            seen = low + half
            s = dot(mine[low:seen], key[:seen], NT)
            weight = 1.0 + s + 0.5 * s * s
            t_at = lax.broadcasted_iota(jnp.int32, (half, seen), 0) + low
            j_at = lax.broadcasted_iota(jnp.int32, (half, seen), 1)
            weight = jnp.where(t_at >= j_at, weight, 0.0).astype(BF16)
            num_ref[0, low:seen, columns] = dot(weight, v_ref[0, :seen, columns])

        @pl.when(chunk == 1)
        def _():
            num_ref[0, :, columns] += dot(phi_ref[0, i], early_ref[i])


def prefix_kernel(slab_ref, line_ref, totals_ref, out_ref):
    run = jnp.zeros(line_ref.shape[1:], F32)
    for s in range(totals_ref.shape[0]):
        keep = jnp.where(s < slab_ref[0], 1.0, 0.0)
        run = run + totals_ref[s].astype(F32) * keep
    for c in range(line_ref.shape[0]):
        out_ref[c] = run.astype(BF16)
        run = run + line_ref[c].astype(F32)


def hidden_kernel(chunk_ref, num_a, num_b, phi_a, phi_b, state_ref, gain_ref, out_ref):
    held = phi_a.shape[1]
    for i in range(2 * held):
        columns = slice(i * HEAD_DIM, (i + 1) * HEAD_DIM)
        num_ref, phi_ref = (num_a, phi_a) if i < held else (num_b, phi_b)
        at = (i % held) * HEAD_DIM
        num = num_ref[0, :, at : at + HEAD_DIM] + dot(phi_ref[0, i % held], state_ref[i])
        mean_square = jnp.mean(num * num, axis=1, keepdims=True)
        hidden = num * lax.rsqrt(mean_square + 1e-05) * gain_ref[:, columns]
        out_ref[:, columns] = hidden.astype(BF16)


def output_kernel(core_ref, layers, mine_ref, other_ref, w_ref, out_ref, hidden_ref):
    core = core_ref[0]

    @pl.when(pl.program_id(0) == 0)
    def _():
        block = mine_ref.shape[1] // layers
        for z in range(layers):
            columns = slice(z * block, (z + 1) * block)
            here = pl.multiple_of((2 * z + core) * block, block)
            there = pl.multiple_of((2 * z + 1 - core) * block, block)
            hidden_ref[:, pl.ds(here, block)] = mine_ref[:, columns]
            hidden_ref[:, pl.ds(there, block)] = other_ref[:, columns]

    width = out_ref.shape[2]
    for c in range(out_ref.shape[0]):
        part = dot(hidden_ref[...], w_ref[:, c * width : (c + 1) * width])
        out_ref[c] = part.astype(BF16)


def whole(shape):
    return pl.BlockSpec(shape, lambda *_: (0,) * len(shape))


def params(mib):
    return pltpu.CompilerParams(vmem_limit_bytes=mib * MIB)


def call(kernel, scalar, grid, in_specs, out_specs, out_shape, args, flops, scratch=(), mib=60):
    return pl.pallas_call(
        kernel,
        grid_spec=pltpu.PrefetchScalarGridSpec(
            num_scalar_prefetch=1,
            grid=grid,
            in_specs=in_specs,
            out_specs=out_specs,
            scratch_shapes=list(scratch),
        ),
        out_shape=out_shape,
        compiler_params=params(mib),
        cost_estimate=pl.CostEstimate(flops=flops, bytes_accessed=12 * MIB, transcendentals=0),
    )(scalar, *args)


def per_device(tokens, w_query, w_key, w_value, w_out, gain):
    slabs = lax.axis_size("seq")
    layers = lax.axis_size("z")
    groups = 2 * layers
    my_slab = lax.axis_index("seq")
    core = lax.axis_index("core").astype(jnp.int32)
    layer = lax.axis_index("z").astype(jnp.int32)
    which = core.reshape(1)
    width = tokens.shape[1]
    rows = tokens.shape[0] // groups
    model, value_width = w_value.shape
    part = model // slabs
    per_group = HEADS // groups
    heads = HEADS // 2
    narrow = w_query.shape[1]
    swap = [(0, 1), (1, 0)]

    first, second, first_bias, second_bias, scale = feature_tables()
    sides = [stacked(first, per_group), stacked(second, per_group)]
    key_table = jnp.asarray(np.concatenate(sides, axis=1), BF16)
    repeat = HELD // 2
    key_bias = jnp.asarray(np.stack([np.tile(first_bias, repeat), np.tile(second_bias, repeat)], axis=1))
    query_a = jnp.asarray(placed(first * scale), BF16)
    query_b = jnp.asarray(placed(second), BF16)
    query_bias = jnp.asarray(np.stack([first_bias * scale, second_bias]))
    gain_mine = lax.dynamic_index_in_dim(gain.reshape(layers, 2, value_width), core, 1, False)
    gain_mine = gain_mine.reshape(1, layers * value_width)

    mine = lax.all_to_all(
        tokens.reshape(layers, 2 * rows, width), "z", split_axis=0, concat_axis=0, tiled=True
    )
    other = lax.ppermute(mine, "core", swap)

    value_part = lax.dynamic_slice_in_dim(w_value, my_slab * part, part, 0)
    up, down = {0: value_part}, {0: value_part}
    for k in range(1, layers):
        up[k] = lax.ppermute(up[k - 1], "z", [(z, z + 1) for z in range(k - 1, layers - 1)])
        down[k] = lax.ppermute(down[k - 1], "z", [(z, z - 1) for z in range(1, layers - k + 1)])
    weights, counts = [w_value], [1]
    for d in range(1, layers):
        slot = jnp.where(layer + d < layers, down[d], up[layers - d])
        if slabs == 4:
            weights.append(slot)
            for m in range(1, slabs):
                weights.append(lax.ppermute(slot, "seq", [(s, s ^ m) for s in range(slabs)]))
            counts.append(slabs)
        else:
            weights.append(lax.all_gather(slot, "seq", axis=0, tiled=True))
            counts.append(1)

    anywhere = pl.BlockSpec(memory_space=pl.ANY)
    query, key, value, early, total = call(
        lambda at_ref, *refs: project_kernel(at_ref, per_group, counts, *refs),
        jnp.stack([core, layer, my_slab.astype(jnp.int32)]),
        (1,),
        [
            whole((layers, 2 * rows, width)),
            whole((layers, 2 * rows, width)),
            whole((model, narrow)),
            whole((model, narrow)),
            pl.BlockSpec((1,) + key_table.shape[1:], lambda i, at: (at[0], 0, 0)),
            whole(key_bias.shape),
        ]
        + [anywhere] * len(weights),
        [
            whole((2, rows, narrow)),
            whole((2, rows, narrow)),
            whole((2, rows, layers * value_width)),
            whole((heads, PACKED, HEAD_DIM)),
            whole((heads, PACKED, HEAD_DIM)),
        ],
        [
            jax.ShapeDtypeStruct((2, rows, narrow), BF16),
            jax.ShapeDtypeStruct((2, rows, narrow), BF16),
            jax.ShapeDtypeStruct((2, rows, layers * value_width), BF16),
            jax.ShapeDtypeStruct((heads, PACKED, HEAD_DIM), BF16),
            jax.ShapeDtypeStruct((heads, PACKED, HEAD_DIM), BF16),
        ],
        (mine, other, w_query, w_key, key_table, key_bias, *weights),
        4 * rows * model * (model // 2 + 2 * narrow),
        [
            pltpu.VMEM((2 * rows, model), BF16),
            pltpu.VMEM((layers, model, value_width), BF16),
            pltpu.VMEM((2, heads * PACKED, rows), BF16),
            pltpu.SemaphoreType.DMA((len(weights),)),
        ],
    )

    def local(part_of_heads):
        offset = part_of_heads * (layers // 2)
        return call(
            lambda core_ref, *refs: local_kernel(core_ref, per_group, offset, *refs),
            which,
            (2, layers // 2),
            [
                pl.BlockSpec((1, rows, narrow), lambda c, i, _: (c, 0, 0)),
                pl.BlockSpec((1, rows, narrow), lambda c, i, _: (c, 0, 0)),
                pl.BlockSpec((1, rows, value_width), lambda c, i, _: (c, 0, i + offset)),
                pl.BlockSpec((per_group, PACKED, HEAD_DIM), lambda c, i, _: (i + offset, 0, 0)),
                whole((HELD, LANES, PACKED)),
                whole((HELD, LANES, PACKED)),
                whole((2, PACKED)),
            ],
            [
                pl.BlockSpec((1, rows, value_width), lambda c, i, _: (c, 0, i)),
                pl.BlockSpec((1, per_group, rows, PACKED), lambda c, i, _: (c, i, 0, 0)),
            ],
            [
                jax.ShapeDtypeStruct((2, rows, layers * value_width // 2), F32),
                jax.ShapeDtypeStruct((2, heads // 2, rows, PACKED), BF16),
            ],
            (query, key, value, early, query_a, query_b, query_bias),
            heads * rows * rows * 600,
        )

    own = total.reshape(layers, per_group, PACKED, HEAD_DIM)
    line = lax.all_to_all(own, "z", split_axis=0, concat_axis=0, tiled=True)
    num_a, phi_a = local(0)
    line, num_a, phi_a = lax.optimization_barrier((line, num_a, phi_a))
    slab_total = jnp.sum(line.astype(F32), axis=0).astype(BF16)
    totals = lax.all_gather(slab_total, "seq", axis=0, tiled=False)
    vmem = pl.BlockSpec(memory_space=pltpu.VMEM)
    prefix = pl.pallas_call(
        prefix_kernel,
        in_specs=[pl.BlockSpec(memory_space=pltpu.SMEM), vmem, vmem],
        out_specs=vmem,
        out_shape=jax.ShapeDtypeStruct(line.shape, BF16),
    )(my_slab.reshape(1), line, totals)
    prefix = lax.all_to_all(prefix, "z", split_axis=0, concat_axis=0, tiled=True)
    prefix = prefix.reshape(heads, PACKED, HEAD_DIM)
    num_b, phi_b = local(1)

    def hidden(chunk):
        some = rows // 2
        numbers = pl.BlockSpec((1, some, heads * HEAD_DIM // 2), lambda i, c: (c[0], i, 0))
        features = pl.BlockSpec((1, heads // 2, some, PACKED), lambda i, c: (c[0], 0, i, 0))
        return call(
            hidden_kernel,
            chunk.reshape(1),
            (2,),
            [
                numbers,
                numbers,
                features,
                features,
                whole((heads, PACKED, HEAD_DIM)),
                whole((1, heads * HEAD_DIM)),
            ],
            pl.BlockSpec((some, heads * HEAD_DIM), lambda i, c: (i, 0)),
            jax.ShapeDtypeStruct((rows, heads * HEAD_DIM), BF16),
            (num_a, num_b, phi_a, phi_b, prefix, gain_mine),
            rows * heads * HEAD_DIM * 600,
        )

    received = lax.ppermute(hidden(1 - core), "core", swap)
    kept = hidden(core)
    steps = 4
    per_out = groups // steps
    out = call(
        lambda core_ref, *refs: output_kernel(core_ref, layers, *refs),
        which,
        (steps,),
        [
            whole((rows, heads * HEAD_DIM)),
            whole((rows, heads * HEAD_DIM)),
            pl.BlockSpec((model, per_out * width), lambda i, _: (0, i)),
        ],
        pl.BlockSpec((per_out, rows, width), lambda i, _: (i, 0, 0)),
        jax.ShapeDtypeStruct((groups, rows, width), BF16),
        (kept, received, w_out),
        2 * rows * model * model,
        [pltpu.VMEM((rows, model), BF16)],
    )
    out = lax.all_to_all(out, ("z", "core"), split_axis=0, concat_axis=0, tiled=True)
    return out.reshape(groups * rows, width)


def solution(mesh):
    slabs, groups = mesh.shape["seq"], mesh.shape["chan"]
    split = jax.sharding.Mesh(mesh.devices.reshape(slabs, groups // 2, 2), ("seq", "z", "core"))
    chan = ("z", "core")
    return jax.shard_map(
        per_device,
        mesh=split,
        in_specs=(P("seq", chan), P(), P(), P(None, chan), P(), P()),
        out_specs=P("seq", chan),
        check_vma=False,
    )
```

```python
import jax
import jax.numpy as jnp
import numpy as np
from jax import lax
from jax.experimental import pallas as pl
from jax.experimental.pallas import tpu as pltpu
from jax.sharding import PartitionSpec as P

HEADS = 16
FEAT = 16
HEAD_DIM = 128
PACKED = 160
LANES = 128
HELD = LANES // FEAT
MIB = 1024 * 1024

F32 = jnp.float32
BF16 = jnp.bfloat16
NN = (((1,), (0,)), ((), ()))
NT = (((1,), (1,)), ((), ()))


def dot(a, b, dims=NN):
    return lax.dot_general(a, b, dims, preferred_element_type=F32)


def feature_tables():
    first = np.zeros((FEAT, PACKED), np.float32)
    second = np.zeros((FEAT, PACKED), np.float32)
    first_bias = np.zeros((PACKED,), np.float32)
    second_bias = np.zeros((PACKED,), np.float32)
    scale = np.zeros((PACKED,), np.float32)
    first_bias[0] = second_bias[0] = scale[0] = 1.0
    place = 1
    for i in range(FEAT):
        first[i, place] = 1.0
        second_bias[place] = 1.0
        scale[place] = 1.0 / 4.0
        place += 1
    for i in range(FEAT):
        for j in range(i, FEAT):
            first[i, place] = 1.0
            second[j, place] = 1.0
            scale[place] = 1.0 / 32.0 if i == j else 1.0 / 16.0
            place += 1
    return first, second, first_bias, second_bias, scale


def placed(table):
    out = np.zeros((HELD, LANES, PACKED), np.float32)
    for place in range(HELD):
        out[place, place * FEAT : (place + 1) * FEAT] = table
    return out


def stacked(table, per_group):
    every = placed(table).transpose(0, 2, 1)
    own = [[p for p in range(HELD) if (p // per_group) % 2 == core] for core in range(2)]
    return np.stack([every[places].reshape(-1, LANES) for places in own])


def project_kernel(at_ref, per_group, counts, layers, *refs):
    n_weights = sum(counts)
    mine, other = refs[:layers], refs[layers : 2 * layers]
    wq_ref, wk_ref, table_ref, bias_ref = refs[2 * layers : 2 * layers + 4]
    weights = refs[2 * layers + 4 : 2 * layers + 4 + n_weights]
    q_ref, k_ref, v_ref, early_ref, *rest = refs[2 * layers + 4 + n_weights :]
    totals, (row_ref, w_ref, phi_ref, sems) = rest[:layers], rest[layers:]
    core, layer, slab = at_ref[0], at_ref[1], at_ref[2]
    both, width = other[0].shape
    rows = both // 2
    copies = []
    place = 0
    for e, count in enumerate(counts):
        for m in range(count):
            source = weights[place]
            part = source.shape[0]
            start = 0 if count == 1 else pl.multiple_of((slab ^ m) * part, part)
            copy = pltpu.make_async_copy(source, w_ref.at[e, pl.ds(start, part)], sems.at[place])
            copy.start()
            copies.append((e, copy))
            place += 1

    for d in range(layers):
        z = lax.rem(layer + layers - d, layers)
        here = pl.multiple_of((2 * z + core) * width, width)
        there = pl.multiple_of((2 * z + 1 - core) * width, width)
        row_ref[:, pl.ds(here, width)] = mine[d][0] if d == 0 else mine[d][...]
        row_ref[:, pl.ds(there, width)] = other[d][...]
    q = dot(row_ref[...], wq_ref[...]).astype(BF16)
    k = dot(row_ref[...], wk_ref[...]).astype(BF16)
    half = table_ref.shape[1] // 2
    for chunk in range(2):
        at = slice(chunk * rows, (chunk + 1) * rows)
        q_ref[chunk] = q[at]
        k_ref[chunk] = k[at]
        for lanes in range(0, k.shape[1], LANES):
            product = dot(table_ref[0], k[at, lanes : lanes + LANES], NT)
            left = product[:half] + bias_ref[:, 0:1]
            right = product[half:] + bias_ref[:, 1:2]
            to = (lanes // LANES) * half
            phi_ref[chunk, to : to + half, :] = (left * right).astype(BF16)

    block = v_ref.shape[2] // layers
    for e in range(layers):
        for slot, copy in copies:
            if slot == e:
                copy.wait()
        z = lax.rem(layer + e, layers)
        first = []
        for chunk in range(2):
            value = dot(row_ref[chunk * rows : (chunk + 1) * rows, :], w_ref[e]).astype(BF16)
            v_ref[chunk, :, e * block : (e + 1) * block] = value
            for i in range(per_group):
                at = pl.multiple_of((z * per_group + i) * PACKED, PACKED)
                phi = phi_ref[chunk, pl.ds(at, PACKED), :]
                state = dot(phi, value[:, i * HEAD_DIM : (i + 1) * HEAD_DIM])
                if chunk == 0:
                    early_ref[e * per_group + i] = state.astype(BF16)
                    first.append(state)
                else:
                    totals[e][i] = (first[i] + state).astype(BF16)


def local_kernel(
    core_ref, per_group, layers, offset, q_ref, k_ref, v_ref, early_ref, ta_ref, tb_ref, bias_ref, num_ref, phi_ref
):
    chunk = pl.program_id(0)
    step = pl.program_id(1) + offset
    rows = q_ref.shape[1]
    half = rows // 2
    for i in range(per_group):
        z = lax.rem(core_ref[1] + step, layers)
        head = (2 * z + core_ref[0]) * per_group + i
        lanes = pl.multiple_of((head // HELD) * LANES, LANES)
        place = lax.rem(head, HELD)
        query = q_ref[0, :, pl.ds(lanes, LANES)]
        key = k_ref[0, :, pl.ds(lanes, LANES)]
        left = dot(query, ta_ref[place]) + bias_ref[0:1]
        right = dot(query, tb_ref[place]) + bias_ref[1:2]
        phi_ref[0, i] = (left * right).astype(BF16)
        lane = lax.broadcasted_iota(jnp.int32, (rows, LANES), 1)
        mine = jnp.where(lane // FEAT == place, query * jnp.asarray(0.25, BF16), jnp.zeros_like(query))
        columns = slice(i * HEAD_DIM, (i + 1) * HEAD_DIM)
        for low in (0, half):
            seen = low + half
            s = dot(mine[low:seen], key[:seen], NT)
            weight = 1.0 + s + 0.5 * s * s
            t_at = lax.broadcasted_iota(jnp.int32, (half, seen), 0) + low
            j_at = lax.broadcasted_iota(jnp.int32, (half, seen), 1)
            weight = jnp.where(t_at >= j_at, weight, 0.0).astype(BF16)
            num_ref[0, low:seen, columns] = dot(weight, v_ref[0, :seen, columns])

        @pl.when(chunk == 1)
        def _():
            num_ref[0, :, columns] += dot(phi_ref[0, i], early_ref[i])


def prefix_kernel(at_ref, layers, *refs):
    pieces, refs = refs[:layers], refs[layers:]
    slabs = len(refs) - layers - 1
    totals, outs, line_ref = refs[:slabs], refs[slabs : slabs + layers], refs[-1]
    layer, slab = at_ref[1], at_ref[2]
    for d in range(layers):
        line_ref[lax.rem(layer + layers - d, layers)] = pieces[d][...].astype(F32)
    run = jnp.zeros(line_ref.shape[1:], F32)
    for m in range(1, slabs):
        keep = jnp.where((slab ^ m) < slab, 1.0, 0.0)
        run = run + totals[m][...].astype(F32) * keep
    for z in range(layers):
        now = line_ref[z]
        line_ref[z] = run
        run = run + now
    for d in range(layers):
        outs[d][...] = line_ref[lax.rem(layer + layers - d, layers)].astype(BF16)


def hidden_kernel(chunk_ref, layers, num_a, num_b, phi_a, phi_b, gain_ref, *rest):
    states, out_ref = rest[:layers], rest[layers]
    held = phi_a.shape[1]
    per_group = 2 * held // layers
    for i in range(2 * held):
        columns = slice(i * HEAD_DIM, (i + 1) * HEAD_DIM)
        num_ref, phi_ref = (num_a, phi_a) if i < held else (num_b, phi_b)
        at = (i % held) * HEAD_DIM
        state = states[i // per_group][i % per_group]
        num = num_ref[0, :, at : at + HEAD_DIM] + dot(phi_ref[0, i % held], state)
        mean_square = jnp.mean(num * num, axis=1, keepdims=True)
        hidden = num * lax.rsqrt(mean_square + 1e-05) * gain_ref[:, columns]
        out_ref[:, columns] = hidden.astype(BF16)


def output_kernel(core_ref, layers, mine_ref, other_ref, w_ref, out_ref, hidden_ref):
    core = core_ref[0]

    @pl.when(pl.program_id(0) == 0)
    def _():
        block = mine_ref.shape[1] // layers
        for e in range(layers):
            z = lax.rem(core_ref[1] + e, layers)
            columns = slice(e * block, (e + 1) * block)
            here = pl.multiple_of((2 * z + core) * block, block)
            there = pl.multiple_of((2 * z + 1 - core) * block, block)
            hidden_ref[:, pl.ds(here, block)] = mine_ref[:, columns]
            hidden_ref[:, pl.ds(there, block)] = other_ref[:, columns]

    width = out_ref.shape[2]
    for c in range(out_ref.shape[0]):
        part = dot(hidden_ref[...], w_ref[:, c * width : (c + 1) * width])
        out_ref[c] = part.astype(BF16)


def whole(shape):
    return pl.BlockSpec(shape, lambda *_: (0,) * len(shape))


def params(mib):
    return pltpu.CompilerParams(vmem_limit_bytes=mib * MIB)


def call(kernel, scalar, grid, in_specs, out_specs, out_shape, args, flops, scratch=(), mib=60):
    return pl.pallas_call(
        kernel,
        grid_spec=pltpu.PrefetchScalarGridSpec(
            num_scalar_prefetch=1,
            grid=grid,
            in_specs=in_specs,
            out_specs=out_specs,
            scratch_shapes=list(scratch),
        ),
        out_shape=out_shape,
        compiler_params=params(mib),
        cost_estimate=pl.CostEstimate(flops=flops, bytes_accessed=12 * MIB, transcendentals=0),
    )(scalar, *args)


def per_device(tokens, w_query, w_key, w_value, w_out, gain):
    slabs = lax.axis_size("seq")
    layers = lax.axis_size("z")
    groups = 2 * layers
    my_slab = lax.axis_index("seq")
    core = lax.axis_index("core").astype(jnp.int32)
    layer = lax.axis_index("z").astype(jnp.int32)
    width = tokens.shape[1]
    rows = tokens.shape[0] // groups
    model, value_width = w_value.shape
    part = model // slabs
    per_group = HEADS // groups
    heads = HEADS // 2
    narrow = w_query.shape[1]
    swap = [(0, 1), (1, 0)]

    first, second, first_bias, second_bias, scale = feature_tables()
    sides = [stacked(first, per_group), stacked(second, per_group)]
    key_table = jnp.asarray(np.concatenate(sides, axis=1), BF16)
    repeat = HELD // 2
    key_bias = jnp.asarray(np.stack([np.tile(first_bias, repeat), np.tile(second_bias, repeat)], axis=1))
    query_a = jnp.asarray(placed(first * scale), BF16)
    query_b = jnp.asarray(placed(second), BF16)
    query_bias = jnp.asarray(np.stack([first_bias * scale, second_bias]))
    gain_mine = lax.dynamic_index_in_dim(gain.reshape(layers, 2, value_width), core, 1, False)
    gain_mine = jnp.concatenate([gain_mine, gain_mine])
    gain_mine = lax.dynamic_slice_in_dim(gain_mine, layer, layers, 0).reshape(1, layers * value_width)
    turn = lambda d: [(z, (z + d) % layers) for z in range(layers)]
    flip = lambda m: [(s, s ^ m) for s in range(slabs)]

    value_part = lax.dynamic_slice_in_dim(w_value, my_slab * part, part, 0)
    up, down = {0: value_part}, {0: value_part}
    for k in range(1, layers):
        up[k] = lax.ppermute(up[k - 1], "z", [(z, z + 1) for z in range(k - 1, layers - 1)])
        down[k] = lax.ppermute(down[k - 1], "z", [(z, z - 1) for z in range(1, layers - k + 1)])

    blocks = tokens.reshape(layers, 2 * rows, width)
    send = lambda d: lax.dynamic_index_in_dim(blocks, lax.rem(layer + d, layers), 0, False)
    mine = [send(0)] + [lax.ppermute(send(d), "z", turn(d)) for d in range(1, layers)]
    other = [lax.ppermute(piece, "core", swap) for piece in mine]

    weights, counts = [w_value], [1]
    for e in range(1, layers):
        slot = jnp.where(layer + e < layers, down[e], up[layers - e])
        if slabs == 4:
            weights.append(slot)
            for m in range(1, slabs):
                weights.append(lax.ppermute(slot, "seq", flip(m)))
            counts.append(slabs)
        else:
            weights.append(lax.all_gather(slot, "seq", axis=0, tiled=True))
            counts.append(1)

    anywhere = pl.BlockSpec(memory_space=pl.ANY)
    at = jnp.stack([core, layer, my_slab.astype(jnp.int32)])
    piece_shape = jax.ShapeDtypeStruct((per_group, PACKED, HEAD_DIM), BF16)
    query, key, value, early, *own = call(
        lambda at_ref, *refs: project_kernel(at_ref, per_group, counts, layers, *refs),
        at,
        (1,),
        [pl.BlockSpec((1, 2 * rows, width), lambda i, at: (at[1], 0, 0))]
        + [whole((2 * rows, width))] * (2 * layers - 1)
        + [
            whole((model, narrow)),
            whole((model, narrow)),
            pl.BlockSpec((1,) + key_table.shape[1:], lambda i, at: (at[0], 0, 0)),
            whole(key_bias.shape),
        ]
        + [anywhere] * len(weights),
        [
            whole((2, rows, narrow)),
            whole((2, rows, narrow)),
            whole((2, rows, layers * value_width)),
            whole((heads, PACKED, HEAD_DIM)),
        ]
        + [whole(piece_shape.shape)] * layers,
        [
            jax.ShapeDtypeStruct((2, rows, narrow), BF16),
            jax.ShapeDtypeStruct((2, rows, narrow), BF16),
            jax.ShapeDtypeStruct((2, rows, layers * value_width), BF16),
            jax.ShapeDtypeStruct((heads, PACKED, HEAD_DIM), BF16),
        ]
        + [piece_shape] * layers,
        (blocks, *mine[1:], *other, w_query, w_key, key_table, key_bias, *weights),
        4 * rows * model * (model // 2 + 2 * narrow),
        [
            pltpu.VMEM((2 * rows, model), BF16),
            pltpu.VMEM((layers, model, value_width), BF16),
            pltpu.VMEM((2, heads * PACKED, rows), BF16),
            pltpu.SemaphoreType.DMA((len(weights),)),
        ],
    )

    def local(part_of_heads):
        offset = part_of_heads * (layers // 2)
        return call(
            lambda core_ref, *refs: local_kernel(core_ref, per_group, layers, offset, *refs),
            at,
            (2, layers // 2),
            [
                pl.BlockSpec((1, rows, narrow), lambda c, i, _: (c, 0, 0)),
                pl.BlockSpec((1, rows, narrow), lambda c, i, _: (c, 0, 0)),
                pl.BlockSpec((1, rows, value_width), lambda c, i, _: (c, 0, i + offset)),
                pl.BlockSpec((per_group, PACKED, HEAD_DIM), lambda c, i, _: (i + offset, 0, 0)),
                whole((HELD, LANES, PACKED)),
                whole((HELD, LANES, PACKED)),
                whole((2, PACKED)),
            ],
            [
                pl.BlockSpec((1, rows, value_width), lambda c, i, _: (c, 0, i)),
                pl.BlockSpec((1, per_group, rows, PACKED), lambda c, i, _: (c, i, 0, 0)),
            ],
            [
                jax.ShapeDtypeStruct((2, rows, layers * value_width // 2), F32),
                jax.ShapeDtypeStruct((2, heads // 2, rows, PACKED), BF16),
            ],
            (query, key, value, early, query_a, query_b, query_bias),
            heads * rows * rows * 600,
        )

    pieces = [own[0]] + [lax.ppermute(own[d], "z", turn(d)) for d in range(1, layers)]
    num_a, phi_a = local(0)
    pieces, num_a, phi_a = lax.optimization_barrier((pieces, num_a, phi_a))
    slab_total = sum(piece.astype(F32) for piece in pieces).astype(BF16)
    totals = [slab_total] + [lax.ppermute(slab_total, "seq", flip(m)) for m in range(1, slabs)]
    vmem = pl.BlockSpec(memory_space=pltpu.VMEM)
    prefix = pl.pallas_call(
        lambda at_ref, *refs: prefix_kernel(at_ref, layers, *refs),
        in_specs=[pl.BlockSpec(memory_space=pltpu.SMEM)] + [vmem] * (layers + slabs),
        out_specs=[vmem] * layers,
        out_shape=[piece_shape] * layers,
        scratch_shapes=[pltpu.VMEM((layers,) + piece_shape.shape, F32)],
    )(at, *pieces, *totals)
    prefix = [prefix[0]] + [lax.ppermute(prefix[d], "z", turn(-d)) for d in range(1, layers)]
    num_b, phi_b = local(1)

    def hidden(chunk):
        some = rows // 2
        numbers = pl.BlockSpec((1, some, heads * HEAD_DIM // 2), lambda i, c: (c[0], i, 0))
        features = pl.BlockSpec((1, heads // 2, some, PACKED), lambda i, c: (c[0], 0, i, 0))
        return call(
            lambda chunk_ref, *refs: hidden_kernel(chunk_ref, layers, *refs),
            chunk.reshape(1),
            (2,),
            [numbers, numbers, features, features, whole((1, heads * HEAD_DIM))]
            + [whole(piece_shape.shape)] * layers,
            pl.BlockSpec((some, heads * HEAD_DIM), lambda i, c: (i, 0)),
            jax.ShapeDtypeStruct((rows, heads * HEAD_DIM), BF16),
            (num_a, num_b, phi_a, phi_b, gain_mine, *prefix),
            rows * heads * HEAD_DIM * 600,
        )

    received = lax.ppermute(hidden(1 - core), "core", swap)
    kept = hidden(core)
    steps = 4
    per_out = groups // steps
    out = call(
        lambda core_ref, *refs: output_kernel(core_ref, layers, *refs),
        at,
        (steps,),
        [
            whole((rows, heads * HEAD_DIM)),
            whole((rows, heads * HEAD_DIM)),
            pl.BlockSpec((model, per_out * width), lambda i, _: (0, i)),
        ],
        pl.BlockSpec((per_out, rows, width), lambda i, _: (i, 0, 0)),
        jax.ShapeDtypeStruct((groups, rows, width), BF16),
        (kept, received, w_out),
        2 * rows * model * model,
        [pltpu.VMEM((rows, model), BF16)],
    )
    out = lax.all_to_all(out, ("z", "core"), split_axis=0, concat_axis=0, tiled=True)
    return out.reshape(groups * rows, width)


def solution(mesh):
    slabs, groups = mesh.shape["seq"], mesh.shape["chan"]
    split = jax.sharding.Mesh(mesh.devices.reshape(slabs, groups // 2, 2), ("seq", "z", "core"))
    chan = ("z", "core")
    return jax.shard_map(
        per_device,
        mesh=split,
        in_specs=(P("seq", chan), P(), P(), P(None, chan), P(), P()),
        out_specs=P("seq", chan),
        check_vma=False,
    )
```

```python
import jax
import jax.numpy as jnp
import numpy as np
from jax import lax
from jax.experimental import pallas as pl
from jax.experimental.pallas import tpu as pltpu
from jax.sharding import PartitionSpec as P

HEADS = 16
FEAT = 16
HEAD_DIM = 128
PACKED = 160
LANES = 128
HELD = LANES // FEAT
MIB = 1024 * 1024

F32 = jnp.float32
BF16 = jnp.bfloat16
NN = (((1,), (0,)), ((), ()))
NT = (((1,), (1,)), ((), ()))


def dot(a, b, dims=NN):
    return lax.dot_general(a, b, dims, preferred_element_type=F32)


def feature_tables():
    first = np.zeros((FEAT, PACKED), np.float32)
    second = np.zeros((FEAT, PACKED), np.float32)
    first_bias = np.zeros((PACKED,), np.float32)
    second_bias = np.zeros((PACKED,), np.float32)
    scale = np.zeros((PACKED,), np.float32)
    first_bias[0] = second_bias[0] = scale[0] = 1.0
    place = 1
    for i in range(FEAT):
        first[i, place] = 1.0
        second_bias[place] = 1.0
        scale[place] = 1.0 / 4.0
        place += 1
    for i in range(FEAT):
        for j in range(i, FEAT):
            first[i, place] = 1.0
            second[j, place] = 1.0
            scale[place] = 1.0 / 32.0 if i == j else 1.0 / 16.0
            place += 1
    return first, second, first_bias, second_bias, scale


def placed(table):
    out = np.zeros((HELD, LANES, PACKED), np.float32)
    for place in range(HELD):
        out[place, place * FEAT : (place + 1) * FEAT] = table
    return out


def stacked(table, per_group):
    every = placed(table).transpose(0, 2, 1)
    own = [[p for p in range(HELD) if (p // per_group) % 2 == core] for core in range(2)]
    return np.stack([every[places].reshape(-1, LANES) for places in own])


def project_kernel(at_ref, per_group, n_weights, gathered, chunk, *refs):
    mine_ref, other_ref, wq_ref, wk_ref, table_ref, bias_ref = refs[:6]
    weights = refs[6 : 6 + n_weights]
    rest = refs[6 + n_weights :]
    if chunk > 0:
        early_ref, *rest = rest
    q_ref, k_ref, v_ref, state_ref, row_ref, w_ref, phi_ref, sems = rest
    core, layer, slab = at_ref[0], at_ref[1], at_ref[2]
    layers, rows, width = mine_ref.shape
    part = weights[1].shape[-2]
    copies = [pltpu.make_async_copy(weights[0], w_ref.at[0], sems.at[0])]
    slots = [0]
    for d in range(1, layers):
        for m in range(w_ref.shape[1] // part):
            if gathered:
                source, start = weights[1].at[m, d - 1], m * part
            else:
                source, start = weights[1 + m].at[d - 1], pl.multiple_of((slab ^ m) * part, part)
            to = w_ref.at[d, pl.ds(start, part)]
            copies.append(pltpu.make_async_copy(source, to, sems.at[len(copies)]))
            slots.append(d)
    for copy in copies:
        copy.start()

    for z in range(layers):
        here = pl.multiple_of((2 * z + core) * width, width)
        there = pl.multiple_of((2 * z + 1 - core) * width, width)
        row_ref[:, pl.ds(here, width)] = mine_ref[z]
        row_ref[:, pl.ds(there, width)] = other_ref[z]
    q_ref[...] = dot(row_ref[...], wq_ref[...]).astype(BF16)
    k = dot(row_ref[...], wk_ref[...]).astype(BF16)
    k_ref[...] = k
    half = table_ref.shape[1] // 2
    for lanes in range(0, k.shape[1], LANES):
        product = dot(table_ref[0], k[:, lanes : lanes + LANES], NT)
        left = product[:half] + bias_ref[:, 0:1]
        right = product[half:] + bias_ref[:, 1:2]
        to = (lanes // LANES) * half
        phi_ref[to : to + half, :] = (left * right).astype(BF16)

    block = v_ref.shape[1] // layers
    for d in range(layers):
        for slot, copy in zip(slots, copies):
            if slot == d:
                copy.wait()
        z = lax.rem(layer + d, layers)
        value = dot(row_ref[...], w_ref[d]).astype(BF16)
        v_ref[:, pl.ds(pl.multiple_of(z * block, block), block)] = value
        for i in range(per_group):
            head = z * per_group + i
            phi = phi_ref[pl.ds(pl.multiple_of(head * PACKED, PACKED), PACKED), :]
            state = dot(phi, value[:, i * HEAD_DIM : (i + 1) * HEAD_DIM])
            if chunk > 0:
                state = state + early_ref[head].astype(F32)
            state_ref[head] = state.astype(BF16)


def local_kernel(core_ref, per_group, chunk, q_ref, k_ref, v_ref, ta_ref, tb_ref, bias_ref, *refs):
    num_ref, phi_ref = refs[-2:]
    step = pl.program_id(0)
    rows = q_ref.shape[0]
    half = rows // 2
    for i in range(per_group):
        head = (2 * step + core_ref[0]) * per_group + i
        lanes = pl.multiple_of((head // HELD) * LANES, LANES)
        place = lax.rem(head, HELD)
        query = q_ref[:, pl.ds(lanes, LANES)]
        key = k_ref[:, pl.ds(lanes, LANES)]
        left = dot(query, ta_ref[place]) + bias_ref[0:1]
        right = dot(query, tb_ref[place]) + bias_ref[1:2]
        phi = (left * right).astype(BF16)
        phi_ref[0, i] = phi
        lane = lax.broadcasted_iota(jnp.int32, (rows, LANES), 1)
        mine = jnp.where(lane // FEAT == place, query * jnp.asarray(0.25, BF16), jnp.zeros_like(query))
        columns = slice(i * HEAD_DIM, (i + 1) * HEAD_DIM)
        for low in (0, half):
            seen = low + half
            s = dot(mine[low:seen], key[:seen], NT)
            weight = 1.0 + s + 0.5 * s * s
            t_at = lax.broadcasted_iota(jnp.int32, (half, seen), 0) + low
            j_at = lax.broadcasted_iota(jnp.int32, (half, seen), 1)
            weight = jnp.where(t_at >= j_at, weight, 0.0).astype(BF16)
            num = dot(weight, v_ref[:seen, columns])
            if chunk > 0:
                num = num + dot(phi[low:seen], refs[0][i])
            num_ref[0, low:seen, columns] = num


def prefix_kernel(at_ref, line_ref, *refs):
    totals, out_ref = refs[:-1], refs[-1]
    slab = at_ref[2]
    run = jnp.zeros(line_ref.shape[1:], F32)
    for m, total in enumerate(totals, 1):
        run = run + total[...].astype(F32) * jnp.where((slab ^ m) < slab, 1.0, 0.0)
    for z in range(line_ref.shape[0]):
        out_ref[z] = run.astype(BF16)
        run = run + line_ref[z].astype(F32)


def hidden_kernel(chunk_ref, num_ref, phi_ref, state_ref, gain_ref, out_ref):
    for i in range(phi_ref.shape[1]):
        columns = slice(i * HEAD_DIM, (i + 1) * HEAD_DIM)
        num = num_ref[0, :, columns] + dot(phi_ref[0, i], state_ref[i])
        mean_square = jnp.mean(num * num, axis=1, keepdims=True)
        hidden = num * lax.rsqrt(mean_square + 1e-05) * gain_ref[:, columns]
        out_ref[:, columns] = hidden.astype(BF16)


def output_kernel(core_ref, layers, mine_ref, other_ref, w_ref, out_ref, hidden_ref):
    core = core_ref[0]

    @pl.when(pl.program_id(0) == 0)
    def _():
        block = mine_ref.shape[1] // layers
        for z in range(layers):
            columns = slice(z * block, (z + 1) * block)
            here = pl.multiple_of((2 * z + core) * block, block)
            there = pl.multiple_of((2 * z + 1 - core) * block, block)
            hidden_ref[:, pl.ds(here, block)] = mine_ref[:, columns]
            hidden_ref[:, pl.ds(there, block)] = other_ref[:, columns]

    width = out_ref.shape[2]
    for c in range(out_ref.shape[0]):
        part = dot(hidden_ref[...], w_ref[:, c * width : (c + 1) * width])
        out_ref[c] = part.astype(BF16)


def whole(shape):
    return pl.BlockSpec(shape, lambda *_: (0,) * len(shape))


def params(mib):
    return pltpu.CompilerParams(vmem_limit_bytes=mib * MIB)


def call(kernel, scalar, grid, in_specs, out_specs, out_shape, args, flops, scratch=(), aliases=None):
    return pl.pallas_call(
        kernel,
        grid_spec=pltpu.PrefetchScalarGridSpec(
            num_scalar_prefetch=1,
            grid=grid,
            in_specs=in_specs,
            out_specs=out_specs,
            scratch_shapes=list(scratch),
        ),
        out_shape=out_shape,
        input_output_aliases=aliases or {},
        compiler_params=params(60),
        cost_estimate=pl.CostEstimate(flops=flops, bytes_accessed=12 * MIB, transcendentals=0),
    )(scalar, *args)


def per_device(tokens, w_query, w_key, w_value, w_out, gain):
    slabs = lax.axis_size("seq")
    layers = lax.axis_size("z")
    groups = 2 * layers
    my_slab = lax.axis_index("seq")
    core = lax.axis_index("core").astype(jnp.int32)
    layer = lax.axis_index("z").astype(jnp.int32)
    which = core.reshape(1)
    width = tokens.shape[1]
    rows = tokens.shape[0] // groups
    model, value_width = w_value.shape
    part = model // slabs
    per_group = HEADS // groups
    heads = HEADS // 2
    narrow = w_query.shape[1]
    swap = [(0, 1), (1, 0)]

    first, second, first_bias, second_bias, scale = feature_tables()
    sides = [stacked(first, per_group), stacked(second, per_group)]
    key_table = jnp.asarray(np.concatenate(sides, axis=1), BF16)
    repeat = HELD // 2
    key_bias = jnp.asarray(np.stack([np.tile(first_bias, repeat), np.tile(second_bias, repeat)], axis=1))
    query_a = jnp.asarray(placed(first * scale), BF16)
    query_b = jnp.asarray(placed(second), BF16)
    query_bias = jnp.asarray(np.stack([first_bias * scale, second_bias]))
    gain_mine = lax.dynamic_index_in_dim(gain.reshape(layers, 2, value_width), core, 1, False)
    gain_mine = gain_mine.reshape(1, layers * value_width)

    flip = lambda m: [(s, s ^ m) for s in range(slabs)]
    value_part = lax.dynamic_slice_in_dim(w_value, my_slab * part, part, 0)
    up, down = {0: value_part}, {0: value_part}
    for k in range(1, layers):
        up[k] = lax.ppermute(up[k - 1], "z", [(z, z + 1) for z in range(k - 1, layers - 1)])
        down[k] = lax.ppermute(down[k - 1], "z", [(z, z - 1) for z in range(1, layers - k + 1)])
    slots = jnp.stack([jnp.where(layer + d < layers, down[d], up[layers - d]) for d in range(1, layers)])
    blocks = tokens.reshape(layers, 2, rows, width)
    halves = [blocks[:, chunk] for chunk in range(2)]
    slots, halves = lax.optimization_barrier((slots, halves))
    if slabs == 4:
        weights = [w_value, slots] + [lax.ppermute(slots, "seq", flip(m)) for m in range(1, slabs)]
    else:
        weights = [w_value, lax.all_gather(slots, "seq", axis=0, tiled=False)]

    anywhere = pl.BlockSpec(memory_space=pl.ANY)
    at = jnp.stack([core, layer, my_slab.astype(jnp.int32)])

    def project(chunk, mine, early):
        other = lax.ppermute(mine, "core", swap)
        early_spec = [whole((heads, PACKED, HEAD_DIM))] if chunk else []
        return call(
            lambda at_ref, *refs: project_kernel(at_ref, per_group, len(weights), slabs != 4, chunk, *refs),
            at,
            (1,),
            [
                whole((layers, rows, width)),
                whole((layers, rows, width)),
                whole((model, narrow)),
                whole((model, narrow)),
                pl.BlockSpec((1,) + key_table.shape[1:], lambda i, at: (at[0], 0, 0)),
                whole(key_bias.shape),
            ]
            + [anywhere] * len(weights)
            + early_spec,
            [
                whole((rows, narrow)),
                whole((rows, narrow)),
                whole((rows, layers * value_width)),
                whole((heads, PACKED, HEAD_DIM)),
            ],
            [
                jax.ShapeDtypeStruct((rows, narrow), BF16),
                jax.ShapeDtypeStruct((rows, narrow), BF16),
                jax.ShapeDtypeStruct((rows, layers * value_width), BF16),
                jax.ShapeDtypeStruct((heads, PACKED, HEAD_DIM), BF16),
            ],
            (mine, other, w_query, w_key, key_table, key_bias, *weights, *([early] if chunk else [])),
            2 * rows * model * (model // 2 + 2 * narrow),
            [
                pltpu.VMEM((rows, model), BF16),
                pltpu.VMEM((layers, model, value_width), BF16),
                pltpu.VMEM((heads * PACKED, rows), BF16),
                pltpu.SemaphoreType.DMA((1 + (layers - 1) * slabs,)),
            ],
        )

    def local(chunk, query, key, value, extra):
        extra_specs = [pl.BlockSpec((per_group, PACKED, HEAD_DIM), lambda i, _: (i, 0, 0))]
        extra_specs += [anywhere] * 2
        return call(
            lambda core_ref, *refs: local_kernel(core_ref, per_group, chunk, *refs),
            at,
            (layers,),
            [
                whole((rows, narrow)),
                whole((rows, narrow)),
                pl.BlockSpec((rows, value_width), lambda i, _: (0, i)),
                whole((HELD, LANES, PACKED)),
                whole((HELD, LANES, PACKED)),
                whole((2, PACKED)),
            ]
            + (extra_specs if chunk else []),
            [
                pl.BlockSpec((1, rows, value_width), lambda i, _: (chunk, 0, i)),
                pl.BlockSpec((1, per_group, rows, PACKED), lambda i, _: (chunk, i, 0, 0)),
            ],
            [
                jax.ShapeDtypeStruct((2, rows, layers * value_width), F32),
                jax.ShapeDtypeStruct((2, heads, rows, PACKED), BF16),
            ],
            (query, key, value, query_a, query_b, query_bias, *extra),
            heads * rows * rows * 600,
            aliases={8: 0, 9: 1} if chunk else None,
        )

    swapped = [
        lax.all_to_all(half, "z", split_axis=0, concat_axis=0, tiled=True) for half in halves
    ]
    query, key, value, early = project(0, swapped[0], None)
    num, phi = local(0, query, key, value, ())
    query, key, value, total = project(1, swapped[1], early)
    own = total.reshape(layers, per_group, PACKED, HEAD_DIM)
    line = lax.all_to_all(own, "z", split_axis=0, concat_axis=0, tiled=True)
    num, phi = local(1, query, key, value, (early, num, phi))
    line, num, phi = lax.optimization_barrier((line, num, phi))
    slab_total = jnp.sum(line.astype(F32), axis=0).astype(BF16)
    totals = [lax.ppermute(slab_total, "seq", flip(m)) for m in range(1, slabs)]
    vmem = pl.BlockSpec(memory_space=pltpu.VMEM)
    prefix = pl.pallas_call(
        prefix_kernel,
        in_specs=[pl.BlockSpec(memory_space=pltpu.SMEM)] + [vmem] * slabs,
        out_specs=vmem,
        out_shape=jax.ShapeDtypeStruct(line.shape, BF16),
    )(at, line, *totals)
    prefix = lax.all_to_all(prefix, "z", split_axis=0, concat_axis=0, tiled=True)
    prefix = prefix.reshape(heads, PACKED, HEAD_DIM)

    def hidden(chunk):
        some = rows // 2
        return call(
            hidden_kernel,
            chunk.reshape(1),
            (2,),
            [
                pl.BlockSpec((1, some, heads * HEAD_DIM), lambda i, c: (c[0], i, 0)),
                pl.BlockSpec((1, heads, some, PACKED), lambda i, c: (c[0], 0, i, 0)),
                whole((heads, PACKED, HEAD_DIM)),
                whole((1, heads * HEAD_DIM)),
            ],
            pl.BlockSpec((some, heads * HEAD_DIM), lambda i, c: (i, 0)),
            jax.ShapeDtypeStruct((rows, heads * HEAD_DIM), BF16),
            (num, phi, prefix, gain_mine),
            rows * heads * HEAD_DIM * 600,
        )

    received = lax.ppermute(hidden(1 - core), "core", swap)
    kept = hidden(core)
    steps = 4
    per_out = groups // steps
    out = call(
        lambda core_ref, *refs: output_kernel(core_ref, layers, *refs),
        which,
        (steps,),
        [
            whole((rows, heads * HEAD_DIM)),
            whole((rows, heads * HEAD_DIM)),
            pl.BlockSpec((model, per_out * width), lambda i, _: (0, i)),
        ],
        pl.BlockSpec((per_out, rows, width), lambda i, _: (i, 0, 0)),
        jax.ShapeDtypeStruct((groups, rows, width), BF16),
        (kept, received, w_out),
        2 * rows * model * model,
        [pltpu.VMEM((rows, model), BF16)],
    )
    out = lax.all_to_all(out, ("z", "core"), split_axis=0, concat_axis=0, tiled=True)
    return out.reshape(groups * rows, width)


def solution(mesh):
    slabs, groups = mesh.shape["seq"], mesh.shape["chan"]
    split = jax.sharding.Mesh(mesh.devices.reshape(slabs, groups // 2, 2), ("seq", "z", "core"))
    chan = ("z", "core")
    return jax.shard_map(
        per_device,
        mesh=split,
        in_specs=(P("seq", chan), P(), P(), P(None, chan), P(), P()),
        out_specs=P("seq", chan),
        check_vma=False,
    )
```

```python
import jax
import jax.numpy as jnp
import numpy as np
from jax import lax
from jax.experimental import pallas as pl
from jax.experimental.pallas import tpu as pltpu
from jax.sharding import PartitionSpec as P

HEADS = 16
FEAT = 16
HEAD_DIM = 128
PACKED = 160
LANES = 128
HELD = LANES // FEAT
MIB = 1024 * 1024

F32 = jnp.float32
BF16 = jnp.bfloat16
NN = (((1,), (0,)), ((), ()))
NT = (((1,), (1,)), ((), ()))


def dot(a, b, dims=NN):
    return lax.dot_general(a, b, dims, preferred_element_type=F32)


def feature_tables():
    first = np.zeros((FEAT, PACKED), np.float32)
    second = np.zeros((FEAT, PACKED), np.float32)
    first_bias = np.zeros((PACKED,), np.float32)
    second_bias = np.zeros((PACKED,), np.float32)
    scale = np.zeros((PACKED,), np.float32)
    first_bias[0] = second_bias[0] = scale[0] = 1.0
    place = 1
    for i in range(FEAT):
        first[i, place] = 1.0
        second_bias[place] = 1.0
        scale[place] = 1.0 / 4.0
        place += 1
    for i in range(FEAT):
        for j in range(i, FEAT):
            first[i, place] = 1.0
            second[j, place] = 1.0
            scale[place] = 1.0 / 32.0 if i == j else 1.0 / 16.0
            place += 1
    return first, second, first_bias, second_bias, scale


def placed(table):
    out = np.zeros((HELD, LANES, PACKED), np.float32)
    for place in range(HELD):
        out[place, place * FEAT : (place + 1) * FEAT] = table
    return out


def stacked(table, per_group):
    every = placed(table).transpose(0, 2, 1)
    own = [[p for p in range(HELD) if (p // per_group) % 2 == core] for core in range(2)]
    return np.stack([every[places].reshape(-1, LANES) for places in own])


def project_kernel(at_ref, per_group, layers, n_weights, gathered, *refs):
    mine, other = refs[:layers], refs[layers : 2 * layers]
    wq_ref, wk_ref, table_ref, bias_ref = refs[2 * layers : 2 * layers + 4]
    weights = refs[2 * layers + 4 : 2 * layers + 4 + n_weights]
    q_ref, k_ref, v_ref, early_ref, total_ref, row_ref, w_ref, phi_ref, sems = refs[2 * layers + 4 + n_weights :]
    core, layer, slab = at_ref[0], at_ref[1], at_ref[2]
    both, width = other[0].shape
    rows = both // 2
    part = weights[1].shape[-2]
    copies = [pltpu.make_async_copy(weights[0], w_ref.at[0], sems.at[0])]
    slots = [0]
    for d in range(1, layers):
        for m in range(w_ref.shape[1] // part):
            if gathered:
                source, start = weights[1].at[m, d - 1], m * part
            else:
                source, start = weights[1 + m].at[d - 1], pl.multiple_of((slab ^ m) * part, part)
            to = w_ref.at[d, pl.ds(start, part)]
            copies.append(pltpu.make_async_copy(source, to, sems.at[len(copies)]))
            slots.append(d)
    for copy in copies:
        copy.start()

    for d in range(layers):
        z = lax.rem(layer + layers - d, layers)
        here = pl.multiple_of((2 * z + core) * width, width)
        there = pl.multiple_of((2 * z + 1 - core) * width, width)
        row_ref[:, pl.ds(here, width)] = mine[d][0] if d == 0 else mine[d][...]
        row_ref[:, pl.ds(there, width)] = other[d][...]
    q = dot(row_ref[...], wq_ref[...]).astype(BF16)
    k = dot(row_ref[...], wk_ref[...]).astype(BF16)
    half = table_ref.shape[1] // 2
    for chunk in range(2):
        at = slice(chunk * rows, (chunk + 1) * rows)
        q_ref[chunk] = q[at]
        k_ref[chunk] = k[at]
        for lanes in range(0, k.shape[1], LANES):
            product = dot(table_ref[0], k[at, lanes : lanes + LANES], NT)
            left = product[:half] + bias_ref[:, 0:1]
            right = product[half:] + bias_ref[:, 1:2]
            to = (lanes // LANES) * half
            phi_ref[chunk, to : to + half, :] = (left * right).astype(BF16)

    block = v_ref.shape[2] // layers
    for d in range(layers):
        for slot, copy in zip(slots, copies):
            if slot == d:
                copy.wait()
        z = lax.rem(layer + d, layers)
        first = []
        for chunk in range(2):
            value = dot(row_ref[chunk * rows : (chunk + 1) * rows, :], w_ref[d]).astype(BF16)
            v_ref[chunk, :, pl.ds(pl.multiple_of(z * block, block), block)] = value
            for i in range(per_group):
                head = z * per_group + i
                phi = phi_ref[chunk, pl.ds(pl.multiple_of(head * PACKED, PACKED), PACKED), :]
                state = dot(phi, value[:, i * HEAD_DIM : (i + 1) * HEAD_DIM])
                if chunk == 0:
                    early_ref[head] = state.astype(BF16)
                    first.append(state)
                else:
                    total_ref[head] = (first[i] + state).astype(BF16)


def local_kernel(
    core_ref, per_group, offset, q_ref, k_ref, v_ref, early_ref, ta_ref, tb_ref, bias_ref, num_ref, phi_ref
):
    chunk = pl.program_id(0)
    step = pl.program_id(1) + offset
    rows = q_ref.shape[1]
    half = rows // 2
    for i in range(per_group):
        head = (2 * step + core_ref[0]) * per_group + i
        lanes = pl.multiple_of((head // HELD) * LANES, LANES)
        place = lax.rem(head, HELD)
        query = q_ref[0, :, pl.ds(lanes, LANES)]
        key = k_ref[0, :, pl.ds(lanes, LANES)]
        left = dot(query, ta_ref[place]) + bias_ref[0:1]
        right = dot(query, tb_ref[place]) + bias_ref[1:2]
        phi_ref[0, i] = (left * right).astype(BF16)
        lane = lax.broadcasted_iota(jnp.int32, (rows, LANES), 1)
        mine = jnp.where(lane // FEAT == place, query * jnp.asarray(0.25, BF16), jnp.zeros_like(query))
        columns = slice(i * HEAD_DIM, (i + 1) * HEAD_DIM)
        for low in (0, half):
            seen = low + half
            s = dot(mine[low:seen], key[:seen], NT)
            weight = 1.0 + s + 0.5 * s * s
            t_at = lax.broadcasted_iota(jnp.int32, (half, seen), 0) + low
            j_at = lax.broadcasted_iota(jnp.int32, (half, seen), 1)
            weight = jnp.where(t_at >= j_at, weight, 0.0).astype(BF16)
            num_ref[0, low:seen, columns] = dot(weight, v_ref[0, :seen, columns])

        @pl.when(chunk == 1)
        def _():
            num_ref[0, :, columns] += dot(phi_ref[0, i], early_ref[i])


def prefix_kernel(at_ref, line_ref, *refs):
    totals, out_ref = refs[:-1], refs[-1]
    slab = at_ref[2]
    run = jnp.zeros(line_ref.shape[1:], F32)
    for m, total in enumerate(totals, 1):
        run = run + total[...].astype(F32) * jnp.where((slab ^ m) < slab, 1.0, 0.0)
    for z in range(line_ref.shape[0]):
        out_ref[z] = run.astype(BF16)
        run = run + line_ref[z].astype(F32)


def hidden_kernel(at_ref, num_a, num_b, phi_a, phi_b, state_ref, gain_ref, out_ref):
    held = phi_a.shape[1]
    for i in range(2 * held):
        columns = slice(i * HEAD_DIM, (i + 1) * HEAD_DIM)
        num_ref, phi_ref = (num_a, phi_a) if i < held else (num_b, phi_b)
        at = (i % held) * HEAD_DIM
        num = num_ref[0, :, at : at + HEAD_DIM] + dot(phi_ref[0, i % held], state_ref[i])
        mean_square = jnp.mean(num * num, axis=1, keepdims=True)
        hidden = num * lax.rsqrt(mean_square + 1e-05) * gain_ref[:, columns]
        out_ref[:, columns] = hidden.astype(BF16)


def output_kernel(at_ref, *refs):
    chunks, w_mine, w_other, out_ref = refs[:-3], refs[-3], refs[-2], refs[-1]
    rows, depth = chunks[0].shape
    width = out_ref.shape[1]
    for i in range(len(chunks) // 2):
        part = dot(chunks[2 * i][...], w_mine[...].reshape(depth, width))
        part = part + dot(chunks[2 * i + 1][...], w_other[...].reshape(depth, width))
        out_ref[i * rows : (i + 1) * rows, :] = part.astype(BF16)


def place_kernel(at_ref, *refs):
    pieces, out_ref, sems = refs[:-2], refs[-2], refs[-1]
    layers = len(pieces)
    copies = []
    for d, piece in enumerate(pieces):
        z = lax.rem(at_ref[1] + layers - d, layers)
        to = out_ref.at[pl.ds(pl.multiple_of(z * piece.shape[0], piece.shape[0]), piece.shape[0])]
        copies.append(pltpu.make_async_copy(piece, to, sems.at[d]))
    for copy in copies:
        copy.start()
    for copy in copies:
        copy.wait()


def whole(shape):
    return pl.BlockSpec(shape, lambda *_: (0,) * len(shape))


def params(mib):
    return pltpu.CompilerParams(vmem_limit_bytes=mib * MIB)


def call(kernel, scalar, grid, in_specs, out_specs, out_shape, args, flops, scratch=()):
    return pl.pallas_call(
        kernel,
        grid_spec=pltpu.PrefetchScalarGridSpec(
            num_scalar_prefetch=1,
            grid=grid,
            in_specs=in_specs,
            out_specs=out_specs,
            scratch_shapes=list(scratch),
        ),
        out_shape=out_shape,
        compiler_params=params(60),
        cost_estimate=pl.CostEstimate(flops=flops, bytes_accessed=12 * MIB, transcendentals=0),
    )(scalar, *args)


def per_device(tokens, w_query, w_key, w_value, w_out, gain):
    slabs = lax.axis_size("seq")
    layers = lax.axis_size("z")
    groups = 2 * layers
    my_slab = lax.axis_index("seq")
    core = lax.axis_index("core").astype(jnp.int32)
    layer = lax.axis_index("z").astype(jnp.int32)
    which = core.reshape(1)
    width = tokens.shape[1]
    rows = tokens.shape[0] // groups
    model, value_width = w_value.shape
    part = model // slabs
    per_group = HEADS // groups
    heads = HEADS // 2
    narrow = w_query.shape[1]
    swap = [(0, 1), (1, 0)]

    first, second, first_bias, second_bias, scale = feature_tables()
    sides = [stacked(first, per_group), stacked(second, per_group)]
    key_table = jnp.asarray(np.concatenate(sides, axis=1), BF16)
    repeat = HELD // 2
    key_bias = jnp.asarray(np.stack([np.tile(first_bias, repeat), np.tile(second_bias, repeat)], axis=1))
    query_a = jnp.asarray(placed(first * scale), BF16)
    query_b = jnp.asarray(placed(second), BF16)
    query_bias = jnp.asarray(np.stack([first_bias * scale, second_bias]))
    gain_mine = lax.dynamic_index_in_dim(gain.reshape(layers, 2, value_width), core, 1, False)
    gain_mine = gain_mine.reshape(1, layers * value_width)

    flip = lambda m: [(s, s ^ m) for s in range(slabs)]
    turn = lambda d: [(z, (z + d) % layers) for z in range(layers)]
    anywhere = pl.BlockSpec(memory_space=pl.ANY)
    vmem = pl.BlockSpec(memory_space=pltpu.VMEM)
    at = jnp.stack([core, layer, my_slab.astype(jnp.int32)])

    value_part = lax.dynamic_slice_in_dim(w_value, my_slab * part, part, 0)
    up, down = {0: value_part}, {0: value_part}
    blocks = tokens.reshape(layers, 2 * rows, width)
    sent = [lax.dynamic_index_in_dim(blocks, lax.rem(layer + d, layers), 0, False) for d in range(layers)]
    for k in range(1, layers):
        up[k] = lax.ppermute(up[k - 1], "z", [(z, z + 1) for z in range(k - 1, layers - 1)])
        down[k] = lax.ppermute(down[k - 1], "z", [(z, z - 1) for z in range(1, layers - k + 1)])
        if k == layers - 2:
            up[k], down[k], sent = lax.optimization_barrier((up[k], down[k], sent))
    slots = jnp.stack([jnp.where(layer + d < layers, down[d], up[layers - d]) for d in range(1, layers)])
    mine = [sent[0]] + [lax.ppermute(sent[d], "z", turn(d)) for d in range(1, layers)]
    if slabs == 4:
        weights = [w_value, slots] + [lax.ppermute(slots, "seq", flip(m)) for m in range(1, slabs)]
    else:
        weights = [w_value, lax.all_gather(slots, "seq", axis=0, tiled=False)]
    mine, weights[2:] = lax.optimization_barrier((mine, weights[2:]))
    other = [lax.ppermute(piece, "core", swap) for piece in mine]

    query, key, value, early, total = call(
        lambda at_ref, *refs: project_kernel(at_ref, per_group, layers, len(weights), slabs != 4, *refs),
        at,
        (1,),
        [pl.BlockSpec((1, 2 * rows, width), lambda i, at: (at[1], 0, 0))]
        + [whole((2 * rows, width))] * (2 * layers - 1)
        + [
            whole((model, narrow)),
            whole((model, narrow)),
            pl.BlockSpec((1,) + key_table.shape[1:], lambda i, at: (at[0], 0, 0)),
            whole(key_bias.shape),
        ]
        + [anywhere] * len(weights),
        [
            whole((2, rows, narrow)),
            whole((2, rows, narrow)),
            whole((2, rows, layers * value_width)),
            whole((heads, PACKED, HEAD_DIM)),
            whole((heads, PACKED, HEAD_DIM)),
        ],
        [
            jax.ShapeDtypeStruct((2, rows, narrow), BF16),
            jax.ShapeDtypeStruct((2, rows, narrow), BF16),
            jax.ShapeDtypeStruct((2, rows, layers * value_width), BF16),
            jax.ShapeDtypeStruct((heads, PACKED, HEAD_DIM), BF16),
            jax.ShapeDtypeStruct((heads, PACKED, HEAD_DIM), BF16),
        ],
        (blocks, *mine[1:], *other, w_query, w_key, key_table, key_bias, *weights),
        4 * rows * model * (model // 2 + 2 * narrow),
        [
            pltpu.VMEM((2 * rows, model), BF16),
            pltpu.VMEM((layers, model, value_width), BF16),
            pltpu.VMEM((2, heads * PACKED, rows), BF16),
            pltpu.SemaphoreType.DMA((1 + (layers - 1) * slabs,)),
        ],
    )

    def local(part_of_heads):
        offset = part_of_heads * (layers // 2)
        return call(
            lambda core_ref, *refs: local_kernel(core_ref, per_group, offset, *refs),
            at,
            (2, layers // 2),
            [
                pl.BlockSpec((1, rows, narrow), lambda c, i, _: (c, 0, 0)),
                pl.BlockSpec((1, rows, narrow), lambda c, i, _: (c, 0, 0)),
                pl.BlockSpec((1, rows, value_width), lambda c, i, _: (c, 0, i + offset)),
                pl.BlockSpec((per_group, PACKED, HEAD_DIM), lambda c, i, _: (i + offset, 0, 0)),
                whole((HELD, LANES, PACKED)),
                whole((HELD, LANES, PACKED)),
                whole((2, PACKED)),
            ],
            [
                pl.BlockSpec((1, rows, value_width), lambda c, i, _: (c, 0, i)),
                pl.BlockSpec((1, per_group, rows, PACKED), lambda c, i, _: (c, i, 0, 0)),
            ],
            [
                jax.ShapeDtypeStruct((2, rows, layers * value_width // 2), F32),
                jax.ShapeDtypeStruct((2, heads // 2, rows, PACKED), BF16),
            ],
            (query, key, value, early, query_a, query_b, query_bias),
            heads * rows * rows * 600,
        )

    own = total.reshape(layers, per_group, PACKED, HEAD_DIM)
    line = lax.all_to_all(own, "z", split_axis=0, concat_axis=0, tiled=True)
    num_a, phi_a = local(0)
    line, num_a, phi_a = lax.optimization_barrier((line, num_a, phi_a))
    slab_total = jnp.sum(line.astype(F32), axis=0).astype(BF16)
    totals = [lax.ppermute(slab_total, "seq", flip(m)) for m in range(1, slabs)]
    prefix = pl.pallas_call(
        prefix_kernel,
        in_specs=[pl.BlockSpec(memory_space=pltpu.SMEM)] + [vmem] * slabs,
        out_specs=vmem,
        out_shape=jax.ShapeDtypeStruct(line.shape, BF16),
    )(at, line, *totals)
    prefix = lax.all_to_all(prefix, "z", split_axis=0, concat_axis=0, tiled=True)
    prefix = prefix.reshape(heads, PACKED, HEAD_DIM)
    num_b, phi_b = local(1)

    def hidden(chunk):
        some = rows // 2
        numbers = pl.BlockSpec((1, some, heads * HEAD_DIM // 2), lambda i, _: (chunk, i, 0))
        features = pl.BlockSpec((1, heads // 2, some, PACKED), lambda i, _: (chunk, 0, i, 0))
        return call(
            hidden_kernel,
            at,
            (2,),
            [
                numbers,
                numbers,
                features,
                features,
                whole((heads, PACKED, HEAD_DIM)),
                whole((1, heads * HEAD_DIM)),
            ],
            pl.BlockSpec((some, heads * HEAD_DIM), lambda i, _: (i, 0)),
            jax.ShapeDtypeStruct((rows, heads * HEAD_DIM), BF16),
            (num_a, num_b, phi_a, phi_b, prefix, gain_mine),
            rows * heads * HEAD_DIM * 600,
        )

    w_rows = w_out.reshape(layers, 2, value_width, model)

    def project_out(d):
        columns = lambda at: 2 * lax.rem(at[1] + d, layers) + at[0]
        return call(
            output_kernel,
            at,
            (1,),
            [whole((rows, heads * HEAD_DIM))] * len(chunks)
            + [
                pl.BlockSpec((layers, 1, value_width, width), lambda i, at: (0, at[0], 0, columns(at))),
                pl.BlockSpec((layers, 1, value_width, width), lambda i, at: (0, 1 - at[0], 0, columns(at))),
            ],
            whole((2 * rows, width)),
            jax.ShapeDtypeStruct((2 * rows, width), BF16),
            (*chunks, w_rows, w_rows),
            4 * rows * model * width,
        )

    chunks = []
    for chunk in range(2):
        kept = hidden(chunk)
        chunks += [kept, lax.ppermute(kept, "core", swap)]
    pieces = {}
    for d in list(range(1, layers)) + [0]:
        part_out = project_out(d)
        pieces[d] = lax.ppermute(part_out, "z", turn(d)) if d else part_out
    return call(
        place_kernel,
        at,
        (1,),
        [anywhere] * layers,
        anywhere,
        jax.ShapeDtypeStruct((groups * rows, width), BF16),
        tuple(pieces[d] for d in range(layers)),
        0,
        [pltpu.SemaphoreType.DMA((layers,))],
    )


def solution(mesh):
    slabs, groups = mesh.shape["seq"], mesh.shape["chan"]
    split = jax.sharding.Mesh(mesh.devices.reshape(slabs, groups // 2, 2), ("seq", "z", "core"))
    chan = ("z", "core")
    return jax.shard_map(
        per_device,
        mesh=split,
        in_specs=(P("seq", chan), P(), P(), P(None, chan), P(), P()),
        out_specs=P("seq", chan),
        check_vma=False,
    )
```

```python
import jax
import jax.numpy as jnp
import numpy as np
from jax import lax
from jax.experimental import pallas as pl
from jax.experimental.pallas import tpu as pltpu
from jax.sharding import PartitionSpec as P

HEADS = 16
FEAT = 16
HEAD_DIM = 128
PACKED = 160
LANES = 128
HELD = LANES // FEAT
MIB = 1024 * 1024

F32 = jnp.float32
BF16 = jnp.bfloat16
NN = (((1,), (0,)), ((), ()))
NT = (((1,), (1,)), ((), ()))


def dot(a, b, dims=NN):
    return lax.dot_general(a, b, dims, preferred_element_type=F32)


def feature_tables():
    first = np.zeros((FEAT, PACKED), np.float32)
    second = np.zeros((FEAT, PACKED), np.float32)
    first_bias = np.zeros((PACKED,), np.float32)
    second_bias = np.zeros((PACKED,), np.float32)
    scale = np.zeros((PACKED,), np.float32)
    first_bias[0] = second_bias[0] = scale[0] = 1.0
    place = 1
    for i in range(FEAT):
        first[i, place] = 1.0
        second_bias[place] = 1.0
        scale[place] = 1.0 / 4.0
        place += 1
    for i in range(FEAT):
        for j in range(i, FEAT):
            first[i, place] = 1.0
            second[j, place] = 1.0
            scale[place] = 1.0 / 32.0 if i == j else 1.0 / 16.0
            place += 1
    return first, second, first_bias, second_bias, scale


def placed(table):
    out = np.zeros((HELD, LANES, PACKED), np.float32)
    for place in range(HELD):
        out[place, place * FEAT : (place + 1) * FEAT] = table
    return out


def stacked(table, per_group):
    every = placed(table).transpose(0, 2, 1)
    own = [[p for p in range(HELD) if (p // per_group) % 2 == core] for core in range(2)]
    return np.stack([every[places].reshape(-1, LANES) for places in own])


def project_kernel(at_ref, per_group, layers, gathered, *refs):
    mine, other = refs[:layers], refs[layers : 2 * layers]
    table_ref, bias_ref, wq_ref, wk_ref, own_ref = refs[2 * layers : 2 * layers + 5]
    rest = refs[2 * layers + 5 :]
    weights, rest = rest[:-10], rest[-10:]
    q_ref, k_ref, v_ref, early_ref, total_ref, row_ref, narrow_ref, w_ref, phi_ref, sems = rest
    inner, outer = weights[: len(weights) // 2], weights[len(weights) // 2 :]
    core, layer, slab = at_ref[0], at_ref[1], at_ref[2]
    both, width = other[0].shape
    rows = both // 2
    model = row_ref.shape[1]
    part = inner[0].shape[-2]
    block = v_ref.shape[2] // layers
    narrow = wq_ref.shape[1]
    copies = []

    def fetch(slot, source, to):
        copies.append((slot, pltpu.make_async_copy(source, to, sems.at[len(copies)])))
        copies[-1][1].start()

    fetch(-1, wq_ref, narrow_ref.at[:, pl.ds(0, narrow)])
    fetch(-1, wk_ref, narrow_ref.at[:, pl.ds(narrow, narrow)])
    fetch(0, own_ref, w_ref.at[0, :, pl.ds(0, block)])
    for d in range(1, layers):
        group, index = (outer, 0 if d == 1 else 1) if d in (1, layers - 1) else (inner, d - 2)
        for m in range(model // part):
            if gathered:
                source, start = group[0].at[m, index], m * part
            else:
                source, start = group[m].at[index], pl.multiple_of((slab ^ m) * part, part)
            fetch(d, source, w_ref.at[d // 2, pl.ds(start, part), pl.ds((d % 2) * block, block)])

    def arrived(slots):
        for slot, copy in copies:
            if slot in slots:
                copy.wait()

    for d in range(layers):
        z = lax.rem(layer + layers - d, layers)
        here = pl.multiple_of((2 * z + core) * width, width)
        there = pl.multiple_of((2 * z + 1 - core) * width, width)
        row_ref[:, pl.ds(here, width)] = mine[d][0] if d == 0 else mine[d][...]
        row_ref[:, pl.ds(there, width)] = other[d][...]
    arrived((-1,))
    half = table_ref.shape[1] // 2
    for chunk in range(2):
        at = slice(chunk * rows, (chunk + 1) * rows)
        both_narrow = dot(row_ref[at, :], narrow_ref[...]).astype(BF16)
        q_ref[chunk] = both_narrow[:, :narrow]
        k_ref[chunk] = both_narrow[:, narrow:]
        for lanes in range(0, narrow, LANES):
            product = dot(table_ref[0], both_narrow[:, narrow + lanes : narrow + lanes + LANES], NT)
            left = product[:half] + bias_ref[:, 0:1]
            right = product[half:] + bias_ref[:, 1:2]
            to = (lanes // LANES) * half
            phi_ref[chunk, to : to + half, :] = (left * right).astype(BF16)

    for pair in range(layers // 2):
        arrived((2 * pair, 2 * pair + 1))
        first = []
        for chunk in range(2):
            at = slice(chunk * rows, (chunk + 1) * rows)
            value = dot(row_ref[at, :], w_ref[pair]).astype(BF16)
            for d in (2 * pair, 2 * pair + 1):
                z = lax.rem(layer + d, layers)
                side = (d % 2) * block
                v_ref[chunk, :, pl.ds(pl.multiple_of(z * block, block), block)] = value[:, side : side + block]
                for i in range(per_group):
                    head = z * per_group + i
                    phi = phi_ref[chunk, pl.ds(pl.multiple_of(head * PACKED, PACKED), PACKED), :]
                    lanes = side + i * HEAD_DIM
                    state = dot(phi, value[:, lanes : lanes + HEAD_DIM])
                    if chunk == 0:
                        early_ref[head] = state.astype(BF16)
                        first.append(state)
                    else:
                        total_ref[head] = (first.pop(0) + state).astype(BF16)


def local_kernel(
    core_ref, per_group, offset, q_ref, k_ref, v_ref, early_ref, ta_ref, tb_ref, bias_ref, num_ref, phi_ref
):
    chunk = pl.program_id(0)
    step = pl.program_id(1) + offset
    rows = q_ref.shape[1]
    half = rows // 2
    for i in range(per_group):
        head = (2 * step + core_ref[0]) * per_group + i
        lanes = pl.multiple_of((head // HELD) * LANES, LANES)
        place = lax.rem(head, HELD)
        query = q_ref[0, :, pl.ds(lanes, LANES)]
        key = k_ref[0, :, pl.ds(lanes, LANES)]
        left = dot(query, ta_ref[place]) + bias_ref[0:1]
        right = dot(query, tb_ref[place]) + bias_ref[1:2]
        phi_ref[0, i] = (left * right).astype(BF16)
        lane = lax.broadcasted_iota(jnp.int32, (rows, LANES), 1)
        mine = jnp.where(lane // FEAT == place, query * jnp.asarray(0.25, BF16), jnp.zeros_like(query))
        columns = slice(i * HEAD_DIM, (i + 1) * HEAD_DIM)
        for low in (0, half):
            seen = low + half
            s = dot(mine[low:seen], key[:seen], NT)
            weight = 1.0 + s + 0.5 * s * s
            t_at = lax.broadcasted_iota(jnp.int32, (half, seen), 0) + low
            j_at = lax.broadcasted_iota(jnp.int32, (half, seen), 1)
            weight = jnp.where(t_at >= j_at, weight, 0.0).astype(BF16)
            num_ref[0, low:seen, columns] = dot(weight, v_ref[0, :seen, columns])

        @pl.when(chunk == 1)
        def _():
            num_ref[0, :, columns] += dot(phi_ref[0, i], early_ref[i])


def prefix_kernel(at_ref, line_ref, *refs):
    totals, out_ref = refs[:-1], refs[-1]
    slab = at_ref[2]
    run = jnp.zeros(line_ref.shape[1:], F32)
    for m, total in enumerate(totals, 1):
        run = run + total[...].astype(F32) * jnp.where((slab ^ m) < slab, 1.0, 0.0)
    for z in range(line_ref.shape[0]):
        out_ref[z] = run.astype(BF16)
        run = run + line_ref[z].astype(F32)


def hidden_kernel(at_ref, state_ref, gain_ref, *refs):
    parts, out_ref = refs[:-1], refs[-1]
    numbers, features = parts[: len(parts) // 2], parts[len(parts) // 2 :]
    held = features[0].shape[1]
    for i in range(held * len(features)):
        columns = slice(i * HEAD_DIM, (i + 1) * HEAD_DIM)
        at = (i % held) * HEAD_DIM
        num = numbers[i // held][0, :, at : at + HEAD_DIM]
        num = num + dot(features[i // held][0, i % held], state_ref[i])
        mean_square = jnp.mean(num * num, axis=1, keepdims=True)
        hidden = num * lax.rsqrt(mean_square + 1e-05) * gain_ref[:, columns]
        out_ref[:, columns] = hidden.astype(BF16)


def output_kernel(at_ref, mine_ref, other_ref, w_mine, w_other, out_ref):
    depth = mine_ref.shape[1]
    width = out_ref.shape[1]
    part = dot(mine_ref[...], w_mine[...].reshape(depth, width))
    part = part + dot(other_ref[...], w_other[...].reshape(depth, width))
    out_ref[...] = part.astype(BF16)


def place_kernel(at_ref, *refs):
    pieces, out_ref, sems = refs[:-2], refs[-2], refs[-1]
    layers = len(pieces) // 2
    copies = []
    for i, piece in enumerate(pieces):
        rows = piece.shape[0]
        z = lax.rem(at_ref[1] + layers - i // 2, layers)
        to = out_ref.at[pl.ds(pl.multiple_of((2 * z + i % 2) * rows, rows), rows)]
        copies.append(pltpu.make_async_copy(piece, to, sems.at[i]))
    for copy in copies:
        copy.start()
    for copy in copies:
        copy.wait()


def whole(shape):
    return pl.BlockSpec(shape, lambda *_: (0,) * len(shape))


def params(mib):
    return pltpu.CompilerParams(vmem_limit_bytes=mib * MIB)


def call(kernel, scalar, grid, in_specs, out_specs, out_shape, args, flops, scratch=(), mib=60):
    return pl.pallas_call(
        kernel,
        grid_spec=pltpu.PrefetchScalarGridSpec(
            num_scalar_prefetch=1,
            grid=grid,
            in_specs=in_specs,
            out_specs=out_specs,
            scratch_shapes=list(scratch),
        ),
        out_shape=out_shape,
        compiler_params=params(mib),
        cost_estimate=pl.CostEstimate(flops=flops, bytes_accessed=12 * MIB, transcendentals=0),
    )(scalar, *args)


def per_device(tokens, w_query, w_key, w_value, w_out, gain):
    slabs = lax.axis_size("seq")
    layers = lax.axis_size("z")
    groups = 2 * layers
    my_slab = lax.axis_index("seq")
    core = lax.axis_index("core").astype(jnp.int32)
    layer = lax.axis_index("z").astype(jnp.int32)
    which = core.reshape(1)
    width = tokens.shape[1]
    rows = tokens.shape[0] // groups
    model, value_width = w_value.shape
    part = model // slabs
    per_group = HEADS // groups
    heads = HEADS // 2
    narrow = w_query.shape[1]
    swap = [(0, 1), (1, 0)]

    first, second, first_bias, second_bias, scale = feature_tables()
    sides = [stacked(first, per_group), stacked(second, per_group)]
    key_table = jnp.asarray(np.concatenate(sides, axis=1), BF16)
    repeat = HELD // 2
    key_bias = jnp.asarray(np.stack([np.tile(first_bias, repeat), np.tile(second_bias, repeat)], axis=1))
    query_a = jnp.asarray(placed(first * scale), BF16)
    query_b = jnp.asarray(placed(second), BF16)
    query_bias = jnp.asarray(np.stack([first_bias * scale, second_bias]))
    gain_mine = lax.dynamic_index_in_dim(gain.reshape(layers, 2, value_width), core, 1, False)
    gain_mine = gain_mine.reshape(1, layers * value_width)

    flip = lambda m: [(s, s ^ m) for s in range(slabs)]
    turn = lambda d: [(z, (z + d) % layers) for z in range(layers)]
    anywhere = pl.BlockSpec(memory_space=pl.ANY)
    vmem = pl.BlockSpec(memory_space=pltpu.VMEM)
    at = jnp.stack([core, layer, my_slab.astype(jnp.int32)])

    value_part = lax.dynamic_slice_in_dim(w_value, my_slab * part, part, 0)
    up, down = {0: value_part}, {0: value_part}
    blocks = tokens.reshape(layers, 2 * rows, width)
    sent = [lax.dynamic_index_in_dim(blocks, lax.rem(layer + d, layers), 0, False) for d in range(layers)]
    for k in range(1, layers):
        up[k] = lax.ppermute(up[k - 1], "z", [(z, z + 1) for z in range(k - 1, layers - 1)])
        down[k] = lax.ppermute(down[k - 1], "z", [(z, z - 1) for z in range(1, layers - k + 1)])
        if k == layers - 2:
            up[k], down[k], sent = lax.optimization_barrier((up[k], down[k], sent))
    slot = lambda d: jnp.where(layer + d < layers, down[d], up[layers - d])

    def to_lines(chosen):
        stack = jnp.stack([slot(d) for d in chosen])
        if slabs == 4:
            return [stack] + [lax.ppermute(stack, "seq", flip(m)) for m in range(1, slabs)]
        return [lax.all_gather(stack, "seq", axis=0, tiled=False)]

    mine = [sent[0]] + [lax.ppermute(sent[d], "z", turn(d)) for d in range(1, layers)]
    inner = to_lines(range(2, layers - 1))
    outer = to_lines((1, layers - 1))
    far = layers // 2
    mine[far], outer[-1] = lax.optimization_barrier((mine[far], outer[-1]))
    other = [lax.ppermute(piece, "core", swap) for piece in mine]
    weights = inner + outer

    query, key, value, early, total = call(
        lambda at_ref, *refs: project_kernel(at_ref, per_group, layers, slabs != 4, *refs),
        at,
        (1,),
        [pl.BlockSpec((1, 2 * rows, width), lambda i, at: (at[1], 0, 0))]
        + [whole((2 * rows, width))] * (2 * layers - 1)
        + [
            pl.BlockSpec((1,) + key_table.shape[1:], lambda i, at: (at[0], 0, 0)),
            whole(key_bias.shape),
        ]
        + [anywhere] * (3 + len(weights)),
        [
            whole((2, rows, narrow)),
            whole((2, rows, narrow)),
            whole((2, rows, layers * value_width)),
            whole((heads, PACKED, HEAD_DIM)),
            whole((heads, PACKED, HEAD_DIM)),
        ],
        [
            jax.ShapeDtypeStruct((2, rows, narrow), BF16),
            jax.ShapeDtypeStruct((2, rows, narrow), BF16),
            jax.ShapeDtypeStruct((2, rows, layers * value_width), BF16),
            jax.ShapeDtypeStruct((heads, PACKED, HEAD_DIM), BF16),
            jax.ShapeDtypeStruct((heads, PACKED, HEAD_DIM), BF16),
        ],
        (blocks, *mine[1:], *other, key_table, key_bias, w_query, w_key, w_value, *weights),
        4 * rows * model * (model // 2 + 2 * narrow),
        [
            pltpu.VMEM((2 * rows, model), BF16),
            pltpu.VMEM((model, 2 * narrow), BF16),
            pltpu.VMEM((layers // 2, model, 2 * value_width), BF16),
            pltpu.VMEM((2, heads * PACKED, rows), BF16),
            pltpu.SemaphoreType.DMA((3 + (layers - 1) * slabs,)),
        ],
    )

    parts = 4
    some_layers = layers // parts

    def local(index):
        offset = index * some_layers
        return call(
            lambda core_ref, *refs: local_kernel(core_ref, per_group, offset, *refs),
            at,
            (2, some_layers),
            [
                pl.BlockSpec((1, rows, narrow), lambda c, i, _: (c, 0, 0)),
                pl.BlockSpec((1, rows, narrow), lambda c, i, _: (c, 0, 0)),
                pl.BlockSpec((1, rows, value_width), lambda c, i, _: (c, 0, i + offset)),
                pl.BlockSpec((per_group, PACKED, HEAD_DIM), lambda c, i, _: (i + offset, 0, 0)),
                whole((HELD, LANES, PACKED)),
                whole((HELD, LANES, PACKED)),
                whole((2, PACKED)),
            ],
            [
                pl.BlockSpec((1, rows, value_width), lambda c, i, _: (c, 0, i)),
                pl.BlockSpec((1, per_group, rows, PACKED), lambda c, i, _: (c, i, 0, 0)),
            ],
            [
                jax.ShapeDtypeStruct((2, rows, some_layers * value_width), F32),
                jax.ShapeDtypeStruct((2, heads // parts, rows, PACKED), BF16),
            ],
            (query, key, value, early, query_a, query_b, query_bias),
            heads * rows * rows * 300,
        )

    own = total.reshape(layers, per_group, PACKED, HEAD_DIM)
    line = lax.all_to_all(own, "z", split_axis=0, concat_axis=0, tiled=True)
    locals_ = [local(0), local(1)]
    line, locals_ = lax.optimization_barrier((line, locals_))
    slab_total = jnp.sum(line.astype(F32), axis=0).astype(BF16)
    totals = [lax.ppermute(slab_total, "seq", flip(m)) for m in range(1, slabs)]
    third = local(2)
    totals, third = lax.optimization_barrier((totals, third))
    prefix = pl.pallas_call(
        prefix_kernel,
        in_specs=[pl.BlockSpec(memory_space=pltpu.SMEM)] + [vmem] * slabs,
        out_specs=vmem,
        out_shape=jax.ShapeDtypeStruct(line.shape, BF16),
    )(at, line, *totals)
    prefix = lax.all_to_all(prefix, "z", split_axis=0, concat_axis=0, tiled=True)
    prefix = prefix.reshape(heads, PACKED, HEAD_DIM)
    locals_ = locals_ + [third, local(3)]

    def hidden(chunk):
        some = rows // 2
        numbers = pl.BlockSpec((1, some, heads * HEAD_DIM // parts), lambda i, _: (chunk, i, 0))
        features = pl.BlockSpec((1, heads // parts, some, PACKED), lambda i, _: (chunk, 0, i, 0))
        return call(
            hidden_kernel,
            at,
            (2,),
            [whole((heads, PACKED, HEAD_DIM)), whole((1, heads * HEAD_DIM))]
            + [numbers] * parts
            + [features] * parts,
            pl.BlockSpec((some, heads * HEAD_DIM), lambda i, _: (i, 0)),
            jax.ShapeDtypeStruct((rows, heads * HEAD_DIM), BF16),
            (prefix, gain_mine, *(num for num, _ in locals_), *(phi for _, phi in locals_)),
            rows * heads * HEAD_DIM * 600,
        )

    w_rows = w_out.reshape(layers, 2, value_width, model)

    def project_out(kept, received, d):
        columns = lambda at: 2 * lax.rem(at[1] + d, layers) + at[0]
        return call(
            output_kernel,
            at,
            (1,),
            [
                whole((rows, heads * HEAD_DIM)),
                whole((rows, heads * HEAD_DIM)),
                pl.BlockSpec((layers, 1, value_width, width), lambda i, at: (0, at[0], 0, columns(at))),
                pl.BlockSpec((layers, 1, value_width, width), lambda i, at: (0, 1 - at[0], 0, columns(at))),
            ],
            whole((rows, width)),
            jax.ShapeDtypeStruct((rows, width), BF16),
            (kept, received, w_rows, w_rows),
            2 * rows * model * width,
        )

    kept = [hidden(chunk) for chunk in range(2)]
    received = [lax.ppermute(half, "core", swap) for half in kept]
    pieces = {}
    for chunk in range(2):
        for d in range(1, layers):
            piece = project_out(kept[chunk], received[chunk], d)
            pieces[d, chunk] = lax.ppermute(piece, "z", turn(d))
    for chunk in range(2):
        pieces[0, chunk] = project_out(kept[chunk], received[chunk], 0)
    return call(
        place_kernel,
        at,
        (1,),
        [vmem] * (2 * layers),
        anywhere,
        jax.ShapeDtypeStruct((groups * rows, width), BF16),
        tuple(pieces[d, chunk] for d in range(layers) for chunk in range(2)),
        0,
        [pltpu.SemaphoreType.DMA((2 * layers,))],
        mib=8,
    )


def solution(mesh):
    slabs, groups = mesh.shape["seq"], mesh.shape["chan"]
    split = jax.sharding.Mesh(mesh.devices.reshape(slabs, groups // 2, 2), ("seq", "z", "core"))
    chan = ("z", "core")
    return jax.shard_map(
        per_device,
        mesh=split,
        in_specs=(P("seq", chan), P(), P(), P(None, chan), P(), P()),
        out_specs=P("seq", chan),
        check_vma=False,
    )
```

```python
import jax
import jax.numpy as jnp
import numpy as np
from jax import lax
from jax.experimental import pallas as pl
from jax.experimental.pallas import tpu as pltpu
from jax.sharding import PartitionSpec as P

HEADS = 16
FEAT = 16
HEAD_DIM = 128
PACKED = 160
LANES = 128
HELD = LANES // FEAT
MIB = 1024 * 1024

F32 = jnp.float32
BF16 = jnp.bfloat16
NN = (((1,), (0,)), ((), ()))
NT = (((1,), (1,)), ((), ()))


def dot(a, b, dims=NN):
    return lax.dot_general(a, b, dims, preferred_element_type=F32)


def feature_tables():
    first = np.zeros((FEAT, PACKED), np.float32)
    second = np.zeros((FEAT, PACKED), np.float32)
    first_bias = np.zeros((PACKED,), np.float32)
    second_bias = np.zeros((PACKED,), np.float32)
    scale = np.zeros((PACKED,), np.float32)
    first_bias[0] = second_bias[0] = scale[0] = 1.0
    place = 1
    for i in range(FEAT):
        first[i, place] = 1.0
        second_bias[place] = 1.0
        scale[place] = 1.0 / 4.0
        place += 1
    for i in range(FEAT):
        for j in range(i, FEAT):
            first[i, place] = 1.0
            second[j, place] = 1.0
            scale[place] = 1.0 / 32.0 if i == j else 1.0 / 16.0
            place += 1
    return first, second, first_bias, second_bias, scale


def placed(table):
    out = np.zeros((HELD, LANES, PACKED), np.float32)
    for place in range(HELD):
        out[place, place * FEAT : (place + 1) * FEAT] = table
    return out


def stacked(table, per_group):
    every = placed(table).transpose(0, 2, 1)
    own = [[p for p in range(HELD) if (p // per_group) % 2 == core] for core in range(2)]
    return np.stack([every[places].reshape(-1, LANES) for places in own])


def project_kernel(at_ref, per_group, layers, gathered, *refs):
    mine, other = refs[:layers], refs[layers : 2 * layers]
    table_ref, bias_ref, wq_ref, wk_ref, own_ref = refs[2 * layers : 2 * layers + 5]
    rest = refs[2 * layers + 5 :]
    weights, rest = rest[:-10], rest[-10:]
    q_ref, k_ref, v_ref, early_ref, total_ref, row_ref, narrow_ref, w_ref, phi_ref, sems = rest
    core, layer, slab = at_ref[0], at_ref[1], at_ref[2]
    both, width = other[0].shape
    rows = both // 2
    model = row_ref.shape[1]
    part = weights[0].shape[-2]
    block = v_ref.shape[2] // layers
    narrow = wq_ref.shape[1]
    copies = []

    def fetch(slot, source, to):
        copies.append((slot, pltpu.make_async_copy(source, to, sems.at[len(copies)])))
        copies[-1][1].start()

    fetch(-1, wq_ref, narrow_ref.at[:, pl.ds(0, narrow)])
    fetch(-1, wk_ref, narrow_ref.at[:, pl.ds(narrow, narrow)])
    fetch(0, own_ref, w_ref.at[0, :, pl.ds(0, block)])
    for d in range(1, layers):
        for m in range(model // part):
            if gathered:
                source, start = weights[0].at[m, d - 1], m * part
            else:
                source, start = weights[m].at[d - 1], pl.multiple_of((slab ^ m) * part, part)
            fetch(d, source, w_ref.at[d // 2, pl.ds(start, part), pl.ds((d % 2) * block, block)])

    def arrived(slots):
        for slot, copy in copies:
            if slot in slots:
                copy.wait()

    for d in range(layers):
        z = lax.rem(layer + layers - d, layers)
        here = pl.multiple_of((2 * z + core) * width, width)
        there = pl.multiple_of((2 * z + 1 - core) * width, width)
        row_ref[:, pl.ds(here, width)] = mine[d][0] if d == 0 else mine[d][...]
        row_ref[:, pl.ds(there, width)] = other[d][...]
    arrived((-1,))
    half = table_ref.shape[1] // 2
    for chunk in range(2):
        at = slice(chunk * rows, (chunk + 1) * rows)
        both_narrow = dot(row_ref[at, :], narrow_ref[...]).astype(BF16)
        q_ref[chunk] = both_narrow[:, :narrow]
        k_ref[chunk] = both_narrow[:, narrow:]
        for lanes in range(0, narrow, LANES):
            product = dot(table_ref[0], both_narrow[:, narrow + lanes : narrow + lanes + LANES], NT)
            left = product[:half] + bias_ref[:, 0:1]
            right = product[half:] + bias_ref[:, 1:2]
            to = (lanes // LANES) * half
            phi_ref[chunk, to : to + half, :] = (left * right).astype(BF16)

    for pair in range(layers // 2):
        arrived((2 * pair, 2 * pair + 1))
        first = []
        for chunk in range(2):
            at = slice(chunk * rows, (chunk + 1) * rows)
            value = dot(row_ref[at, :], w_ref[pair]).astype(BF16)
            for d in (2 * pair, 2 * pair + 1):
                z = lax.rem(layer + d, layers)
                side = (d % 2) * block
                v_ref[chunk, :, pl.ds(pl.multiple_of(z * block, block), block)] = value[:, side : side + block]
                for i in range(per_group):
                    head = z * per_group + i
                    phi = phi_ref[chunk, pl.ds(pl.multiple_of(head * PACKED, PACKED), PACKED), :]
                    lanes = side + i * HEAD_DIM
                    state = dot(phi, value[:, lanes : lanes + HEAD_DIM])
                    if chunk == 0:
                        early_ref[head] = state.astype(BF16)
                        first.append(state)
                    else:
                        total_ref[head] = (first.pop(0) + state).astype(BF16)


def local_kernel(core_ref, per_group, offset, q_ref, k_ref, v_ref, early_ref, table_ref, bias_ref, num_ref, phi_ref):
    chunk = pl.program_id(0)
    step = pl.program_id(1) + offset
    rows = q_ref.shape[1]
    cut = LANES * -(-rows // (2 * LANES))
    wide = table_ref.shape[2] // 2
    for i in range(per_group):
        head = (2 * step + core_ref[0]) * per_group + i
        lanes = pl.multiple_of((head // HELD) * LANES, LANES)
        place = lax.rem(head, HELD)
        query = q_ref[0, :, pl.ds(lanes, LANES)]
        key = k_ref[0, :, pl.ds(lanes, LANES)]
        sides = dot(query, table_ref[place]) + bias_ref[...]
        phi_ref[0, i] = (sides[:, :PACKED] * sides[:, wide : wide + PACKED]).astype(BF16)
        lane = lax.broadcasted_iota(jnp.int32, (rows, LANES), 1)
        mine = jnp.where(lane // FEAT == place, query * jnp.asarray(0.25, BF16), jnp.zeros_like(query))
        columns = slice(i * HEAD_DIM, (i + 1) * HEAD_DIM)
        for low, high in ((0, cut), (cut, rows)):
            span = high - low
            s = dot(mine[low:high], key[low:high], NT)
            t_at = lax.broadcasted_iota(jnp.int32, (span, span), 0)
            j_at = lax.broadcasted_iota(jnp.int32, (span, span), 1)
            weight = jnp.where(t_at >= j_at, (0.5 * s + 1.0) * s + 1.0, 0.0).astype(BF16)
            num = dot(weight, v_ref[0, low:high, columns])
            if low > 0:
                s = dot(mine[low:high], key[:low], NT)
                weight = ((0.5 * s + 1.0) * s + 1.0).astype(BF16)
                num = num + dot(weight, v_ref[0, :low, columns])
            num_ref[0, low:high, columns] = num

        @pl.when(chunk == 1)
        def _():
            num_ref[0, :, columns] += dot(phi_ref[0, i], early_ref[i])


def prefix_kernel(at_ref, line_ref, *refs):
    totals, out_ref = refs[:-1], refs[-1]
    slab = at_ref[2]
    run = jnp.zeros(line_ref.shape[1:], F32)
    for m, total in enumerate(totals, 1):
        run = run + total[...].astype(F32) * jnp.where((slab ^ m) < slab, 1.0, 0.0)
    for z in range(line_ref.shape[0]):
        out_ref[z] = run.astype(BF16)
        run = run + line_ref[z].astype(F32)


def hidden_kernel(at_ref, state_ref, gain_ref, *refs):
    parts, out_ref = refs[:-1], refs[-1]
    numbers, features = parts[: len(parts) // 2], parts[len(parts) // 2 :]
    held = features[0].shape[1]
    ones = jnp.full((HEAD_DIM, HEAD_DIM), 1.0 / HEAD_DIM, BF16)
    for i in range(held * len(features)):
        columns = slice(i * HEAD_DIM, (i + 1) * HEAD_DIM)
        at = (i % held) * HEAD_DIM
        num = numbers[i // held][0, :, at : at + HEAD_DIM]
        num = num + dot(features[i // held][0, i % held], state_ref[i])
        mean_square = dot((num * num).astype(BF16), ones)
        hidden = num * lax.rsqrt(mean_square + 1e-05) * gain_ref[:, columns]
        out_ref[:, columns] = hidden.astype(BF16)


def output_kernel(at_ref, mine_ref, other_ref, *refs):
    outs = refs[len(refs) * 2 // 3 :]
    weights = [w[...].reshape(mine_ref.shape[1], -1) for w in refs[: 2 * len(outs)]]
    width = weights[0].shape[1]
    part = dot(mine_ref[...], jnp.concatenate(weights[0::2], axis=1))
    part = part + dot(other_ref[...], jnp.concatenate(weights[1::2], axis=1))
    for i, out_ref in enumerate(outs):
        out_ref[...] = part[:, i * width : (i + 1) * width].astype(BF16)


def place_kernel(at_ref, *refs):
    pieces, out_ref, sems = refs[:-2], refs[-2], refs[-1]
    layers = len(pieces) // 2
    copies = []
    for i, piece in enumerate(pieces):
        rows = piece.shape[0]
        z = lax.rem(at_ref[1] + layers - i // 2, layers)
        to = out_ref.at[pl.ds(pl.multiple_of((2 * z + i % 2) * rows, rows), rows)]
        copies.append(pltpu.make_async_copy(piece, to, sems.at[i]))
    for copy in copies:
        copy.start()
    for copy in copies:
        copy.wait()


def whole(shape):
    return pl.BlockSpec(shape, lambda *_: (0,) * len(shape))


def params(mib):
    return pltpu.CompilerParams(vmem_limit_bytes=mib * MIB)


def call(kernel, scalar, grid, in_specs, out_specs, out_shape, args, flops, scratch=(), mib=60):
    return pl.pallas_call(
        kernel,
        grid_spec=pltpu.PrefetchScalarGridSpec(
            num_scalar_prefetch=1,
            grid=grid,
            in_specs=in_specs,
            out_specs=out_specs,
            scratch_shapes=list(scratch),
        ),
        out_shape=out_shape,
        compiler_params=params(mib),
        cost_estimate=pl.CostEstimate(flops=flops, bytes_accessed=12 * MIB, transcendentals=0),
    )(scalar, *args)


def per_device(tokens, w_query, w_key, w_value, w_out, gain):
    slabs = lax.axis_size("seq")
    layers = lax.axis_size("z")
    groups = 2 * layers
    my_slab = lax.axis_index("seq")
    core = lax.axis_index("core").astype(jnp.int32)
    layer = lax.axis_index("z").astype(jnp.int32)
    which = core.reshape(1)
    width = tokens.shape[1]
    rows = tokens.shape[0] // groups
    model, value_width = w_value.shape
    part = model // slabs
    per_group = HEADS // groups
    heads = HEADS // 2
    narrow = w_query.shape[1]
    swap = [(0, 1), (1, 0)]

    first, second, first_bias, second_bias, scale = feature_tables()
    sides = [stacked(first, per_group), stacked(second, per_group)]
    key_table = jnp.asarray(np.concatenate(sides, axis=1), BF16)
    repeat = HELD // 2
    key_bias = jnp.asarray(np.stack([np.tile(first_bias, repeat), np.tile(second_bias, repeat)], axis=1))
    wide = 2 * LANES
    query_table = np.zeros((HELD, LANES, 2 * wide), np.float32)
    query_bias = np.zeros((1, 2 * wide), np.float32)
    query_table[:, :, :PACKED] = placed(first * scale)
    query_table[:, :, wide : wide + PACKED] = placed(second)
    query_bias[0, :PACKED] = first_bias * scale
    query_bias[0, wide : wide + PACKED] = second_bias
    query_table, query_bias = jnp.asarray(query_table, BF16), jnp.asarray(query_bias)
    gain_mine = lax.dynamic_index_in_dim(gain.reshape(layers, 2, value_width), core, 1, False)
    gain_mine = gain_mine.reshape(1, layers * value_width)

    flip = lambda m: [(s, s ^ m) for s in range(slabs)]
    turn = lambda d: [(z, (z + d) % layers) for z in range(layers)]
    anywhere = pl.BlockSpec(memory_space=pl.ANY)
    vmem = pl.BlockSpec(memory_space=pltpu.VMEM)
    at = jnp.stack([core, layer, my_slab.astype(jnp.int32)])

    value_part = lax.dynamic_slice_in_dim(w_value, my_slab * part, part, 0)
    up, down = {0: value_part}, {0: value_part}
    blocks = tokens.reshape(layers, 2 * rows, width)
    sent = [lax.dynamic_index_in_dim(blocks, lax.rem(layer + d, layers), 0, False) for d in range(layers)]
    for k in range(1, layers):
        up[k] = lax.ppermute(up[k - 1], "z", [(z, z + 1) for z in range(k - 1, layers - 1)])
        down[k] = lax.ppermute(down[k - 1], "z", [(z, z - 1) for z in range(1, layers - k + 1)])
    stack = jnp.stack([jnp.where(layer + d < layers, down[d], up[layers - d]) for d in range(1, layers)])
    stack, sent = lax.optimization_barrier((stack, sent))
    if slabs == 4:
        weights = [stack] + [lax.ppermute(stack, "seq", flip(m)) for m in range(1, slabs)]
    else:
        weights = [lax.all_gather(stack, "seq", axis=0, tiled=False)]
    far = layers // 2
    mine = {d: lax.ppermute(sent[d], "z", turn(d)) for d in [far] + [d for d in range(1, layers) if d != far]}
    mine = [sent[0]] + [mine[d] for d in range(1, layers)]
    mine[far], weights[1:] = lax.optimization_barrier((mine[far], weights[1:]))
    other = [lax.ppermute(piece, "core", swap) for piece in mine]

    query, key, value, early, total = call(
        lambda at_ref, *refs: project_kernel(at_ref, per_group, layers, slabs != 4, *refs),
        at,
        (1,),
        [pl.BlockSpec((1, 2 * rows, width), lambda i, at: (at[1], 0, 0))]
        + [whole((2 * rows, width))] * (2 * layers - 1)
        + [
            pl.BlockSpec((1,) + key_table.shape[1:], lambda i, at: (at[0], 0, 0)),
            whole(key_bias.shape),
        ]
        + [anywhere] * (3 + len(weights)),
        [
            whole((2, rows, narrow)),
            whole((2, rows, narrow)),
            whole((2, rows, layers * value_width)),
            whole((heads, PACKED, HEAD_DIM)),
            whole((heads, PACKED, HEAD_DIM)),
        ],
        [
            jax.ShapeDtypeStruct((2, rows, narrow), BF16),
            jax.ShapeDtypeStruct((2, rows, narrow), BF16),
            jax.ShapeDtypeStruct((2, rows, layers * value_width), BF16),
            jax.ShapeDtypeStruct((heads, PACKED, HEAD_DIM), BF16),
            jax.ShapeDtypeStruct((heads, PACKED, HEAD_DIM), BF16),
        ],
        (blocks, *mine[1:], *other, key_table, key_bias, w_query, w_key, w_value, *weights),
        4 * rows * model * (model // 2 + 2 * narrow),
        [
            pltpu.VMEM((2 * rows, model), BF16),
            pltpu.VMEM((model, 2 * narrow), BF16),
            pltpu.VMEM((layers // 2, model, 2 * value_width), BF16),
            pltpu.VMEM((2, heads * PACKED, rows), BF16),
            pltpu.SemaphoreType.DMA((3 + (layers - 1) * slabs,)),
        ],
    )

    parts = 4
    some_layers = layers // parts

    def local(index):
        offset = index * some_layers
        return call(
            lambda core_ref, *refs: local_kernel(core_ref, per_group, offset, *refs),
            at,
            (2, some_layers),
            [
                pl.BlockSpec((1, rows, narrow), lambda c, i, _: (c, 0, 0)),
                pl.BlockSpec((1, rows, narrow), lambda c, i, _: (c, 0, 0)),
                pl.BlockSpec((1, rows, value_width), lambda c, i, _: (c, 0, i + offset)),
                pl.BlockSpec((per_group, PACKED, HEAD_DIM), lambda c, i, _: (i + offset, 0, 0)),
                whole(query_table.shape),
                whole(query_bias.shape),
            ],
            [
                pl.BlockSpec((1, rows, value_width), lambda c, i, _: (c, 0, i)),
                pl.BlockSpec((1, per_group, rows, PACKED), lambda c, i, _: (c, i, 0, 0)),
            ],
            [
                jax.ShapeDtypeStruct((2, rows, some_layers * value_width), F32),
                jax.ShapeDtypeStruct((2, heads // parts, rows, PACKED), BF16),
            ],
            (query, key, value, early, query_table, query_bias),
            heads * rows * rows * 300,
        )

    own = total.reshape(layers, per_group, PACKED, HEAD_DIM)
    line = lax.all_to_all(own, "z", split_axis=0, concat_axis=0, tiled=True)
    locals_ = [local(0), local(1)]
    line, locals_ = lax.optimization_barrier((line, locals_))
    slab_total = jnp.sum(line.astype(F32), axis=0).astype(BF16)
    totals = [lax.ppermute(slab_total, "seq", flip(m)) for m in range(1, slabs)]
    third = local(2)
    totals, third = lax.optimization_barrier((totals, third))
    prefix = pl.pallas_call(
        prefix_kernel,
        in_specs=[pl.BlockSpec(memory_space=pltpu.SMEM)] + [vmem] * slabs,
        out_specs=vmem,
        out_shape=jax.ShapeDtypeStruct(line.shape, BF16),
    )(at, line, *totals)
    prefix = lax.all_to_all(prefix, "z", split_axis=0, concat_axis=0, tiled=True)
    prefix = prefix.reshape(heads, PACKED, HEAD_DIM)
    locals_ = locals_ + [third, local(3)]

    def hidden(chunk):
        some = rows // 2
        numbers = pl.BlockSpec((1, some, heads * HEAD_DIM // parts), lambda i, _: (chunk, i, 0))
        features = pl.BlockSpec((1, heads // parts, some, PACKED), lambda i, _: (chunk, 0, i, 0))
        return call(
            hidden_kernel,
            at,
            (2,),
            [whole((heads, PACKED, HEAD_DIM)), whole((1, heads * HEAD_DIM))]
            + [numbers] * parts
            + [features] * parts,
            pl.BlockSpec((some, heads * HEAD_DIM), lambda i, _: (i, 0)),
            jax.ShapeDtypeStruct((rows, heads * HEAD_DIM), BF16),
            (prefix, gain_mine, *(num for num, _ in locals_), *(phi for _, phi in locals_)),
            rows * heads * HEAD_DIM * 600,
        )

    w_rows = w_out.reshape(layers, 2, value_width, model)

    def project_out(kept, received, to):
        block = (layers, 1, value_width, width)
        specs = []
        for d in to:
            columns = lambda at, d=d: 2 * lax.rem(at[1] + d, layers) + at[0]
            specs.append(pl.BlockSpec(block, lambda i, at, columns=columns: (0, at[0], 0, columns(at))))
            specs.append(pl.BlockSpec(block, lambda i, at, columns=columns: (0, 1 - at[0], 0, columns(at))))
        return call(
            output_kernel,
            at,
            (1,),
            [whole((rows, heads * HEAD_DIM))] * 2 + specs,
            [whole((rows, width))] * len(to),
            [jax.ShapeDtypeStruct((rows, width), BF16)] * len(to),
            (kept, received, *[w_rows] * len(specs)),
            2 * rows * model * width * len(to),
        )

    kept = [hidden(chunk) for chunk in range(2)]
    received = [lax.ppermute(half, "core", swap) for half in kept]
    order = [far] + [d for d in range(1, layers) if d != far] + [0]
    pieces = {}
    for start in range(0, layers, 2):
        to = order[start : start + 2]
        for chunk in range(2):
            for d, piece in zip(to, project_out(kept[chunk], received[chunk], to)):
                pieces[d, chunk] = lax.ppermute(piece, "z", turn(d)) if d else piece
    return call(
        place_kernel,
        at,
        (1,),
        [vmem] * (2 * layers),
        anywhere,
        jax.ShapeDtypeStruct((groups * rows, width), BF16),
        tuple(pieces[d, chunk] for d in range(layers) for chunk in range(2)),
        0,
        [pltpu.SemaphoreType.DMA((2 * layers,))],
        mib=8,
    )


def solution(mesh):
    slabs, groups = mesh.shape["seq"], mesh.shape["chan"]
    split = jax.sharding.Mesh(mesh.devices.reshape(slabs, groups // 2, 2), ("seq", "z", "core"))
    chan = ("z", "core")
    return jax.shard_map(
        per_device,
        mesh=split,
        in_specs=(P("seq", chan), P(), P(), P(None, chan), P(), P()),
        out_specs=P("seq", chan),
        check_vma=False,
    )
```

```python
import jax
import jax.numpy as jnp
import numpy as np
from jax import lax
from jax.experimental import pallas as pl
from jax.experimental.pallas import tpu as pltpu
from jax.sharding import PartitionSpec as P

HEADS = 16
FEAT = 16
HEAD_DIM = 128
PACKED = 160
LANES = 128
HELD = LANES // FEAT
MIB = 1024 * 1024

F32 = jnp.float32
BF16 = jnp.bfloat16
NN = (((1,), (0,)), ((), ()))
NT = (((1,), (1,)), ((), ()))


def dot(a, b, dims=NN):
    return lax.dot_general(a, b, dims, preferred_element_type=F32)


def feature_tables():
    first = np.zeros((FEAT, PACKED), np.float32)
    second = np.zeros((FEAT, PACKED), np.float32)
    first_bias = np.zeros((PACKED,), np.float32)
    second_bias = np.zeros((PACKED,), np.float32)
    scale = np.zeros((PACKED,), np.float32)
    first_bias[0] = second_bias[0] = scale[0] = 1.0
    place = 1
    for i in range(FEAT):
        first[i, place] = 1.0
        second_bias[place] = 1.0
        scale[place] = 1.0 / 4.0
        place += 1
    for i in range(FEAT):
        for j in range(i, FEAT):
            first[i, place] = 1.0
            second[j, place] = 1.0
            scale[place] = 1.0 / 32.0 if i == j else 1.0 / 16.0
            place += 1
    return first, second, first_bias, second_bias, scale


def placed(table):
    out = np.zeros((HELD, LANES, PACKED), np.float32)
    for place in range(HELD):
        out[place, place * FEAT : (place + 1) * FEAT] = table
    return out


def stacked(table, per_group):
    every = placed(table).transpose(0, 2, 1)
    own = [[p for p in range(HELD) if (p // per_group) % 2 == core] for core in range(2)]
    return np.stack([every[places].reshape(-1, LANES) for places in own])


def project_kernel(at_ref, per_group, layers, gathered, *refs):
    mine, other = refs[:layers], refs[layers : 2 * layers]
    table_ref, bias_ref, wq_ref, wk_ref, own_ref = refs[2 * layers : 2 * layers + 5]
    rest = refs[2 * layers + 5 :]
    weights, rest = rest[:-10], rest[-10:]
    q_ref, k_ref, v_ref, early_ref, total_ref, row_ref, narrow_ref, w_ref, phi_ref, sems = rest
    core, layer, slab = at_ref[0], at_ref[1], at_ref[2]
    both, width = other[0].shape
    rows = both // 2
    model = row_ref.shape[1]
    part = weights[0].shape[-2]
    block = v_ref.shape[2] // layers
    narrow = wq_ref.shape[1]
    copies = []

    def fetch(slot, source, to):
        copies.append((slot, pltpu.make_async_copy(source, to, sems.at[len(copies)])))
        copies[-1][1].start()

    fetch(-1, wq_ref, narrow_ref.at[:, pl.ds(0, narrow)])
    fetch(-1, wk_ref, narrow_ref.at[:, pl.ds(narrow, narrow)])
    fetch(0, own_ref, w_ref.at[0, :, pl.ds(0, block)])
    for d in range(1, layers):
        for m in range(model // part):
            if gathered:
                source, start = weights[0].at[m, d - 1], m * part
            else:
                source, start = weights[m].at[d - 1], pl.multiple_of((slab ^ m) * part, part)
            fetch(d, source, w_ref.at[d // 2, pl.ds(start, part), pl.ds((d % 2) * block, block)])

    def arrived(slots):
        for slot, copy in copies:
            if slot in slots:
                copy.wait()

    for d in range(layers):
        z = lax.rem(layer + layers - d, layers)
        here = pl.multiple_of((2 * z + core) * width, width)
        there = pl.multiple_of((2 * z + 1 - core) * width, width)
        row_ref[:, pl.ds(here, width)] = mine[d][0] if d == 0 else mine[d][...]
        row_ref[:, pl.ds(there, width)] = other[d][...]
    arrived((-1,))
    half = table_ref.shape[1] // 2
    both_narrow = dot(row_ref[...], narrow_ref[...]).astype(BF16)
    for chunk in range(2):
        at = slice(chunk * rows, (chunk + 1) * rows)
        q_ref[chunk] = both_narrow[at, :narrow]
        k_ref[chunk] = both_narrow[at, narrow:]
        for lanes in range(0, narrow, LANES):
            product = dot(table_ref[0], both_narrow[at, narrow + lanes : narrow + lanes + LANES], NT)
            left = product[:half] + bias_ref[:, 0:1]
            right = product[half:] + bias_ref[:, 1:2]
            to = (lanes // LANES) * half
            phi_ref[chunk, to : to + half, :] = (left * right).astype(BF16)

    for pair in range(layers // 2):
        arrived((2 * pair, 2 * pair + 1))
        value = dot(row_ref[...], w_ref[pair]).astype(BF16)
        for d in (2 * pair, 2 * pair + 1):
            z = lax.rem(layer + d, layers)
            side = (d % 2) * block
            lanes = pl.multiple_of(z * block, block)
            for chunk in range(2):
                at = slice(chunk * rows, (chunk + 1) * rows)
                v_ref[chunk, :, pl.ds(lanes, block)] = value[at, side : side + block]
            for i in range(per_group):
                head = z * per_group + i
                place = pl.multiple_of(head * PACKED, PACKED)
                column = side + i * HEAD_DIM
                early = dot(phi_ref[0, pl.ds(place, PACKED), :], value[:rows, column : column + HEAD_DIM])
                late = dot(phi_ref[1, pl.ds(place, PACKED), :], value[rows:, column : column + HEAD_DIM])
                early_ref[head] = early.astype(BF16)
                total_ref[head] = (early + late).astype(BF16)


def local_kernel(at_ref, per_group, offset, q_ref, k_ref, v_ref, early_ref, table_ref, bias_ref, num_ref, phi_ref):
    rows = q_ref.shape[1]
    cut = LANES * -(-rows // (2 * LANES))
    wide = table_ref.shape[2] // 2
    lane = lax.broadcasted_iota(jnp.int32, (rows, LANES), 1) // FEAT
    for i in range(early_ref.shape[0]):
        head = (2 * (i // per_group + offset) + at_ref[0]) * per_group + i % per_group
        lanes = pl.multiple_of((head // HELD) * LANES, LANES)
        place = lax.rem(head, HELD)
        columns = slice(i * HEAD_DIM, (i + 1) * HEAD_DIM)
        for chunk in range(2):
            query = q_ref[chunk, :, pl.ds(lanes, LANES)]
            key = k_ref[chunk, :, pl.ds(lanes, LANES)]
            sides = dot(query, table_ref[place]) + bias_ref[...]
            phi = (sides[:, :PACKED] * sides[:, wide : wide + PACKED]).astype(BF16)
            phi_ref[chunk, i] = phi
            mine = jnp.where(lane == place, query * jnp.asarray(0.25, BF16), jnp.zeros_like(query))
            for low, high in ((0, cut), (cut, rows)):
                span = high - low
                s = dot(mine[low:high], key[low:high], NT)
                t_at = lax.broadcasted_iota(jnp.int32, (span, span), 0)
                j_at = lax.broadcasted_iota(jnp.int32, (span, span), 1)
                weight = jnp.where(t_at >= j_at, (0.5 * s + 1.0) * s + 1.0, 0.0).astype(BF16)
                num = dot(weight, v_ref[chunk, low:high, columns])
                if low > 0:
                    s = dot(mine[low:high], key[:low], NT)
                    weight = ((0.5 * s + 1.0) * s + 1.0).astype(BF16)
                    num = num + dot(weight, v_ref[chunk, :low, columns])
                if chunk > 0:
                    num = num + dot(phi[low:high], early_ref[i])
                num_ref[chunk, low:high, columns] = num


def prefix_kernel(at_ref, line_ref, *refs):
    layers = line_ref.shape[0]
    totals, outs, sum_ref = refs[: -layers - 1], refs[-layers - 1 : -1], refs[-1]
    layer, slab = at_ref[1], at_ref[2]
    run = jnp.zeros(line_ref.shape[1:], F32)
    for m, total in enumerate(totals, 1):
        run = run + total[...].astype(F32) * jnp.where((slab ^ m) < slab, 1.0, 0.0)
    for z in range(layers):
        sum_ref[z] = run.astype(BF16)
        run = run + line_ref[z].astype(F32)
    for d in range(layers):
        outs[d][...] = sum_ref[lax.rem(layer + layers - d, layers)]


def hidden_kernel(at_ref, layers, gain_ref, *refs):
    pieces, parts, out_ref, state_ref = refs[:layers], refs[layers:-2], refs[-2], refs[-1]
    numbers, features = parts[: len(parts) // 2], parts[len(parts) // 2 :]
    held = features[0].shape[1]
    group = pieces[0].shape[0]
    for d in range(layers):
        state_ref[lax.rem(at_ref[1] + d, layers)] = pieces[d][...]
    for i in range(held * len(features)):
        columns = slice(i * HEAD_DIM, (i + 1) * HEAD_DIM)
        at = (i % held) * HEAD_DIM
        num = numbers[i // held][0, :, at : at + HEAD_DIM]
        num = num + dot(features[i // held][0, i % held], state_ref[i // group, i % group])
        mean_square = jnp.mean(num * num, axis=1, keepdims=True)
        hidden = num * lax.rsqrt(mean_square + 1e-05) * gain_ref[:, columns]
        out_ref[:, columns] = hidden.astype(BF16)


def output_kernel(at_ref, mine_ref, other_ref, *refs):
    outs = refs[len(refs) * 2 // 3 :]
    weights = [w[...].reshape(mine_ref.shape[1], -1) for w in refs[: 2 * len(outs)]]
    width = weights[0].shape[1]
    part = dot(mine_ref[...], jnp.concatenate(weights[0::2], axis=1))
    part = part + dot(other_ref[...], jnp.concatenate(weights[1::2], axis=1))
    for i, out_ref in enumerate(outs):
        out_ref[...] = part[:, i * width : (i + 1) * width].astype(BF16)


def place_kernel(at_ref, *refs):
    pieces, out_ref, sems = refs[:-2], refs[-2], refs[-1]
    layers = len(pieces) // 2
    copies = []
    for i, piece in enumerate(pieces):
        rows = piece.shape[0]
        z = lax.rem(at_ref[1] + layers - i // 2, layers)
        to = out_ref.at[pl.ds(pl.multiple_of((2 * z + i % 2) * rows, rows), rows)]
        copies.append(pltpu.make_async_copy(piece, to, sems.at[i]))
    for copy in copies:
        copy.start()
    for copy in copies:
        copy.wait()


def whole(shape):
    return pl.BlockSpec(shape, lambda *_: (0,) * len(shape))


def params(mib):
    return pltpu.CompilerParams(vmem_limit_bytes=mib * MIB)


def call(kernel, scalar, grid, in_specs, out_specs, out_shape, args, flops, scratch=(), mib=60):
    return pl.pallas_call(
        kernel,
        grid_spec=pltpu.PrefetchScalarGridSpec(
            num_scalar_prefetch=1,
            grid=grid,
            in_specs=in_specs,
            out_specs=out_specs,
            scratch_shapes=list(scratch),
        ),
        out_shape=out_shape,
        compiler_params=params(mib),
        cost_estimate=pl.CostEstimate(flops=flops, bytes_accessed=12 * MIB, transcendentals=0),
    )(scalar, *args)


def per_device(tokens, w_query, w_key, w_value, w_out, gain):
    slabs = lax.axis_size("seq")
    layers = lax.axis_size("z")
    groups = 2 * layers
    my_slab = lax.axis_index("seq")
    core = lax.axis_index("core").astype(jnp.int32)
    layer = lax.axis_index("z").astype(jnp.int32)
    which = core.reshape(1)
    width = tokens.shape[1]
    rows = tokens.shape[0] // groups
    model, value_width = w_value.shape
    part = model // slabs
    per_group = HEADS // groups
    heads = HEADS // 2
    narrow = w_query.shape[1]
    swap = [(0, 1), (1, 0)]

    first, second, first_bias, second_bias, scale = feature_tables()
    sides = [stacked(first, per_group), stacked(second, per_group)]
    key_table = jnp.asarray(np.concatenate(sides, axis=1), BF16)
    repeat = HELD // 2
    key_bias = jnp.asarray(np.stack([np.tile(first_bias, repeat), np.tile(second_bias, repeat)], axis=1))
    wide = 2 * LANES
    query_table = np.zeros((HELD, LANES, 2 * wide), np.float32)
    query_bias = np.zeros((1, 2 * wide), np.float32)
    query_table[:, :, :PACKED] = placed(first * scale)
    query_table[:, :, wide : wide + PACKED] = placed(second)
    query_bias[0, :PACKED] = first_bias * scale
    query_bias[0, wide : wide + PACKED] = second_bias
    query_table, query_bias = jnp.asarray(query_table, BF16), jnp.asarray(query_bias)
    gain_mine = lax.dynamic_index_in_dim(gain.reshape(layers, 2, value_width), core, 1, False)
    gain_mine = gain_mine.reshape(1, layers * value_width)

    flip = lambda m: [(s, s ^ m) for s in range(slabs)]
    turn = lambda d: [(z, (z + d) % layers) for z in range(layers)]
    anywhere = pl.BlockSpec(memory_space=pl.ANY)
    vmem = pl.BlockSpec(memory_space=pltpu.VMEM)
    at = jnp.stack([core, layer, my_slab.astype(jnp.int32)])

    value_part = lax.dynamic_slice_in_dim(w_value, my_slab * part, part, 0)
    blocks = tokens.reshape(layers, 2 * rows, width)
    sent = [lax.dynamic_index_in_dim(blocks, lax.rem(layer + d, layers), 0, False) for d in range(layers)]
    stack = jnp.stack([lax.ppermute(value_part, "z", turn(-d)) for d in range(1, layers)])
    stack, sent = lax.optimization_barrier((stack, sent))
    if slabs == 4:
        weights = [stack] + [lax.ppermute(stack, "seq", flip(m)) for m in range(1, slabs)]
    else:
        weights = [lax.all_gather(stack, "seq", axis=0, tiled=False)]
    far = layers // 2
    mine = {d: lax.ppermute(sent[d], "z", turn(d)) for d in [far] + [d for d in range(1, layers) if d != far]}
    mine = [sent[0]] + [mine[d] for d in range(1, layers)]
    mine[far], weights[1:] = lax.optimization_barrier((mine[far], weights[1:]))
    other = [lax.ppermute(piece, "core", swap) for piece in mine]

    query, key, value, early, total = call(
        lambda at_ref, *refs: project_kernel(at_ref, per_group, layers, slabs != 4, *refs),
        at,
        (1,),
        [pl.BlockSpec((1, 2 * rows, width), lambda i, at: (at[1], 0, 0))]
        + [whole((2 * rows, width))] * (2 * layers - 1)
        + [
            pl.BlockSpec((1,) + key_table.shape[1:], lambda i, at: (at[0], 0, 0)),
            whole(key_bias.shape),
        ]
        + [anywhere] * (3 + len(weights)),
        [
            whole((2, rows, narrow)),
            whole((2, rows, narrow)),
            whole((2, rows, layers * value_width)),
            whole((heads, PACKED, HEAD_DIM)),
            whole((heads, PACKED, HEAD_DIM)),
        ],
        [
            jax.ShapeDtypeStruct((2, rows, narrow), BF16),
            jax.ShapeDtypeStruct((2, rows, narrow), BF16),
            jax.ShapeDtypeStruct((2, rows, layers * value_width), BF16),
            jax.ShapeDtypeStruct((heads, PACKED, HEAD_DIM), BF16),
            jax.ShapeDtypeStruct((heads, PACKED, HEAD_DIM), BF16),
        ],
        (blocks, *mine[1:], *other, key_table, key_bias, w_query, w_key, w_value, *weights),
        4 * rows * model * (model // 2 + 2 * narrow),
        [
            pltpu.VMEM((2 * rows, model), BF16),
            pltpu.VMEM((model, 2 * narrow), BF16),
            pltpu.VMEM((layers // 2, model, 2 * value_width), BF16),
            pltpu.VMEM((2, heads * PACKED, rows), BF16),
            pltpu.SemaphoreType.DMA((3 + (layers - 1) * slabs,)),
        ],
    )

    parts = 4
    some_layers = layers // parts

    def local(index):
        offset = index * some_layers
        return call(
            lambda core_ref, *refs: local_kernel(core_ref, per_group, offset, *refs),
            at,
            (1,),
            [
                whole((2, rows, narrow)),
                whole((2, rows, narrow)),
                pl.BlockSpec((2, rows, some_layers * value_width), lambda i, _: (0, 0, index)),
                pl.BlockSpec((heads // parts, PACKED, HEAD_DIM), lambda i, _: (index, 0, 0)),
                whole(query_table.shape),
                whole(query_bias.shape),
            ],
            [
                whole((2, rows, some_layers * value_width)),
                whole((2, heads // parts, rows, PACKED)),
            ],
            [
                jax.ShapeDtypeStruct((2, rows, some_layers * value_width), F32),
                jax.ShapeDtypeStruct((2, heads // parts, rows, PACKED), BF16),
            ],
            (query, key, value, early, query_table, query_bias),
            heads * rows * rows * 300,
        )

    own = total.reshape(layers, per_group, PACKED, HEAD_DIM)
    line = lax.all_to_all(own, "z", split_axis=0, concat_axis=0, tiled=True)
    locals_ = [local(0), local(1)]
    line, locals_ = lax.optimization_barrier((line, locals_))
    slab_total = jnp.sum(line.astype(F32), axis=0).astype(BF16)
    totals = [lax.ppermute(slab_total, "seq", flip(m)) for m in range(1, slabs)]
    third = local(2)
    totals, third = lax.optimization_barrier((totals, third))
    piece_shape = (per_group, PACKED, HEAD_DIM)
    prefix = pl.pallas_call(
        prefix_kernel,
        in_specs=[pl.BlockSpec(memory_space=pltpu.SMEM)] + [vmem] * slabs,
        out_specs=[vmem] * layers,
        out_shape=[jax.ShapeDtypeStruct(piece_shape, BF16)] * layers,
        scratch_shapes=[pltpu.VMEM((layers,) + piece_shape, BF16)],
    )(at, line, *totals)
    prefix = [prefix[0]] + [lax.ppermute(prefix[d], "z", turn(-d)) for d in range(1, layers)]
    locals_ = locals_ + [third, local(3)]

    def hidden(chunk):
        some = rows // 2
        numbers = pl.BlockSpec((1, some, heads * HEAD_DIM // parts), lambda i, _: (chunk, i, 0))
        features = pl.BlockSpec((1, heads // parts, some, PACKED), lambda i, _: (chunk, 0, i, 0))
        return call(
            lambda at_ref, *refs: hidden_kernel(at_ref, layers, *refs),
            at,
            (2,),
            [whole((1, heads * HEAD_DIM))]
            + [whole(piece_shape)] * layers
            + [numbers] * parts
            + [features] * parts,
            pl.BlockSpec((some, heads * HEAD_DIM), lambda i, _: (i, 0)),
            jax.ShapeDtypeStruct((rows, heads * HEAD_DIM), BF16),
            (gain_mine, *prefix, *(num for num, _ in locals_), *(phi for _, phi in locals_)),
            rows * heads * HEAD_DIM * 600,
            [pltpu.VMEM((layers,) + piece_shape, BF16)],
        )

    w_rows = w_out.reshape(layers, 2, value_width, model)

    def project_out(kept, received, to):
        block = (layers, 1, value_width, width)
        specs = []
        for d in to:
            columns = lambda at, d=d: 2 * lax.rem(at[1] + d, layers) + at[0]
            specs.append(pl.BlockSpec(block, lambda i, at, columns=columns: (0, at[0], 0, columns(at))))
            specs.append(pl.BlockSpec(block, lambda i, at, columns=columns: (0, 1 - at[0], 0, columns(at))))
        return call(
            output_kernel,
            at,
            (1,),
            [whole((rows, heads * HEAD_DIM))] * 2 + specs,
            [whole((rows, width))] * len(to),
            [jax.ShapeDtypeStruct((rows, width), BF16)] * len(to),
            (kept, received, *[w_rows] * len(specs)),
            2 * rows * model * width * len(to),
            mib=20,
        )

    kept = [hidden(chunk) for chunk in range(2)]
    received = [lax.ppermute(half, "core", swap) for half in kept]
    order = [far] + [d for d in range(1, layers) if d != far] + [0]
    pieces = {}
    for start in range(0, layers, 2):
        to = order[start : start + 2]
        for chunk in range(2):
            for d, piece in zip(to, project_out(kept[chunk], received[chunk], to)):
                pieces[d, chunk] = lax.ppermute(piece, "z", turn(d)) if d else piece
    return call(
        place_kernel,
        at,
        (1,),
        [vmem] * (2 * layers),
        anywhere,
        jax.ShapeDtypeStruct((groups * rows, width), BF16),
        tuple(pieces[d, chunk] for d in range(layers) for chunk in range(2)),
        0,
        [pltpu.SemaphoreType.DMA((2 * layers,))],
        mib=8,
    )


def solution(mesh):
    slabs, groups = mesh.shape["seq"], mesh.shape["chan"]
    split = jax.sharding.Mesh(mesh.devices.reshape(slabs, groups // 2, 2), ("seq", "z", "core"))
    chan = ("z", "core")
    return jax.shard_map(
        per_device,
        mesh=split,
        in_specs=(P("seq", chan), P(), P(), P(None, chan), P(), P()),
        out_specs=P("seq", chan),
        check_vma=False,
    )
```

```python
import jax
import jax.numpy as jnp
import numpy as np
from jax import lax
from jax.experimental import pallas as pl
from jax.experimental.pallas import tpu as pltpu
from jax.sharding import PartitionSpec as P

HEADS = 16
FEAT = 16
HEAD_DIM = 128
PACKED = 160
LANES = 128
HELD = LANES // FEAT
MIB = 1024 * 1024

F32 = jnp.float32
BF16 = jnp.bfloat16
NN = (((1,), (0,)), ((), ()))
NT = (((1,), (1,)), ((), ()))


def dot(a, b, dims=NN):
    return lax.dot_general(a, b, dims, preferred_element_type=F32)


def feature_tables():
    first = np.zeros((FEAT, PACKED), np.float32)
    second = np.zeros((FEAT, PACKED), np.float32)
    first_bias = np.zeros((PACKED,), np.float32)
    second_bias = np.zeros((PACKED,), np.float32)
    scale = np.zeros((PACKED,), np.float32)
    first_bias[0] = second_bias[0] = scale[0] = 1.0
    place = 1
    for i in range(FEAT):
        first[i, place] = 1.0
        second_bias[place] = 1.0
        scale[place] = 1.0 / 4.0
        place += 1
    for i in range(FEAT):
        for j in range(i, FEAT):
            first[i, place] = 1.0
            second[j, place] = 1.0
            scale[place] = 1.0 / 32.0 if i == j else 1.0 / 16.0
            place += 1
    return first, second, first_bias, second_bias, scale


def placed(table):
    out = np.zeros((HELD, LANES, PACKED), np.float32)
    for place in range(HELD):
        out[place, place * FEAT : (place + 1) * FEAT] = table
    return out


def stacked(table, per_group):
    every = placed(table).transpose(0, 2, 1)
    own = [[p for p in range(HELD) if (p // per_group) % 2 == core] for core in range(2)]
    return np.stack([every[places].reshape(-1, LANES) for places in own])


def project_kernel(at_ref, per_group, layers, gathered, *refs):
    mine, other = refs[:layers], refs[layers : 2 * layers]
    table_ref, bias_ref, wq_ref, wk_ref, own_ref = refs[2 * layers : 2 * layers + 5]
    rest = refs[2 * layers + 5 :]
    weights, rest = rest[:-10], rest[-10:]
    q_ref, k_ref, v_ref, early_ref, total_ref, row_ref, narrow_ref, w_ref, phi_ref, sems = rest
    core, layer, slab = at_ref[0], at_ref[1], at_ref[2]
    both, width = other[0].shape
    rows = both // 2
    model = row_ref.shape[1]
    part = weights[0].shape[-2]
    block = v_ref.shape[2] // layers
    narrow = wq_ref.shape[1]
    copies = []

    def fetch(slot, source, to):
        copies.append((slot, pltpu.make_async_copy(source, to, sems.at[len(copies)])))
        copies[-1][1].start()

    fetch(-1, wq_ref, narrow_ref.at[:, pl.ds(0, narrow)])
    fetch(-1, wk_ref, narrow_ref.at[:, pl.ds(narrow, narrow)])
    fetch(0, own_ref, w_ref.at[0, :, pl.ds(0, block)])
    for d in range(1, layers):
        for m in range(model // part):
            if gathered:
                source, start = weights[0].at[m, d - 1], m * part
            else:
                source, start = weights[m].at[d - 1], pl.multiple_of((slab ^ m) * part, part)
            fetch(d, source, w_ref.at[d // 2, pl.ds(start, part), pl.ds((d % 2) * block, block)])

    def arrived(slots):
        for slot, copy in copies:
            if slot in slots:
                copy.wait()

    for d in range(layers):
        z = lax.rem(layer + layers - d, layers)
        here = pl.multiple_of((2 * z + core) * width, width)
        there = pl.multiple_of((2 * z + 1 - core) * width, width)
        row_ref[:, pl.ds(here, width)] = mine[d][0] if d == 0 else mine[d][...]
        row_ref[:, pl.ds(there, width)] = other[d][...]
    arrived((-1,))
    half = table_ref.shape[1] // 2
    both_narrow = dot(row_ref[...], narrow_ref[...]).astype(BF16)
    for chunk in range(2):
        at = slice(chunk * rows, (chunk + 1) * rows)
        q_ref[chunk] = both_narrow[at, :narrow]
        k_ref[chunk] = both_narrow[at, narrow:]
        for lanes in range(0, narrow, LANES):
            product = dot(table_ref[0], both_narrow[at, narrow + lanes : narrow + lanes + LANES], NT)
            left = product[:half] + bias_ref[:, 0:1]
            right = product[half:] + bias_ref[:, 1:2]
            to = (lanes // LANES) * half
            phi_ref[chunk, to : to + half, :] = (left * right).astype(BF16)

    for pair in range(layers // 2):
        arrived((2 * pair, 2 * pair + 1))
        value = dot(row_ref[...], w_ref[pair]).astype(BF16)
        for d in (2 * pair, 2 * pair + 1):
            z = lax.rem(layer + d, layers)
            side = (d % 2) * block
            lanes = pl.multiple_of(z * block, block)
            for chunk in range(2):
                at = slice(chunk * rows, (chunk + 1) * rows)
                v_ref[chunk, :, pl.ds(lanes, block)] = value[at, side : side + block]
            for i in range(per_group):
                head = z * per_group + i
                place = pl.multiple_of(head * PACKED, PACKED)
                column = side + i * HEAD_DIM
                early = dot(phi_ref[0, pl.ds(place, PACKED), :], value[:rows, column : column + HEAD_DIM])
                late = dot(phi_ref[1, pl.ds(place, PACKED), :], value[rows:, column : column + HEAD_DIM])
                early_ref[head] = early.astype(BF16)
                total_ref[head] = (early + late).astype(BF16)


def local_kernel(at_ref, per_group, offset, q_ref, k_ref, v_ref, early_ref, table_ref, bias_ref, num_ref, phi_ref):
    rows = q_ref.shape[1]
    cut = LANES * -(-rows // (2 * LANES))
    wide = table_ref.shape[2] // 2
    lane = lax.broadcasted_iota(jnp.int32, (rows, LANES), 1) // FEAT
    for i in range(early_ref.shape[0]):
        head = (2 * (i // per_group + offset) + at_ref[0]) * per_group + i % per_group
        lanes = pl.multiple_of((head // HELD) * LANES, LANES)
        place = lax.rem(head, HELD)
        columns = slice(i * HEAD_DIM, (i + 1) * HEAD_DIM)
        for chunk in range(2):
            query = q_ref[chunk, :, pl.ds(lanes, LANES)]
            key = k_ref[chunk, :, pl.ds(lanes, LANES)]
            sides = dot(query, table_ref[place]) + bias_ref[...]
            phi = (sides[:, :PACKED] * sides[:, wide : wide + PACKED]).astype(BF16)
            phi_ref[chunk, i] = phi
            mine = jnp.where(lane == place, query * jnp.asarray(0.25, BF16), jnp.zeros_like(query))
            for low, high in ((0, cut), (cut, rows)):
                span = high - low
                s = dot(mine[low:high], key[low:high], NT)
                t_at = lax.broadcasted_iota(jnp.int32, (span, span), 0)
                j_at = lax.broadcasted_iota(jnp.int32, (span, span), 1)
                weight = jnp.where(t_at >= j_at, (0.5 * s + 1.0) * s + 1.0, 0.0).astype(BF16)
                num = dot(weight, v_ref[chunk, low:high, columns])
                if low > 0:
                    s = dot(mine[low:high], key[:low], NT)
                    weight = ((0.5 * s + 1.0) * s + 1.0).astype(BF16)
                    num = num + dot(weight, v_ref[chunk, :low, columns])
                if chunk > 0:
                    num = num + dot(phi[low:high], early_ref[i])
                num_ref[chunk, low:high, columns] = num


def prefix_kernel(at_ref, line_ref, *refs):
    layers = line_ref.shape[0]
    totals, outs, sum_ref = refs[: -layers - 1], refs[-layers - 1 : -1], refs[-1]
    layer, slab = at_ref[1], at_ref[2]
    run = jnp.zeros(line_ref.shape[1:], F32)
    for m, total in enumerate(totals, 1):
        run = run + total[...].astype(F32) * jnp.where((slab ^ m) < slab, 1.0, 0.0)
    for z in range(layers):
        sum_ref[z] = run.astype(BF16)
        run = run + line_ref[z].astype(F32)
    for d in range(layers):
        outs[d][...] = sum_ref[lax.rem(layer + layers - d, layers)]


def hidden_kernel(at_ref, layers, gain_ref, *refs):
    pieces, parts, out_ref, state_ref = refs[:layers], refs[layers:-2], refs[-2], refs[-1]
    numbers, features = parts[: len(parts) // 2], parts[len(parts) // 2 :]
    held = features[0].shape[1]
    group = pieces[0].shape[0]
    for d in range(layers):
        state_ref[lax.rem(at_ref[1] + d, layers)] = pieces[d][...]
    for i in range(held * len(features)):
        columns = slice(i * HEAD_DIM, (i + 1) * HEAD_DIM)
        at = (i % held) * HEAD_DIM
        num = numbers[i // held][0, :, at : at + HEAD_DIM]
        num = num + dot(features[i // held][0, i % held], state_ref[i // group, i % group])
        mean_square = jnp.mean(num * num, axis=1, keepdims=True)
        hidden = num * lax.rsqrt(mean_square + 1e-05) * gain_ref[:, columns]
        out_ref[:, columns] = hidden.astype(BF16)


def output_kernel(at_ref, mine_ref, other_ref, *refs):
    outs = refs[len(refs) * 2 // 3 :]
    weights = [w[...].reshape(mine_ref.shape[1], -1) for w in refs[: 2 * len(outs)]]
    width = weights[0].shape[1]
    part = dot(mine_ref[...], jnp.concatenate(weights[0::2], axis=1))
    part = part + dot(other_ref[...], jnp.concatenate(weights[1::2], axis=1))
    for i, out_ref in enumerate(outs):
        out_ref[...] = part[:, i * width : (i + 1) * width].astype(BF16)


def place_kernel(at_ref, *refs):
    pieces, out_ref, sems = refs[:-2], refs[-2], refs[-1]
    layers = len(pieces) // 2
    copies = []
    for i, piece in enumerate(pieces):
        rows = piece.shape[0]
        z = lax.rem(at_ref[1] + layers - i // 2, layers)
        to = out_ref.at[pl.ds(pl.multiple_of((2 * z + i % 2) * rows, rows), rows)]
        copies.append(pltpu.make_async_copy(piece, to, sems.at[i]))
    for copy in copies:
        copy.start()
    for copy in copies:
        copy.wait()


def whole(shape):
    return pl.BlockSpec(shape, lambda *_: (0,) * len(shape))


def params(mib):
    return pltpu.CompilerParams(vmem_limit_bytes=mib * MIB)


def call(kernel, scalar, grid, in_specs, out_specs, out_shape, args, flops, scratch=(), *, mib):
    return pl.pallas_call(
        kernel,
        grid_spec=pltpu.PrefetchScalarGridSpec(
            num_scalar_prefetch=1,
            grid=grid,
            in_specs=in_specs,
            out_specs=out_specs,
            scratch_shapes=list(scratch),
        ),
        out_shape=out_shape,
        compiler_params=params(mib),
        cost_estimate=pl.CostEstimate(flops=flops, bytes_accessed=12 * MIB, transcendentals=0),
    )(scalar, *args)


def per_device(tokens, w_query, w_key, w_value, w_out, gain):
    slabs = lax.axis_size("seq")
    layers = lax.axis_size("z")
    groups = 2 * layers
    my_slab = lax.axis_index("seq")
    core = lax.axis_index("core").astype(jnp.int32)
    layer = lax.axis_index("z").astype(jnp.int32)
    which = core.reshape(1)
    width = tokens.shape[1]
    rows = tokens.shape[0] // groups
    model, value_width = w_value.shape
    part = model // slabs
    per_group = HEADS // groups
    heads = HEADS // 2
    narrow = w_query.shape[1]
    swap = [(0, 1), (1, 0)]

    first, second, first_bias, second_bias, scale = feature_tables()
    sides = [stacked(first, per_group), stacked(second, per_group)]
    key_table = jnp.asarray(np.concatenate(sides, axis=1), BF16)
    repeat = HELD // 2
    key_bias = jnp.asarray(np.stack([np.tile(first_bias, repeat), np.tile(second_bias, repeat)], axis=1))
    wide = 2 * LANES
    query_table = np.zeros((HELD, LANES, 2 * wide), np.float32)
    query_bias = np.zeros((1, 2 * wide), np.float32)
    query_table[:, :, :PACKED] = placed(first * scale)
    query_table[:, :, wide : wide + PACKED] = placed(second)
    query_bias[0, :PACKED] = first_bias * scale
    query_bias[0, wide : wide + PACKED] = second_bias
    query_table, query_bias = jnp.asarray(query_table, BF16), jnp.asarray(query_bias)
    gain_mine = lax.dynamic_index_in_dim(gain.reshape(layers, 2, value_width), core, 1, False)
    gain_mine = gain_mine.reshape(1, layers * value_width)

    flip = lambda m: [(s, s ^ m) for s in range(slabs)]
    turn = lambda d: [(z, (z + d) % layers) for z in range(layers)]
    anywhere = pl.BlockSpec(memory_space=pl.ANY)
    vmem = pl.BlockSpec(memory_space=pltpu.VMEM)
    at = jnp.stack([core, layer, my_slab.astype(jnp.int32)])

    value_part = lax.dynamic_slice_in_dim(w_value, my_slab * part, part, 0)
    blocks = tokens.reshape(layers, 2 * rows, width)
    sent = [lax.dynamic_index_in_dim(blocks, lax.rem(layer + d, layers), 0, False) for d in range(layers)]
    stack = jnp.stack([lax.ppermute(value_part, "z", turn(-d)) for d in range(1, layers)])
    stack, sent = lax.optimization_barrier((stack, sent))
    if slabs == 4:
        weights = [stack] + [lax.ppermute(stack, "seq", flip(m)) for m in range(1, slabs)]
    else:
        weights = [lax.all_gather(stack, "seq", axis=0, tiled=False)]
    far = layers // 2
    mine = {d: lax.ppermute(sent[d], "z", turn(d)) for d in [far] + [d for d in range(1, layers) if d != far]}
    mine = [sent[0]] + [mine[d] for d in range(1, layers)]
    mine[far], weights[1:] = lax.optimization_barrier((mine[far], weights[1:]))
    other = [lax.ppermute(piece, "core", swap) for piece in mine]

    query, key, value, early, total = call(
        lambda at_ref, *refs: project_kernel(at_ref, per_group, layers, slabs != 4, *refs),
        at,
        (1,),
        [pl.BlockSpec((1, 2 * rows, width), lambda i, at: (at[1], 0, 0))]
        + [whole((2 * rows, width))] * (2 * layers - 1)
        + [
            pl.BlockSpec((1,) + key_table.shape[1:], lambda i, at: (at[0], 0, 0)),
            whole(key_bias.shape),
        ]
        + [anywhere] * (3 + len(weights)),
        [
            whole((2, rows, narrow)),
            whole((2, rows, narrow)),
            whole((2, rows, layers * value_width)),
            whole((heads, PACKED, HEAD_DIM)),
            whole((heads, PACKED, HEAD_DIM)),
        ],
        [
            jax.ShapeDtypeStruct((2, rows, narrow), BF16),
            jax.ShapeDtypeStruct((2, rows, narrow), BF16),
            jax.ShapeDtypeStruct((2, rows, layers * value_width), BF16),
            jax.ShapeDtypeStruct((heads, PACKED, HEAD_DIM), BF16),
            jax.ShapeDtypeStruct((heads, PACKED, HEAD_DIM), BF16),
        ],
        (blocks, *mine[1:], *other, key_table, key_bias, w_query, w_key, w_value, *weights),
        4 * rows * model * (model // 2 + 2 * narrow),
        [
            pltpu.VMEM((2 * rows, model), BF16),
            pltpu.VMEM((model, 2 * narrow), BF16),
            pltpu.VMEM((layers // 2, model, 2 * value_width), BF16),
            pltpu.VMEM((2, heads * PACKED, rows), BF16),
            pltpu.SemaphoreType.DMA((3 + (layers - 1) * slabs,)),
        ],
        mib=36,
    )

    parts = 4
    some_layers = layers // parts

    def local(index):
        offset = index * some_layers
        return call(
            lambda core_ref, *refs: local_kernel(core_ref, per_group, offset, *refs),
            at,
            (1,),
            [
                whole((2, rows, narrow)),
                whole((2, rows, narrow)),
                pl.BlockSpec((2, rows, some_layers * value_width), lambda i, _: (0, 0, index)),
                pl.BlockSpec((heads // parts, PACKED, HEAD_DIM), lambda i, _: (index, 0, 0)),
                whole(query_table.shape),
                whole(query_bias.shape),
            ],
            [
                whole((2, rows, some_layers * value_width)),
                whole((2, heads // parts, rows, PACKED)),
            ],
            [
                jax.ShapeDtypeStruct((2, rows, some_layers * value_width), F32),
                jax.ShapeDtypeStruct((2, heads // parts, rows, PACKED), BF16),
            ],
            (query, key, value, early, query_table, query_bias),
            heads * rows * rows * 300,
            mib=20,
        )

    own = total.reshape(layers, per_group, PACKED, HEAD_DIM)
    line = lax.all_to_all(own, "z", split_axis=0, concat_axis=0, tiled=True)
    locals_ = [local(0), local(1)]
    line, locals_ = lax.optimization_barrier((line, locals_))
    slab_total = jnp.sum(line.astype(F32), axis=0).astype(BF16)
    totals = [lax.ppermute(slab_total, "seq", flip(m)) for m in range(1, slabs)]
    third = local(2)
    totals, third = lax.optimization_barrier((totals, third))
    piece_shape = (per_group, PACKED, HEAD_DIM)
    prefix = pl.pallas_call(
        prefix_kernel,
        in_specs=[pl.BlockSpec(memory_space=pltpu.SMEM)] + [vmem] * slabs,
        out_specs=[vmem] * layers,
        out_shape=[jax.ShapeDtypeStruct(piece_shape, BF16)] * layers,
        scratch_shapes=[pltpu.VMEM((layers,) + piece_shape, BF16)],
    )(at, line, *totals)
    prefix = [prefix[0]] + [lax.ppermute(prefix[d], "z", turn(-d)) for d in range(1, layers)]
    locals_ = locals_ + [third, local(3)]

    def hidden(chunk):
        some = rows // 2
        numbers = pl.BlockSpec((1, some, heads * HEAD_DIM // parts), lambda i, _: (chunk, i, 0))
        features = pl.BlockSpec((1, heads // parts, some, PACKED), lambda i, _: (chunk, 0, i, 0))
        return call(
            lambda at_ref, *refs: hidden_kernel(at_ref, layers, *refs),
            at,
            (2,),
            [whole((1, heads * HEAD_DIM))]
            + [whole(piece_shape)] * layers
            + [numbers] * parts
            + [features] * parts,
            pl.BlockSpec((some, heads * HEAD_DIM), lambda i, _: (i, 0)),
            jax.ShapeDtypeStruct((rows, heads * HEAD_DIM), BF16),
            (gain_mine, *prefix, *(num for num, _ in locals_), *(phi for _, phi in locals_)),
            rows * heads * HEAD_DIM * 600,
            [pltpu.VMEM((layers,) + piece_shape, BF16)],
            mib=16,
        )

    w_rows = w_out.reshape(layers, 2, value_width, model)

    def project_out(kept, received, to):
        block = (layers, 1, value_width, width)
        specs = []
        for d in to:
            columns = lambda at, d=d: 2 * lax.rem(at[1] + d, layers) + at[0]
            specs.append(pl.BlockSpec(block, lambda i, at, columns=columns: (0, at[0], 0, columns(at))))
            specs.append(pl.BlockSpec(block, lambda i, at, columns=columns: (0, 1 - at[0], 0, columns(at))))
        return call(
            output_kernel,
            at,
            (1,),
            [whole((rows, heads * HEAD_DIM))] * 2 + specs,
            [whole((rows, width))] * len(to),
            [jax.ShapeDtypeStruct((rows, width), BF16)] * len(to),
            (kept, received, *[w_rows] * len(specs)),
            2 * rows * model * width * len(to),
            mib=20,
        )

    kept = [hidden(chunk) for chunk in range(2)]
    received = [lax.ppermute(half, "core", swap) for half in kept]
    order = [far] + [d for d in range(1, layers) if d != far] + [0]
    pieces = {}
    for start in range(0, layers, 2):
        to = order[start : start + 2]
        for chunk in range(2):
            for d, piece in zip(to, project_out(kept[chunk], received[chunk], to)):
                pieces[d, chunk] = lax.ppermute(piece, "z", turn(d)) if d else piece
    return call(
        place_kernel,
        at,
        (1,),
        [vmem] * (2 * layers),
        anywhere,
        jax.ShapeDtypeStruct((groups * rows, width), BF16),
        tuple(pieces[d, chunk] for d in range(layers) for chunk in range(2)),
        0,
        [pltpu.SemaphoreType.DMA((2 * layers,))],
        mib=8,
    )


def solution(mesh):
    slabs, groups = mesh.shape["seq"], mesh.shape["chan"]
    split = jax.sharding.Mesh(mesh.devices.reshape(slabs, groups // 2, 2), ("seq", "z", "core"))
    chan = ("z", "core")
    return jax.shard_map(
        per_device,
        mesh=split,
        in_specs=(P("seq", chan), P(), P(), P(None, chan), P(), P()),
        out_specs=P("seq", chan),
        check_vma=False,
    )
```

```python
import jax
import jax.numpy as jnp
import numpy as np
from jax import lax
from jax.experimental import pallas as pl
from jax.experimental.pallas import tpu as pltpu
from jax.sharding import PartitionSpec as P

HEADS = 16
FEAT = 16
HEAD_DIM = 128
PACKED = 160
LANES = 128
HELD = LANES // FEAT
MIB = 1024 * 1024

F32 = jnp.float32
BF16 = jnp.bfloat16
NN = (((1,), (0,)), ((), ()))
NT = (((1,), (1,)), ((), ()))


def dot(a, b, dims=NN):
    return lax.dot_general(a, b, dims, preferred_element_type=F32)


def feature_tables():
    first = np.zeros((FEAT, PACKED), np.float32)
    second = np.zeros((FEAT, PACKED), np.float32)
    first_bias = np.zeros((PACKED,), np.float32)
    second_bias = np.zeros((PACKED,), np.float32)
    scale = np.zeros((PACKED,), np.float32)
    first_bias[0] = second_bias[0] = scale[0] = 1.0
    place = 1
    for i in range(FEAT):
        first[i, place] = 1.0
        second_bias[place] = 1.0
        scale[place] = 1.0 / 4.0
        place += 1
    for i in range(FEAT):
        for j in range(i, FEAT):
            first[i, place] = 1.0
            second[j, place] = 1.0
            scale[place] = 1.0 / 32.0 if i == j else 1.0 / 16.0
            place += 1
    return first, second, first_bias, second_bias, scale


def placed(table):
    out = np.zeros((HELD, LANES, PACKED), np.float32)
    for place in range(HELD):
        out[place, place * FEAT : (place + 1) * FEAT] = table
    return out


def stacked(table, per_group):
    every = placed(table).transpose(0, 2, 1)
    own = [[p for p in range(HELD) if (p // per_group) % 2 == core] for core in range(2)]
    return np.stack([every[places].reshape(-1, LANES) for places in own])


def project_kernel(at_ref, per_group, layers, gathered, *refs):
    mine, other = refs[:layers], refs[layers : 2 * layers]
    table_ref, bias_ref, wq_ref, wk_ref, own_ref = refs[2 * layers : 2 * layers + 5]
    rest = refs[2 * layers + 5 :]
    weights, rest = rest[:-10], rest[-10:]
    q_ref, k_ref, v_ref, early_ref, total_ref, row_ref, narrow_ref, w_ref, phi_ref, sems = rest
    core, layer, slab = at_ref[0], at_ref[1], at_ref[2]
    both, width = other[0].shape
    rows = both // 2
    model = row_ref.shape[1]
    part = weights[0].shape[-2]
    block = v_ref.shape[2] // layers
    narrow = wq_ref.shape[1]
    copies = []

    def fetch(slot, source, to):
        copies.append((slot, pltpu.make_async_copy(source, to, sems.at[len(copies)])))
        copies[-1][1].start()

    fetch(-1, wq_ref, narrow_ref.at[:, pl.ds(0, narrow)])
    fetch(-1, wk_ref, narrow_ref.at[:, pl.ds(narrow, narrow)])
    fetch(0, own_ref, w_ref.at[0, :, pl.ds(0, block)])
    for d in range(1, layers):
        for m in range(model // part):
            if gathered:
                source, start = weights[0].at[m, d - 1], m * part
            else:
                source, start = weights[m].at[d - 1], pl.multiple_of((slab ^ m) * part, part)
            fetch(d, source, w_ref.at[d // 2, pl.ds(start, part), pl.ds((d % 2) * block, block)])

    def arrived(slots):
        for slot, copy in copies:
            if slot in slots:
                copy.wait()

    for d in range(layers):
        z = lax.rem(layer + layers - d, layers)
        here = pl.multiple_of((2 * z + core) * width, width)
        there = pl.multiple_of((2 * z + 1 - core) * width, width)
        row_ref[:, pl.ds(here, width)] = mine[d][0] if d == 0 else mine[d][...]
        row_ref[:, pl.ds(there, width)] = other[d][...]
    arrived((-1,))
    half = table_ref.shape[1] // 2
    both_narrow = dot(row_ref[...], narrow_ref[...]).astype(BF16)
    for chunk in range(2):
        at = slice(chunk * rows, (chunk + 1) * rows)
        q_ref[chunk] = both_narrow[at, :narrow]
        k_ref[chunk] = both_narrow[at, narrow:]
        for lanes in range(0, narrow, LANES):
            product = dot(table_ref[0], both_narrow[at, narrow + lanes : narrow + lanes + LANES], NT)
            left = product[:half] + bias_ref[:, 0:1]
            right = product[half:] + bias_ref[:, 1:2]
            to = (lanes // LANES) * half
            phi_ref[chunk, to : to + half, :] = (left * right).astype(BF16)

    for pair in range(layers // 2):
        arrived((2 * pair, 2 * pair + 1))
        value = dot(row_ref[...], w_ref[pair]).astype(BF16)
        for d in (2 * pair, 2 * pair + 1):
            z = lax.rem(layer + d, layers)
            side = (d % 2) * block
            lanes = pl.multiple_of(z * block, block)
            for chunk in range(2):
                at = slice(chunk * rows, (chunk + 1) * rows)
                v_ref[chunk, :, pl.ds(lanes, block)] = value[at, side : side + block]
            for i in range(per_group):
                head = z * per_group + i
                place = pl.multiple_of(head * PACKED, PACKED)
                column = side + i * HEAD_DIM
                early = dot(phi_ref[0, pl.ds(place, PACKED), :], value[:rows, column : column + HEAD_DIM])
                late = dot(phi_ref[1, pl.ds(place, PACKED), :], value[rows:, column : column + HEAD_DIM])
                early_ref[head] = early.astype(BF16)
                total_ref[head] = (early + late).astype(BF16)


def local_kernel(at_ref, per_group, offset, q_ref, k_ref, v_ref, early_ref, table_ref, bias_ref, num_ref, phi_ref):
    rows = q_ref.shape[1]
    cut = LANES * -(-rows // (2 * LANES))
    wide = table_ref.shape[2] // 2
    local_head = pl.program_id(0) + offset
    head = (2 * (local_head // per_group) + at_ref[0]) * per_group + lax.rem(local_head, per_group)
    lanes = pl.multiple_of((head // HELD) * LANES, LANES)
    place = lax.rem(head, HELD)
    lane = lax.broadcasted_iota(jnp.int32, (rows, LANES), 1) // FEAT
    for chunk in range(2):
        query = q_ref[chunk, :, pl.ds(lanes, LANES)]
        key = k_ref[chunk, :, pl.ds(lanes, LANES)]
        sides = dot(query, table_ref[place]) + bias_ref[...]
        phi = (sides[:, :PACKED] * sides[:, wide : wide + PACKED]).astype(BF16)
        phi_ref[chunk, 0] = phi
        mine = jnp.where(lane == place, query * jnp.asarray(0.25, BF16), jnp.zeros_like(query))
        for low, high in ((0, cut), (cut, rows)):
            span = high - low
            s = dot(mine[low:high], key[low:high], NT)
            t_at = lax.broadcasted_iota(jnp.int32, (span, span), 0)
            j_at = lax.broadcasted_iota(jnp.int32, (span, span), 1)
            weight = jnp.where(t_at >= j_at, (0.5 * s + 1.0) * s + 1.0, 0.0).astype(BF16)
            num = dot(weight, v_ref[chunk, low:high, :])
            if low > 0:
                s = dot(mine[low:high], key[:low], NT)
                weight = ((0.5 * s + 1.0) * s + 1.0).astype(BF16)
                num = num + dot(weight, v_ref[chunk, :low, :])
            if chunk > 0:
                num = num + dot(phi[low:high], early_ref[0])
            num_ref[chunk, low:high, :] = num


def prefix_kernel(at_ref, line_ref, *refs):
    layers = line_ref.shape[0]
    totals, outs, sum_ref = refs[: -layers - 1], refs[-layers - 1 : -1], refs[-1]
    layer, slab = at_ref[1], at_ref[2]
    run = jnp.zeros(line_ref.shape[1:], F32)
    for m, total in enumerate(totals, 1):
        run = run + total[...].astype(F32) * jnp.where((slab ^ m) < slab, 1.0, 0.0)
    for z in range(layers):
        sum_ref[z] = run.astype(BF16)
        run = run + line_ref[z].astype(F32)
    for d in range(layers):
        outs[d][...] = sum_ref[lax.rem(layer + layers - d, layers)]


def hidden_kernel(at_ref, layers, gain_ref, *refs):
    pieces, parts, out_ref, state_ref = refs[:layers], refs[layers:-2], refs[-2], refs[-1]
    group = pieces[0].shape[0]
    for d in range(layers):
        state_ref[lax.rem(at_ref[1] + d, layers)] = pieces[d][...]
    head = 0
    for num_ref, phi_ref in zip(parts[0::2], parts[1::2]):
        for i in range(phi_ref.shape[1]):
            columns = slice(head * HEAD_DIM, (head + 1) * HEAD_DIM)
            num = num_ref[0, :, i * HEAD_DIM : (i + 1) * HEAD_DIM]
            num = num + dot(phi_ref[0, i], state_ref[head // group, head % group])
            mean_square = jnp.mean(num * num, axis=1, keepdims=True)
            hidden = num * lax.rsqrt(mean_square + 1e-05) * gain_ref[:, columns]
            out_ref[:, columns] = hidden.astype(BF16)
            head += 1


def output_kernel(at_ref, mine_ref, other_ref, *refs):
    outs = refs[len(refs) * 2 // 3 :]
    weights = [w[...].reshape(mine_ref.shape[1], -1) for w in refs[: 2 * len(outs)]]
    width = weights[0].shape[1]
    part = dot(mine_ref[...], jnp.concatenate(weights[0::2], axis=1))
    part = part + dot(other_ref[...], jnp.concatenate(weights[1::2], axis=1))
    for i, out_ref in enumerate(outs):
        out_ref[...] = part[:, i * width : (i + 1) * width].astype(BF16)


def place_kernel(at_ref, *refs):
    pieces, out_ref, sems = refs[:-2], refs[-2], refs[-1]
    layers = len(pieces) // 2
    copies = []
    for i, piece in enumerate(pieces):
        rows = piece.shape[0]
        z = lax.rem(at_ref[1] + layers - i // 2, layers)
        to = out_ref.at[pl.ds(pl.multiple_of((2 * z + i % 2) * rows, rows), rows)]
        copies.append(pltpu.make_async_copy(piece, to, sems.at[i]))
    for copy in copies:
        copy.start()
    for copy in copies:
        copy.wait()


def whole(shape):
    return pl.BlockSpec(shape, lambda *_: (0,) * len(shape))


def params(mib):
    return pltpu.CompilerParams(vmem_limit_bytes=mib * MIB)


def call(kernel, scalar, grid, in_specs, out_specs, out_shape, args, flops, scratch=(), mib=60):
    return pl.pallas_call(
        kernel,
        grid_spec=pltpu.PrefetchScalarGridSpec(
            num_scalar_prefetch=1,
            grid=grid,
            in_specs=in_specs,
            out_specs=out_specs,
            scratch_shapes=list(scratch),
        ),
        out_shape=out_shape,
        compiler_params=params(mib),
        cost_estimate=pl.CostEstimate(flops=flops, bytes_accessed=12 * MIB, transcendentals=0),
    )(scalar, *args)


def per_device(tokens, w_query, w_key, w_value, w_out, gain):
    slabs = lax.axis_size("seq")
    layers = lax.axis_size("z")
    groups = 2 * layers
    my_slab = lax.axis_index("seq")
    core = lax.axis_index("core").astype(jnp.int32)
    layer = lax.axis_index("z").astype(jnp.int32)
    which = core.reshape(1)
    width = tokens.shape[1]
    rows = tokens.shape[0] // groups
    model, value_width = w_value.shape
    part = model // slabs
    per_group = HEADS // groups
    heads = HEADS // 2
    narrow = w_query.shape[1]
    swap = [(0, 1), (1, 0)]

    first, second, first_bias, second_bias, scale = feature_tables()
    sides = [stacked(first, per_group), stacked(second, per_group)]
    key_table = jnp.asarray(np.concatenate(sides, axis=1), BF16)
    repeat = HELD // 2
    key_bias = jnp.asarray(np.stack([np.tile(first_bias, repeat), np.tile(second_bias, repeat)], axis=1))
    wide = 2 * LANES
    query_table = np.zeros((HELD, LANES, 2 * wide), np.float32)
    query_bias = np.zeros((1, 2 * wide), np.float32)
    query_table[:, :, :PACKED] = placed(first * scale)
    query_table[:, :, wide : wide + PACKED] = placed(second)
    query_bias[0, :PACKED] = first_bias * scale
    query_bias[0, wide : wide + PACKED] = second_bias
    query_table, query_bias = jnp.asarray(query_table, BF16), jnp.asarray(query_bias)
    gain_mine = lax.dynamic_index_in_dim(gain.reshape(layers, 2, value_width), core, 1, False)
    gain_mine = gain_mine.reshape(1, layers * value_width)

    flip = lambda m: [(s, s ^ m) for s in range(slabs)]
    turn = lambda d: [(z, (z + d) % layers) for z in range(layers)]
    anywhere = pl.BlockSpec(memory_space=pl.ANY)
    vmem = pl.BlockSpec(memory_space=pltpu.VMEM)
    at = jnp.stack([core, layer, my_slab.astype(jnp.int32)])

    value_part = lax.dynamic_slice_in_dim(w_value, my_slab * part, part, 0)
    blocks = tokens.reshape(layers, 2 * rows, width)
    sent = [lax.dynamic_index_in_dim(blocks, lax.rem(layer + d, layers), 0, False) for d in range(layers)]
    stack = jnp.stack([lax.ppermute(value_part, "z", turn(-d)) for d in range(1, layers)])
    stack, sent = lax.optimization_barrier((stack, sent))
    if slabs == 4:
        weights = [stack] + [lax.ppermute(stack, "seq", flip(m)) for m in range(1, slabs)]
    else:
        weights = [lax.all_gather(stack, "seq", axis=0, tiled=False)]
    far = layers // 2
    mine = {d: lax.ppermute(sent[d], "z", turn(d)) for d in [far] + [d for d in range(1, layers) if d != far]}
    mine = [sent[0]] + [mine[d] for d in range(1, layers)]
    mine[1:], weights[1:] = lax.optimization_barrier((mine[1:], weights[1:]))
    other = [lax.ppermute(piece, "core", swap) for piece in mine]

    query, key, value, early, total = call(
        lambda at_ref, *refs: project_kernel(at_ref, per_group, layers, slabs != 4, *refs),
        at,
        (1,),
        [pl.BlockSpec((1, 2 * rows, width), lambda i, at: (at[1], 0, 0))]
        + [whole((2 * rows, width))] * (2 * layers - 1)
        + [
            pl.BlockSpec((1,) + key_table.shape[1:], lambda i, at: (at[0], 0, 0)),
            whole(key_bias.shape),
        ]
        + [anywhere] * (3 + len(weights)),
        [
            whole((2, rows, narrow)),
            whole((2, rows, narrow)),
            whole((2, rows, layers * value_width)),
            whole((heads, PACKED, HEAD_DIM)),
            whole((heads, PACKED, HEAD_DIM)),
        ],
        [
            jax.ShapeDtypeStruct((2, rows, narrow), BF16),
            jax.ShapeDtypeStruct((2, rows, narrow), BF16),
            jax.ShapeDtypeStruct((2, rows, layers * value_width), BF16),
            jax.ShapeDtypeStruct((heads, PACKED, HEAD_DIM), BF16),
            jax.ShapeDtypeStruct((heads, PACKED, HEAD_DIM), BF16),
        ],
        (blocks, *mine[1:], *other, key_table, key_bias, w_query, w_key, w_value, *weights),
        4 * rows * model * (model // 2 + 2 * narrow),
        [
            pltpu.VMEM((2 * rows, model), BF16),
            pltpu.VMEM((model, 2 * narrow), BF16),
            pltpu.VMEM((layers // 2, model, 2 * value_width), BF16),
            pltpu.VMEM((2, heads * PACKED, rows), BF16),
            pltpu.SemaphoreType.DMA((3 + (layers - 1) * slabs,)),
        ],
    )

    def local(offset, count):
        return call(
            lambda core_ref, *refs: local_kernel(core_ref, per_group, offset, *refs),
            at,
            (count,),
            [
                whole((2, rows, narrow)),
                whole((2, rows, narrow)),
                pl.BlockSpec((2, rows, HEAD_DIM), lambda i, _: (0, 0, i + offset)),
                pl.BlockSpec((1, PACKED, HEAD_DIM), lambda i, _: (i + offset, 0, 0)),
                whole(query_table.shape),
                whole(query_bias.shape),
            ],
            [
                pl.BlockSpec((2, rows, HEAD_DIM), lambda i, _: (0, 0, i)),
                pl.BlockSpec((2, 1, rows, PACKED), lambda i, _: (0, i, 0, 0)),
            ],
            [
                jax.ShapeDtypeStruct((2, rows, count * HEAD_DIM), F32),
                jax.ShapeDtypeStruct((2, count, rows, PACKED), BF16),
            ],
            (query, key, value, early, query_table, query_bias),
            count * rows * rows * 1200,
        )

    own = total.reshape(layers, per_group, PACKED, HEAD_DIM)
    line = lax.all_to_all(own, "z", split_axis=0, concat_axis=0, tiled=True)
    locals_ = [local(0, heads // 2)]
    line, locals_ = lax.optimization_barrier((line, locals_))
    slab_total = jnp.sum(line.astype(F32), axis=0).astype(BF16)
    totals = [lax.ppermute(slab_total, "seq", flip(m)) for m in range(1, slabs)]
    third = local(heads // 2, heads // 4)
    totals, third = lax.optimization_barrier((totals, third))
    piece_shape = (per_group, PACKED, HEAD_DIM)
    prefix = pl.pallas_call(
        prefix_kernel,
        in_specs=[pl.BlockSpec(memory_space=pltpu.SMEM)] + [vmem] * slabs,
        out_specs=[vmem] * layers,
        out_shape=[jax.ShapeDtypeStruct(piece_shape, BF16)] * layers,
        scratch_shapes=[pltpu.VMEM((layers,) + piece_shape, BF16)],
    )(at, line, *totals)
    prefix = [prefix[0]] + [lax.ppermute(prefix[d], "z", turn(-d)) for d in range(1, layers)]
    locals_ = locals_ + [third, local(3 * heads // 4, heads // 4)]

    def hidden(chunk):
        some = rows // 2
        specs, arrays = [], []
        for num, phi in locals_:
            count = phi.shape[1]
            specs.append(pl.BlockSpec((1, some, count * HEAD_DIM), lambda i, _: (chunk, i, 0)))
            specs.append(pl.BlockSpec((1, count, some, PACKED), lambda i, _: (chunk, 0, i, 0)))
            arrays += [num, phi]
        return call(
            lambda at_ref, *refs: hidden_kernel(at_ref, layers, *refs),
            at,
            (2,),
            [whole((1, heads * HEAD_DIM))] + [whole(piece_shape)] * layers + specs,
            pl.BlockSpec((some, heads * HEAD_DIM), lambda i, _: (i, 0)),
            jax.ShapeDtypeStruct((rows, heads * HEAD_DIM), BF16),
            (gain_mine, *prefix, *arrays),
            rows * heads * HEAD_DIM * 600,
            [pltpu.VMEM((layers,) + piece_shape, BF16)],
            mib=16,
        )

    w_rows = w_out.reshape(layers, 2, value_width, model)

    def project_out(kept, received, to):
        block = (layers, 1, value_width, width)
        specs = []
        for d in to:
            columns = lambda at, d=d: 2 * lax.rem(at[1] + d, layers) + at[0]
            specs.append(pl.BlockSpec(block, lambda i, at, columns=columns: (0, at[0], 0, columns(at))))
            specs.append(pl.BlockSpec(block, lambda i, at, columns=columns: (0, 1 - at[0], 0, columns(at))))
        return call(
            output_kernel,
            at,
            (1,),
            [whole((rows, heads * HEAD_DIM))] * 2 + specs,
            [whole((rows, width))] * len(to),
            [jax.ShapeDtypeStruct((rows, width), BF16)] * len(to),
            (kept, received, *[w_rows] * len(specs)),
            2 * rows * model * width * len(to),
            mib=20,
        )

    kept = [hidden(chunk) for chunk in range(2)]
    received = [lax.ppermute(half, "core", swap) for half in kept]
    order = [far] + [d for d in range(1, layers) if d != far] + [0]
    pieces = {}
    for start in range(0, layers, 2):
        to = order[start : start + 2]
        for chunk in range(2):
            for d, piece in zip(to, project_out(kept[chunk], received[chunk], to)):
                pieces[d, chunk] = lax.ppermute(piece, "z", turn(d)) if d else piece
    return call(
        place_kernel,
        at,
        (1,),
        [vmem] * (2 * layers),
        anywhere,
        jax.ShapeDtypeStruct((groups * rows, width), BF16),
        tuple(pieces[d, chunk] for d in range(layers) for chunk in range(2)),
        0,
        [pltpu.SemaphoreType.DMA((2 * layers,))],
        mib=8,
    )


def solution(mesh):
    slabs, groups = mesh.shape["seq"], mesh.shape["chan"]
    split = jax.sharding.Mesh(mesh.devices.reshape(slabs, groups // 2, 2), ("seq", "z", "core"))
    chan = ("z", "core")
    return jax.shard_map(
        per_device,
        mesh=split,
        in_specs=(P("seq", chan), P(), P(), P(None, chan), P(), P()),
        out_specs=P("seq", chan),
        check_vma=False,
    )
```

```python
import jax
import jax.numpy as jnp
import numpy as np
from jax import lax
from jax.experimental import pallas as pl
from jax.experimental.pallas import tpu as pltpu
from jax.sharding import PartitionSpec as P

HEADS = 16
FEAT = 16
HEAD_DIM = 128
PACKED = 160
LANES = 128
HELD = LANES // FEAT
MIB = 1024 * 1024

F32 = jnp.float32
BF16 = jnp.bfloat16
NN = (((1,), (0,)), ((), ()))
NT = (((1,), (1,)), ((), ()))


def dot(a, b, dims=NN):
    return lax.dot_general(a, b, dims, preferred_element_type=F32)


def feature_tables():
    first = np.zeros((FEAT, PACKED), np.float32)
    second = np.zeros((FEAT, PACKED), np.float32)
    first_bias = np.zeros((PACKED,), np.float32)
    second_bias = np.zeros((PACKED,), np.float32)
    scale = np.zeros((PACKED,), np.float32)
    first_bias[0] = second_bias[0] = scale[0] = 1.0
    place = 1
    for i in range(FEAT):
        first[i, place] = 1.0
        second_bias[place] = 1.0
        scale[place] = 1.0 / 4.0
        place += 1
    for i in range(FEAT):
        for j in range(i, FEAT):
            first[i, place] = 1.0
            second[j, place] = 1.0
            scale[place] = 1.0 / 32.0 if i == j else 1.0 / 16.0
            place += 1
    return first, second, first_bias, second_bias, scale


def placed(table):
    out = np.zeros((HELD, LANES, PACKED), np.float32)
    for place in range(HELD):
        out[place, place * FEAT : (place + 1) * FEAT] = table
    return out


def places_of(core, per_group):
    return [p for p in range(HELD) if (p // per_group) % 2 == core]


def stacked(table, per_group):
    every = placed(table).transpose(0, 2, 1)
    return np.stack([every[places_of(core, per_group)].reshape(-1, LANES) for core in range(2)])


def project_kernel(at_ref, per_group, layers, gathered, *refs):
    mine, other = refs[:layers], refs[layers : 2 * layers]
    table_ref, bias_ref, wq_ref, wk_ref, own_ref = refs[2 * layers : 2 * layers + 5]
    rest = refs[2 * layers + 5 :]
    weights, rest = rest[:-16], rest[-16:]
    results, rest = rest[:5], rest[5:]
    q_ref, k_ref, v_ref, early_ref, total_ref, row_ref, narrow_ref, w_ref, phi_ref, sems, out_sems = rest
    core, layer, slab = at_ref[0], at_ref[1], at_ref[2]
    both, width = other[0].shape
    rows = both // 2
    model = row_ref.shape[1]
    part = weights[0].shape[-2]
    block = v_ref.shape[2] // layers
    narrow = wq_ref.shape[1]
    copies = []

    def fetch(slot, source, to):
        copies.append((slot, pltpu.make_async_copy(source, to, sems.at[len(copies)])))
        copies[-1][1].start()

    fetch(-1, wq_ref, narrow_ref.at[:, pl.ds(0, narrow)])
    fetch(-1, wk_ref, narrow_ref.at[:, pl.ds(narrow, narrow)])
    fetch(0, own_ref, w_ref.at[0, :, pl.ds(0, block)])
    for d in range(1, layers):
        if gathered:
            sources = [(weights[0].at[m, d - 1], m * part) for m in range(model // part)]
        else:
            upper, lower, upper_1, lower_2, upper_2, lower_1 = weights
            base = [pl.multiple_of((slab ^ m) * 2 * part, part) for m in range(4)]
            sources = [
                (upper.at[d - 1], base[0]),
                (lower.at[d - 1], base[0] + part),
                (upper_1.at[d - 1], base[1]),
                (lower_2.at[d - 1], base[2] + part),
                (upper_2.at[0, d - 1], base[2]),
                (lower_1.at[0, d - 1], base[1] + part),
                (upper_2.at[1, d - 1], base[3]),
                (lower_1.at[1, d - 1], base[3] + part),
            ]
        for source, start in sources:
            start = pl.multiple_of(start, part)
            fetch(d, source, w_ref.at[d // 2, pl.ds(start, part), pl.ds((d % 2) * block, block)])

    kept = []

    def keep(source, to):
        kept.append(pltpu.make_async_copy(source, to, out_sems.at[len(kept)]))
        kept[-1].start()

    def arrived(slots):
        for slot, copy in copies:
            if slot in slots:
                copy.wait()

    for d in range(layers):
        z = lax.rem(layer + layers - d, layers)
        here = pl.multiple_of((2 * z + core) * width, width)
        there = pl.multiple_of((2 * z + 1 - core) * width, width)
        row_ref[:, pl.ds(here, width)] = mine[d][0] if d == 0 else mine[d][...]
        row_ref[:, pl.ds(there, width)] = other[d][...]
    arrived((-1,))
    half = table_ref.shape[1] // 2
    both_narrow = dot(row_ref[...], narrow_ref[...]).astype(BF16)
    for chunk in range(2):
        at = slice(chunk * rows, (chunk + 1) * rows)
        q_ref[chunk] = both_narrow[at, :narrow]
        k_ref[chunk] = both_narrow[at, narrow:]
        for lanes in range(0, narrow, LANES):
            product = dot(table_ref[0], both_narrow[at, narrow + lanes : narrow + lanes + LANES], NT)
            left = product[:half] + bias_ref[:, 0:1]
            right = product[half:] + bias_ref[:, 1:2]
            to = (lanes // LANES) * half
            phi_ref[chunk, to : to + half, :] = (left * right).astype(BF16)
    keep(q_ref, results[0])
    keep(k_ref, results[1])

    for pair in range(layers // 2):
        arrived((2 * pair, 2 * pair + 1))
        value = dot(row_ref[...], w_ref[pair]).astype(BF16)
        for d in (2 * pair, 2 * pair + 1):
            z = lax.rem(layer + d, layers)
            side = (d % 2) * block
            lanes = pl.multiple_of(z * block, block)
            for chunk in range(2):
                at = slice(chunk * rows, (chunk + 1) * rows)
                v_ref[chunk, :, pl.ds(lanes, block)] = value[at, side : side + block]
            for i in range(per_group):
                head = z * per_group + i
                place = pl.multiple_of(head * PACKED, PACKED)
                column = side + i * HEAD_DIM
                early = dot(phi_ref[0, pl.ds(place, PACKED), :], value[:rows, column : column + HEAD_DIM])
                late = dot(phi_ref[1, pl.ds(place, PACKED), :], value[rows:, column : column + HEAD_DIM])
                early_ref[head] = early.astype(BF16)
                total_ref[head] = (early + late).astype(BF16)
            own = pl.ds(z * per_group, per_group)
            keep(total_ref.at[own], results[4].at[own])
            keep(early_ref.at[own], results[3].at[own])
            keep(v_ref.at[:, :, pl.ds(lanes, block)], results[2].at[:, :, pl.ds(lanes, block)])
    for copy in kept:
        copy.wait()


def local_kernel(at_ref, per_group, offset, q_ref, k_ref, v_ref, early_ref, table_ref, bias_ref, num_ref, phi_ref):
    rows = q_ref.shape[1]
    cut = LANES * -(-rows // (2 * LANES))
    wide = table_ref.shape[-1] // 2
    local_head = pl.program_id(0) + offset
    head = (2 * (local_head // per_group) + at_ref[0]) * per_group + lax.rem(local_head, per_group)
    lanes = pl.multiple_of((head // HELD) * LANES, LANES)
    place = lax.rem(head, HELD)
    lane = lax.broadcasted_iota(jnp.int32, (rows, LANES), 1) // FEAT
    for chunk in range(2):
        query = q_ref[chunk, :, pl.ds(lanes, LANES)]
        key = k_ref[chunk, :, pl.ds(lanes, LANES)]
        sides = dot(query, table_ref[0, lax.rem(local_head, HELD // 2)]) + bias_ref[...]
        phi = (sides[:, :PACKED] * sides[:, wide : wide + PACKED]).astype(BF16)
        phi_ref[chunk, 0] = phi
        mine = jnp.where(lane == place, query * jnp.asarray(0.25, BF16), jnp.zeros_like(query))
        for low, high in ((0, cut), (cut, rows)):
            span = high - low
            s = dot(mine[low:high], key[low:high], NT)
            t_at = lax.broadcasted_iota(jnp.int32, (span, span), 0)
            j_at = lax.broadcasted_iota(jnp.int32, (span, span), 1)
            weight = jnp.where(t_at >= j_at, (0.5 * s + 1.0) * s + 1.0, 0.0).astype(BF16)
            num = dot(weight, v_ref[chunk, low:high, :])
            if low > 0:
                s = dot(mine[low:high], key[:low], NT)
                weight = ((0.5 * s + 1.0) * s + 1.0).astype(BF16)
                num = num + dot(weight, v_ref[chunk, :low, :])
            if chunk > 0:
                num = num + dot(phi[low:high], early_ref[0])
            num_ref[chunk, low:high, :] = num.astype(BF16)


def prefix_kernel(at_ref, line_ref, *refs):
    layers = line_ref.shape[0]
    totals, outs, sum_ref = refs[: -layers - 1], refs[-layers - 1 : -1], refs[-1]
    layer, slab = at_ref[1], at_ref[2]
    run = jnp.zeros(line_ref.shape[1:], F32)
    for m, total in enumerate(totals, 1):
        run = run + total[...].astype(F32) * jnp.where((slab ^ m) < slab, 1.0, 0.0)
    for z in range(layers):
        sum_ref[z] = run.astype(BF16)
        run = run + line_ref[z].astype(F32)
    for d in range(layers):
        outs[d][...] = sum_ref[lax.rem(layer + layers - d, layers)]


def hidden_kernel(at_ref, layers, gain_ref, *refs):
    pieces, parts, out_ref, state_ref = refs[:layers], refs[layers:-2], refs[-2], refs[-1]
    group = pieces[0].shape[0]
    for d in range(layers):
        state_ref[lax.rem(at_ref[1] + d, layers)] = pieces[d][...]
    head = 0
    for num_ref, phi_ref in zip(parts[0::2], parts[1::2]):
        for i in range(phi_ref.shape[1]):
            columns = slice(head * HEAD_DIM, (head + 1) * HEAD_DIM)
            num = num_ref[0, :, i * HEAD_DIM : (i + 1) * HEAD_DIM].astype(F32)
            num = num + dot(phi_ref[0, i], state_ref[head // group, head % group])
            mean_square = jnp.mean(num * num, axis=1, keepdims=True)
            hidden = num * lax.rsqrt(mean_square + 1e-05) * gain_ref[:, columns]
            out_ref[:, columns] = hidden.astype(BF16)
            head += 1


def output_kernel(at_ref, mine_ref, other_ref, *refs):
    outs = refs[len(refs) * 2 // 3 :]
    weights = [w[...].reshape(mine_ref.shape[1], -1) for w in refs[: 2 * len(outs)]]
    width = weights[0].shape[1]
    part = dot(mine_ref[...], jnp.concatenate(weights[0::2], axis=1))
    part = part + dot(other_ref[...], jnp.concatenate(weights[1::2], axis=1))
    for i, out_ref in enumerate(outs):
        out_ref[...] = part[:, i * width : (i + 1) * width].astype(BF16)


def place_kernel(at_ref, *refs):
    pieces, out_ref, sems = refs[:-2], refs[-2], refs[-1]
    layers = len(pieces) // 2
    copies = []
    for i, piece in enumerate(pieces):
        rows = piece.shape[0]
        z = lax.rem(at_ref[1] + layers - i // 2, layers)
        to = out_ref.at[pl.ds(pl.multiple_of((2 * z + i % 2) * rows, rows), rows)]
        copies.append(pltpu.make_async_copy(piece, to, sems.at[i]))
    for copy in copies:
        copy.start()
    for copy in copies:
        copy.wait()


def whole(shape):
    return pl.BlockSpec(shape, lambda *_: (0,) * len(shape))


def params(mib):
    return pltpu.CompilerParams(vmem_limit_bytes=mib * MIB)


def call(kernel, scalar, grid, in_specs, out_specs, out_shape, args, flops, scratch=(), mib=60):
    return pl.pallas_call(
        kernel,
        grid_spec=pltpu.PrefetchScalarGridSpec(
            num_scalar_prefetch=1,
            grid=grid,
            in_specs=in_specs,
            out_specs=out_specs,
            scratch_shapes=list(scratch),
        ),
        out_shape=out_shape,
        compiler_params=params(mib),
        cost_estimate=pl.CostEstimate(flops=flops, bytes_accessed=12 * MIB, transcendentals=0),
    )(scalar, *args)


def per_device(tokens, w_query, w_key, w_value, w_out, gain):
    slabs = lax.axis_size("seq")
    layers = lax.axis_size("z")
    groups = 2 * layers
    my_slab = lax.axis_index("seq")
    core = lax.axis_index("core").astype(jnp.int32)
    layer = lax.axis_index("z").astype(jnp.int32)
    which = core.reshape(1)
    width = tokens.shape[1]
    rows = tokens.shape[0] // groups
    model, value_width = w_value.shape
    part = model // slabs
    per_group = HEADS // groups
    heads = HEADS // 2
    narrow = w_query.shape[1]
    swap = [(0, 1), (1, 0)]

    first, second, first_bias, second_bias, scale = feature_tables()
    sides = [stacked(first, per_group), stacked(second, per_group)]
    key_table = jnp.asarray(np.concatenate(sides, axis=1), BF16)
    repeat = HELD // 2
    key_bias = jnp.asarray(np.stack([np.tile(first_bias, repeat), np.tile(second_bias, repeat)], axis=1))
    wide = 2 * LANES
    query_table = np.zeros((HELD, LANES, 2 * wide), np.float32)
    query_bias = np.zeros((1, 2 * wide), np.float32)
    query_table[:, :, :PACKED] = placed(first * scale)
    query_table[:, :, wide : wide + PACKED] = placed(second)
    query_table = np.stack([query_table[places_of(core, per_group)] for core in range(2)])
    query_bias[0, :PACKED] = first_bias * scale
    query_bias[0, wide : wide + PACKED] = second_bias
    query_table, query_bias = jnp.asarray(query_table, BF16), jnp.asarray(query_bias)
    gain_mine = lax.dynamic_index_in_dim(gain.reshape(layers, 2, value_width), core, 1, False)
    gain_mine = gain_mine.reshape(1, layers * value_width)

    flip = lambda m: [(s, s ^ m) for s in range(slabs)]
    turn = lambda d: [(z, (z + d) % layers) for z in range(layers)]
    anywhere = pl.BlockSpec(memory_space=pl.ANY)
    vmem = pl.BlockSpec(memory_space=pltpu.VMEM)
    at = jnp.stack([core, layer, my_slab.astype(jnp.int32)])

    value_part = lax.dynamic_slice_in_dim(w_value, my_slab * part, part, 0)
    blocks = tokens.reshape(layers, 2 * rows, width)
    sent = [lax.dynamic_index_in_dim(blocks, lax.rem(layer + d, layers), 0, False) for d in range(layers)]
    quarters = [lax.ppermute(value_part, "z", turn(-d)) for d in range(1, layers)]
    upper = jnp.stack([quarter[: part // 2] for quarter in quarters])
    lower = jnp.stack([quarter[part // 2 :] for quarter in quarters])
    upper, lower, sent = lax.optimization_barrier((upper, lower, sent))
    if slabs == 4:
        upper_1 = lax.ppermute(upper, "seq", flip(1))
        lower_2 = lax.ppermute(lower, "seq", flip(2))
        upper_2 = lax.ppermute(jnp.stack([upper, upper_1]), "seq", flip(2))
        lower_1 = lax.ppermute(jnp.stack([lower, lower_2]), "seq", flip(1))
        weights = [upper, lower, upper_1, lower_2, upper_2, lower_1]
    else:
        stack = jnp.concatenate([upper, lower], axis=1)
        weights = [lax.all_gather(stack, "seq", axis=0, tiled=False)]
    far = layers // 2
    mine = {d: lax.ppermute(sent[d], "z", turn(d)) for d in [far] + [d for d in range(1, layers) if d != far]}
    mine = [sent[0]] + [mine[d] for d in range(1, layers)]
    mine[1:], weights[2:] = lax.optimization_barrier((mine[1:], weights[2:]))
    other = [lax.ppermute(piece, "core", swap) for piece in mine]

    query, key, value, early, total = call(
        lambda at_ref, *refs: project_kernel(at_ref, per_group, layers, slabs != 4, *refs),
        at,
        (1,),
        [pl.BlockSpec((1, 2 * rows, width), lambda i, at: (at[1], 0, 0))]
        + [whole((2 * rows, width))] * (2 * layers - 1)
        + [
            pl.BlockSpec((1,) + key_table.shape[1:], lambda i, at: (at[0], 0, 0)),
            whole(key_bias.shape),
        ]
        + [anywhere] * (3 + len(weights)),
        [anywhere] * 5,
        [
            jax.ShapeDtypeStruct((2, rows, narrow), BF16),
            jax.ShapeDtypeStruct((2, rows, narrow), BF16),
            jax.ShapeDtypeStruct((2, rows, layers * value_width), BF16),
            jax.ShapeDtypeStruct((heads, PACKED, HEAD_DIM), BF16),
            jax.ShapeDtypeStruct((heads, PACKED, HEAD_DIM), BF16),
        ],
        (blocks, *mine[1:], *other, key_table, key_bias, w_query, w_key, w_value, *weights),
        4 * rows * model * (model // 2 + 2 * narrow),
        [
            pltpu.VMEM((2, rows, narrow), BF16),
            pltpu.VMEM((2, rows, narrow), BF16),
            pltpu.VMEM((2, rows, layers * value_width), BF16),
            pltpu.VMEM((heads, PACKED, HEAD_DIM), BF16),
            pltpu.VMEM((heads, PACKED, HEAD_DIM), BF16),
            pltpu.VMEM((2 * rows, model), BF16),
            pltpu.VMEM((model, 2 * narrow), BF16),
            pltpu.VMEM((layers // 2, model, 2 * value_width), BF16),
            pltpu.VMEM((2, heads * PACKED, rows), BF16),
            pltpu.SemaphoreType.DMA((3 + (layers - 1) * max(8, slabs),)),
            pltpu.SemaphoreType.DMA((2 + 3 * layers,)),
        ],
    )

    def local(offset, count):
        return call(
            lambda core_ref, *refs: local_kernel(core_ref, per_group, offset, *refs),
            at,
            (count,),
            [
                whole((2, rows, narrow)),
                whole((2, rows, narrow)),
                pl.BlockSpec((2, rows, HEAD_DIM), lambda i, _: (0, 0, i + offset)),
                pl.BlockSpec((1, PACKED, HEAD_DIM), lambda i, _: (i + offset, 0, 0)),
                pl.BlockSpec((1,) + query_table.shape[1:], lambda i, at: (at[0], 0, 0, 0)),
                whole(query_bias.shape),
            ],
            [
                pl.BlockSpec((2, rows, HEAD_DIM), lambda i, _: (0, 0, i)),
                pl.BlockSpec((2, 1, rows, PACKED), lambda i, _: (0, i, 0, 0)),
            ],
            [
                jax.ShapeDtypeStruct((2, rows, count * HEAD_DIM), BF16),
                jax.ShapeDtypeStruct((2, count, rows, PACKED), BF16),
            ],
            (query, key, value, early, query_table, query_bias),
            count * rows * rows * 1200,
        )

    own = total.reshape(layers, per_group, PACKED, HEAD_DIM)
    line = lax.all_to_all(own, "z", split_axis=0, concat_axis=0, tiled=True)
    locals_ = [local(0, heads // 2)]
    line, locals_ = lax.optimization_barrier((line, locals_))
    slab_total = jnp.sum(line.astype(F32), axis=0).astype(BF16)
    totals = [lax.ppermute(slab_total, "seq", flip(m)) for m in range(1, slabs)]
    third = local(heads // 2, heads // 4)
    totals, third = lax.optimization_barrier((totals, third))
    piece_shape = (per_group, PACKED, HEAD_DIM)
    prefix = pl.pallas_call(
        prefix_kernel,
        in_specs=[pl.BlockSpec(memory_space=pltpu.SMEM)] + [vmem] * slabs,
        out_specs=[vmem] * layers,
        out_shape=[jax.ShapeDtypeStruct(piece_shape, BF16)] * layers,
        scratch_shapes=[pltpu.VMEM((layers,) + piece_shape, BF16)],
    )(at, line, *totals)
    prefix = [prefix[0]] + [lax.ppermute(prefix[d], "z", turn(-d)) for d in range(1, layers)]
    locals_ = locals_ + [third, local(3 * heads // 4, heads // 4)]

    def hidden(chunk):
        some = rows // 2
        specs, arrays = [], []
        for num, phi in locals_:
            count = phi.shape[1]
            specs.append(pl.BlockSpec((1, some, count * HEAD_DIM), lambda i, _: (chunk, i, 0)))
            specs.append(pl.BlockSpec((1, count, some, PACKED), lambda i, _: (chunk, 0, i, 0)))
            arrays += [num, phi]
        return call(
            lambda at_ref, *refs: hidden_kernel(at_ref, layers, *refs),
            at,
            (2,),
            [whole((1, heads * HEAD_DIM))] + [whole(piece_shape)] * layers + specs,
            pl.BlockSpec((some, heads * HEAD_DIM), lambda i, _: (i, 0)),
            jax.ShapeDtypeStruct((rows, heads * HEAD_DIM), BF16),
            (gain_mine, *prefix, *arrays),
            rows * heads * HEAD_DIM * 600,
            [pltpu.VMEM((layers,) + piece_shape, BF16)],
            mib=16,
        )

    w_rows = w_out.reshape(layers, 2, value_width, model)

    def project_out(kept, received, to):
        block = (layers, 1, value_width, width)
        specs = []
        for d in to:
            columns = lambda at, d=d: 2 * lax.rem(at[1] + d, layers) + at[0]
            specs.append(pl.BlockSpec(block, lambda i, at, columns=columns: (0, at[0], 0, columns(at))))
            specs.append(pl.BlockSpec(block, lambda i, at, columns=columns: (0, 1 - at[0], 0, columns(at))))
        return call(
            output_kernel,
            at,
            (1,),
            [whole((rows, heads * HEAD_DIM))] * 2 + specs,
            [whole((rows, width))] * len(to),
            [jax.ShapeDtypeStruct((rows, width), BF16)] * len(to),
            (kept, received, *[w_rows] * len(specs)),
            2 * rows * model * width * len(to),
            mib=20,
        )

    kept = [hidden(chunk) for chunk in range(2)]
    received = [lax.ppermute(half, "core", swap) for half in kept]
    order = [far] + [d for d in range(1, layers) if d != far] + [0]
    pieces = {}
    for start in range(0, layers, 2):
        to = order[start : start + 2]
        for chunk in range(2):
            for d, piece in zip(to, project_out(kept[chunk], received[chunk], to)):
                pieces[d, chunk] = lax.ppermute(piece, "z", turn(d)) if d else piece
    return call(
        place_kernel,
        at,
        (1,),
        [vmem] * (2 * layers),
        anywhere,
        jax.ShapeDtypeStruct((groups * rows, width), BF16),
        tuple(pieces[d, chunk] for d in range(layers) for chunk in range(2)),
        0,
        [pltpu.SemaphoreType.DMA((2 * layers,))],
        mib=8,
    )


def solution(mesh):
    slabs, groups = mesh.shape["seq"], mesh.shape["chan"]
    split = jax.sharding.Mesh(mesh.devices.reshape(slabs, groups // 2, 2), ("seq", "z", "core"))
    chan = ("z", "core")
    return jax.shard_map(
        per_device,
        mesh=split,
        in_specs=(P("seq", chan), P(), P(), P(None, chan), P(), P()),
        out_specs=P("seq", chan),
        check_vma=False,
    )
```

```python
import jax
import jax.numpy as jnp
import numpy as np
from jax import lax
from jax.experimental import pallas as pl
from jax.experimental.pallas import tpu as pltpu
from jax.sharding import PartitionSpec as P

HEADS = 16
FEAT = 16
HEAD_DIM = 128
PACKED = 160
LANES = 128
HELD = LANES // FEAT
MIB = 1024 * 1024

F32 = jnp.float32
BF16 = jnp.bfloat16
NN = (((1,), (0,)), ((), ()))
NT = (((1,), (1,)), ((), ()))


def dot(a, b, dims=NN):
    return lax.dot_general(a, b, dims, preferred_element_type=F32)


def feature_tables():
    first = np.zeros((FEAT, PACKED), np.float32)
    second = np.zeros((FEAT, PACKED), np.float32)
    first_bias = np.zeros((PACKED,), np.float32)
    second_bias = np.zeros((PACKED,), np.float32)
    scale = np.zeros((PACKED,), np.float32)
    first_bias[0] = second_bias[0] = scale[0] = 1.0
    place = 1
    for i in range(FEAT):
        first[i, place] = 1.0
        second_bias[place] = 1.0
        scale[place] = 1.0 / 4.0
        place += 1
    for i in range(FEAT):
        for j in range(i, FEAT):
            first[i, place] = 1.0
            second[j, place] = 1.0
            scale[place] = 1.0 / 32.0 if i == j else 1.0 / 16.0
            place += 1
    return first, second, first_bias, second_bias, scale


def placed(table):
    out = np.zeros((HELD, LANES, PACKED), np.float32)
    for place in range(HELD):
        out[place, place * FEAT : (place + 1) * FEAT] = table
    return out


def places_of(core, per_group):
    return [p for p in range(HELD) if (p // per_group) % 2 == core]


def stacked(table, per_group):
    every = placed(table).transpose(0, 2, 1)
    return np.stack([every[places_of(core, per_group)].reshape(-1, LANES) for core in range(2)])


def project_kernel(at_ref, per_group, layers, gathered, *refs):
    mine, other = refs[:layers], refs[layers : 2 * layers]
    table_ref, bias_ref, wq_ref, wk_ref, own_ref = refs[2 * layers : 2 * layers + 5]
    rest = refs[2 * layers + 5 :]
    weights, rest = rest[:-10], rest[-10:]
    q_ref, k_ref, v_ref, early_ref, total_ref, row_ref, narrow_ref, w_ref, phi_ref, sems = rest
    core, layer, slab = at_ref[0], at_ref[1], at_ref[2]
    both, width = other[0].shape
    rows = both // 2
    model = row_ref.shape[1]
    part = weights[0].shape[-2]
    block = v_ref.shape[2] // layers
    narrow = wq_ref.shape[1]
    copies = []

    def fetch(slot, source, to):
        copies.append((slot, pltpu.make_async_copy(source, to, sems.at[len(copies)])))
        copies[-1][1].start()

    for chunk in range(2):
        for d in range(layers):
            z = lax.rem(layer + layers - d, layers)
            for piece, place in ((mine[d].at[layer] if d == 0 else mine[d], core), (other[d], 1 - core)):
                columns = pl.ds(pl.multiple_of((2 * z + place) * width, width), width)
                at = pl.ds(chunk * rows, rows)
                fetch(-1 - chunk, piece.at[at], row_ref.at[at, columns])
        if chunk == 0:
            fetch(-3, wq_ref, narrow_ref.at[:, pl.ds(0, narrow)])
            fetch(-3, wk_ref, narrow_ref.at[:, pl.ds(narrow, narrow)])
    fetch(0, own_ref, w_ref.at[0, :, pl.ds(0, block)])
    for d in range(1, layers):
        for m in range(model // part):
            if gathered:
                source, start = weights[0].at[m, d - 1], m * part
            else:
                source, start = weights[m].at[d - 1], pl.multiple_of((slab ^ m) * part, part)
            fetch(d, source, w_ref.at[d // 2, pl.ds(start, part), pl.ds((d % 2) * block, block)])

    def arrived(slots):
        for slot, copy in copies:
            if slot in slots:
                copy.wait()

    half = table_ref.shape[1] // 2
    for chunk in range(2):
        arrived((-1, -3) if chunk == 0 else (-2,))
        both_narrow = dot(row_ref[chunk * rows : (chunk + 1) * rows, :], narrow_ref[...]).astype(BF16)
        q_ref[chunk] = both_narrow[:, :narrow]
        k_ref[chunk] = both_narrow[:, narrow:]
        for lanes in range(0, narrow, LANES):
            product = dot(table_ref[0], both_narrow[:, narrow + lanes : narrow + lanes + LANES], NT)
            left = product[:half] + bias_ref[:, 0:1]
            right = product[half:] + bias_ref[:, 1:2]
            to = (lanes // LANES) * half
            phi_ref[chunk, to : to + half, :] = (left * right).astype(BF16)

    for pair in range(layers // 2):
        arrived((2 * pair, 2 * pair + 1))
        value = dot(row_ref[...], w_ref[pair]).astype(BF16)
        for d in (2 * pair, 2 * pair + 1):
            z = lax.rem(layer + d, layers)
            side = (d % 2) * block
            lanes = pl.multiple_of(z * block, block)
            for chunk in range(2):
                at = slice(chunk * rows, (chunk + 1) * rows)
                v_ref[chunk, :, pl.ds(lanes, block)] = value[at, side : side + block]
            for i in range(per_group):
                head = z * per_group + i
                place = pl.multiple_of(head * PACKED, PACKED)
                column = side + i * HEAD_DIM
                early = dot(phi_ref[0, pl.ds(place, PACKED), :], value[:rows, column : column + HEAD_DIM])
                late = dot(phi_ref[1, pl.ds(place, PACKED), :], value[rows:, column : column + HEAD_DIM])
                early_ref[head] = early.astype(BF16)
                total_ref[head] = (early + late).astype(BF16)


def local_kernel(at_ref, per_group, offset, q_ref, k_ref, v_ref, early_ref, table_ref, bias_ref, num_ref, phi_ref):
    rows = q_ref.shape[1]
    cut = LANES * -(-rows // (2 * LANES))
    wide = table_ref.shape[-1] // 2
    local_head = pl.program_id(0) + offset
    head = (2 * (local_head // per_group) + at_ref[0]) * per_group + lax.rem(local_head, per_group)
    lanes = pl.multiple_of((head // HELD) * LANES, LANES)
    place = lax.rem(head, HELD)
    lane = lax.broadcasted_iota(jnp.int32, (rows, LANES), 1) // FEAT
    for chunk in range(2):
        query = q_ref[chunk, :, pl.ds(lanes, LANES)]
        key = k_ref[chunk, :, pl.ds(lanes, LANES)]
        sides = dot(query, table_ref[0, lax.rem(local_head, HELD // 2)]) + bias_ref[...]
        phi = (sides[:, :PACKED] * sides[:, wide : wide + PACKED]).astype(BF16)
        phi_ref[chunk, 0] = phi
        mine = jnp.where(lane == place, query * jnp.asarray(0.25, BF16), jnp.zeros_like(query))
        for low, high in ((0, cut), (cut, rows)):
            span = high - low
            s = dot(mine[low:high], key[low:high], NT)
            t_at = lax.broadcasted_iota(jnp.int32, (span, span), 0)
            j_at = lax.broadcasted_iota(jnp.int32, (span, span), 1)
            weight = jnp.where(t_at >= j_at, (0.5 * s + 1.0) * s + 1.0, 0.0).astype(BF16)
            num = dot(weight, v_ref[chunk, low:high, :])
            if low > 0:
                s = dot(mine[low:high], key[:low], NT)
                weight = ((0.5 * s + 1.0) * s + 1.0).astype(BF16)
                num = num + dot(weight, v_ref[chunk, :low, :])
            if chunk > 0:
                num = num + dot(phi[low:high], early_ref[0])
            num_ref[chunk, low:high, :] = num


def prefix_kernel(at_ref, line_ref, *refs):
    layers = line_ref.shape[0]
    totals, outs, sum_ref = refs[: -layers - 1], refs[-layers - 1 : -1], refs[-1]
    layer, slab = at_ref[1], at_ref[2]
    run = jnp.zeros(line_ref.shape[1:], F32)
    for m, total in enumerate(totals, 1):
        run = run + total[...].astype(F32) * jnp.where((slab ^ m) < slab, 1.0, 0.0)
    for z in range(layers):
        sum_ref[z] = run.astype(BF16)
        run = run + line_ref[z].astype(F32)
    for d in range(layers):
        outs[d][...] = sum_ref[lax.rem(layer + layers - d, layers)]


def hidden_kernel(at_ref, layers, gain_ref, *refs):
    pieces, parts, out_ref, state_ref = refs[:layers], refs[layers:-2], refs[-2], refs[-1]
    group = pieces[0].shape[0]
    for d in range(layers):
        state_ref[lax.rem(at_ref[1] + d, layers)] = pieces[d][...]
    head = 0
    for num_ref, phi_ref in zip(parts[0::2], parts[1::2]):
        for i in range(phi_ref.shape[1]):
            columns = slice(head * HEAD_DIM, (head + 1) * HEAD_DIM)
            num = num_ref[0, :, i * HEAD_DIM : (i + 1) * HEAD_DIM]
            num = num + dot(phi_ref[0, i], state_ref[head // group, head % group])
            mean_square = jnp.mean(num * num, axis=1, keepdims=True)
            hidden = num * lax.rsqrt(mean_square + 1e-05) * gain_ref[:, columns]
            out_ref[:, columns] = hidden.astype(BF16)
            head += 1


def output_kernel(at_ref, mine_ref, other_ref, *refs):
    outs = refs[len(refs) * 2 // 3 :]
    weights = [w[...].reshape(mine_ref.shape[1], -1) for w in refs[: 2 * len(outs)]]
    width = weights[0].shape[1]
    part = dot(mine_ref[...], jnp.concatenate(weights[0::2], axis=1))
    part = part + dot(other_ref[...], jnp.concatenate(weights[1::2], axis=1))
    for i, out_ref in enumerate(outs):
        out_ref[...] = part[:, i * width : (i + 1) * width].astype(BF16)


def place_kernel(at_ref, *refs):
    pieces, out_ref, sems = refs[:-2], refs[-2], refs[-1]
    layers = len(pieces) // 2
    copies = []
    for i, piece in enumerate(pieces):
        rows = piece.shape[0]
        z = lax.rem(at_ref[1] + layers - i // 2, layers)
        to = out_ref.at[pl.ds(pl.multiple_of((2 * z + i % 2) * rows, rows), rows)]
        copies.append(pltpu.make_async_copy(piece, to, sems.at[i]))
    for copy in copies:
        copy.start()
    for copy in copies:
        copy.wait()


def whole(shape):
    return pl.BlockSpec(shape, lambda *_: (0,) * len(shape))


def params(mib):
    return pltpu.CompilerParams(vmem_limit_bytes=mib * MIB)


def call(kernel, scalar, grid, in_specs, out_specs, out_shape, args, flops, scratch=(), mib=60):
    return pl.pallas_call(
        kernel,
        grid_spec=pltpu.PrefetchScalarGridSpec(
            num_scalar_prefetch=1,
            grid=grid,
            in_specs=in_specs,
            out_specs=out_specs,
            scratch_shapes=list(scratch),
        ),
        out_shape=out_shape,
        compiler_params=params(mib),
        cost_estimate=pl.CostEstimate(flops=flops, bytes_accessed=12 * MIB, transcendentals=0),
    )(scalar, *args)


def per_device(tokens, w_query, w_key, w_value, w_out, gain):
    slabs = lax.axis_size("seq")
    layers = lax.axis_size("z")
    groups = 2 * layers
    my_slab = lax.axis_index("seq")
    core = lax.axis_index("core").astype(jnp.int32)
    layer = lax.axis_index("z").astype(jnp.int32)
    which = core.reshape(1)
    width = tokens.shape[1]
    rows = tokens.shape[0] // groups
    model, value_width = w_value.shape
    part = model // slabs
    per_group = HEADS // groups
    heads = HEADS // 2
    narrow = w_query.shape[1]
    swap = [(0, 1), (1, 0)]

    first, second, first_bias, second_bias, scale = feature_tables()
    sides = [stacked(first, per_group), stacked(second, per_group)]
    key_table = jnp.asarray(np.concatenate(sides, axis=1), BF16)
    repeat = HELD // 2
    key_bias = jnp.asarray(np.stack([np.tile(first_bias, repeat), np.tile(second_bias, repeat)], axis=1))
    wide = 2 * LANES
    query_table = np.zeros((HELD, LANES, 2 * wide), np.float32)
    query_bias = np.zeros((1, 2 * wide), np.float32)
    query_table[:, :, :PACKED] = placed(first * scale)
    query_table[:, :, wide : wide + PACKED] = placed(second)
    query_table = np.stack([query_table[places_of(core, per_group)] for core in range(2)])
    query_bias[0, :PACKED] = first_bias * scale
    query_bias[0, wide : wide + PACKED] = second_bias
    query_table, query_bias = jnp.asarray(query_table, BF16), jnp.asarray(query_bias)
    gain_mine = lax.dynamic_index_in_dim(gain.reshape(layers, 2, value_width), core, 1, False)
    gain_mine = gain_mine.reshape(1, layers * value_width)

    flip = lambda m: [(s, s ^ m) for s in range(slabs)]
    turn = lambda d: [(z, (z + d) % layers) for z in range(layers)]
    anywhere = pl.BlockSpec(memory_space=pl.ANY)
    vmem = pl.BlockSpec(memory_space=pltpu.VMEM)
    at = jnp.stack([core, layer, my_slab.astype(jnp.int32)])

    value_part = lax.dynamic_slice_in_dim(w_value, my_slab * part, part, 0)
    blocks = tokens.reshape(layers, 2 * rows, width)
    sent = [lax.dynamic_index_in_dim(blocks, lax.rem(layer + d, layers), 0, False) for d in range(layers)]
    stack = jnp.stack([lax.ppermute(value_part, "z", turn(-d)) for d in range(1, layers)])
    stack, sent = lax.optimization_barrier((stack, sent))
    if slabs == 4:
        weights = [stack] + [lax.ppermute(stack, "seq", flip(m)) for m in range(1, slabs)]
    else:
        weights = [lax.all_gather(stack, "seq", axis=0, tiled=False)]
    far = layers // 2
    mine = {d: lax.ppermute(sent[d], "z", turn(d)) for d in [far] + [d for d in range(1, layers) if d != far]}
    mine = [sent[0]] + [mine[d] for d in range(1, layers)]
    mine[1:], weights[1:] = lax.optimization_barrier((mine[1:], weights[1:]))
    other = [lax.ppermute(piece, "core", swap) for piece in mine]

    query, key, value, early, total = call(
        lambda at_ref, *refs: project_kernel(at_ref, per_group, layers, slabs != 4, *refs),
        at,
        (1,),
        [anywhere] * (2 * layers)
        + [
            pl.BlockSpec((1,) + key_table.shape[1:], lambda i, at: (at[0], 0, 0)),
            whole(key_bias.shape),
        ]
        + [anywhere] * (3 + len(weights)),
        [
            whole((2, rows, narrow)),
            whole((2, rows, narrow)),
            whole((2, rows, layers * value_width)),
            whole((heads, PACKED, HEAD_DIM)),
            whole((heads, PACKED, HEAD_DIM)),
        ],
        [
            jax.ShapeDtypeStruct((2, rows, narrow), BF16),
            jax.ShapeDtypeStruct((2, rows, narrow), BF16),
            jax.ShapeDtypeStruct((2, rows, layers * value_width), BF16),
            jax.ShapeDtypeStruct((heads, PACKED, HEAD_DIM), BF16),
            jax.ShapeDtypeStruct((heads, PACKED, HEAD_DIM), BF16),
        ],
        (blocks, *mine[1:], *other, key_table, key_bias, w_query, w_key, w_value, *weights),
        4 * rows * model * (model // 2 + 2 * narrow),
        [
            pltpu.VMEM((2 * rows, model), BF16),
            pltpu.VMEM((model, 2 * narrow), BF16),
            pltpu.VMEM((layers // 2, model, 2 * value_width), BF16),
            pltpu.VMEM((2, heads * PACKED, rows), BF16),
            pltpu.SemaphoreType.DMA((3 + 4 * layers + (layers - 1) * slabs,)),
        ],
    )

    def local(offset, count):
        return call(
            lambda core_ref, *refs: local_kernel(core_ref, per_group, offset, *refs),
            at,
            (count,),
            [
                whole((2, rows, narrow)),
                whole((2, rows, narrow)),
                pl.BlockSpec((2, rows, HEAD_DIM), lambda i, _: (0, 0, i + offset)),
                pl.BlockSpec((1, PACKED, HEAD_DIM), lambda i, _: (i + offset, 0, 0)),
                pl.BlockSpec((1,) + query_table.shape[1:], lambda i, at: (at[0], 0, 0, 0)),
                whole(query_bias.shape),
            ],
            [
                pl.BlockSpec((2, rows, HEAD_DIM), lambda i, _: (0, 0, i)),
                pl.BlockSpec((2, 1, rows, PACKED), lambda i, _: (0, i, 0, 0)),
            ],
            [
                jax.ShapeDtypeStruct((2, rows, count * HEAD_DIM), F32),
                jax.ShapeDtypeStruct((2, count, rows, PACKED), BF16),
            ],
            (query, key, value, early, query_table, query_bias),
            count * rows * rows * 1200,
        )

    own = total.reshape(layers, per_group, PACKED, HEAD_DIM)
    line = lax.all_to_all(own, "z", split_axis=0, concat_axis=0, tiled=True)
    locals_ = [local(0, 5 * heads // 8)]
    line, locals_ = lax.optimization_barrier((line, locals_))
    slab_total = jnp.sum(line.astype(F32), axis=0).astype(BF16)
    totals = [lax.ppermute(slab_total, "seq", flip(m)) for m in range(1, slabs)]
    rest = local(5 * heads // 8, 3 * heads // 8)
    totals, rest = lax.optimization_barrier((totals, rest))
    piece_shape = (per_group, PACKED, HEAD_DIM)
    prefix = pl.pallas_call(
        prefix_kernel,
        in_specs=[pl.BlockSpec(memory_space=pltpu.SMEM)] + [vmem] * slabs,
        out_specs=[vmem] * layers,
        out_shape=[jax.ShapeDtypeStruct(piece_shape, BF16)] * layers,
        scratch_shapes=[pltpu.VMEM((layers,) + piece_shape, BF16)],
    )(at, line, *totals)
    prefix = [prefix[0]] + [lax.ppermute(prefix[d], "z", turn(-d)) for d in range(1, layers)]
    locals_ = locals_ + [rest]

    def hidden(chunk):
        some = rows // 2
        specs, arrays = [], []
        for num, phi in locals_:
            count = phi.shape[1]
            specs.append(pl.BlockSpec((1, some, count * HEAD_DIM), lambda i, _: (chunk, i, 0)))
            specs.append(pl.BlockSpec((1, count, some, PACKED), lambda i, _: (chunk, 0, i, 0)))
            arrays += [num, phi]
        return call(
            lambda at_ref, *refs: hidden_kernel(at_ref, layers, *refs),
            at,
            (2,),
            [whole((1, heads * HEAD_DIM))] + [whole(piece_shape)] * layers + specs,
            pl.BlockSpec((some, heads * HEAD_DIM), lambda i, _: (i, 0)),
            jax.ShapeDtypeStruct((rows, heads * HEAD_DIM), BF16),
            (gain_mine, *prefix, *arrays),
            rows * heads * HEAD_DIM * 600,
            [pltpu.VMEM((layers,) + piece_shape, BF16)],
            mib=16,
        )

    w_rows = w_out.reshape(layers, 2, value_width, model)

    def project_out(kept, received, to):
        block = (layers, 1, value_width, width)
        specs = []
        for d in to:
            columns = lambda at, d=d: 2 * lax.rem(at[1] + d, layers) + at[0]
            specs.append(pl.BlockSpec(block, lambda i, at, columns=columns: (0, at[0], 0, columns(at))))
            specs.append(pl.BlockSpec(block, lambda i, at, columns=columns: (0, 1 - at[0], 0, columns(at))))
        return call(
            output_kernel,
            at,
            (1,),
            [whole((rows, heads * HEAD_DIM))] * 2 + specs,
            [whole((rows, width))] * len(to),
            [jax.ShapeDtypeStruct((rows, width), BF16)] * len(to),
            (kept, received, *[w_rows] * len(specs)),
            2 * rows * model * width * len(to),
            mib=20,
        )

    kept = [hidden(chunk) for chunk in range(2)]
    received = [lax.ppermute(half, "core", swap) for half in kept]
    order = [far] + [d for d in range(1, layers) if d != far] + [0]
    pieces = {}
    for start in range(0, layers, 2):
        to = order[start : start + 2]
        for chunk in range(2):
            for d, piece in zip(to, project_out(kept[chunk], received[chunk], to)):
                pieces[d, chunk] = lax.ppermute(piece, "z", turn(d)) if d else piece
    return call(
        place_kernel,
        at,
        (1,),
        [vmem] * (2 * layers),
        anywhere,
        jax.ShapeDtypeStruct((groups * rows, width), BF16),
        tuple(pieces[d, chunk] for d in range(layers) for chunk in range(2)),
        0,
        [pltpu.SemaphoreType.DMA((2 * layers,))],
        mib=8,
    )


def solution(mesh):
    slabs, groups = mesh.shape["seq"], mesh.shape["chan"]
    split = jax.sharding.Mesh(mesh.devices.reshape(slabs, groups // 2, 2), ("seq", "z", "core"))
    chan = ("z", "core")
    return jax.shard_map(
        per_device,
        mesh=split,
        in_specs=(P("seq", chan), P(), P(), P(None, chan), P(), P()),
        out_specs=P("seq", chan),
        check_vma=False,
    )
```

```python
import jax
import jax.numpy as jnp
import numpy as np
from jax import lax
from jax.experimental import pallas as pl
from jax.experimental.pallas import tpu as pltpu
from jax.sharding import PartitionSpec as P

HEADS = 16
FEAT = 16
HEAD_DIM = 128
PACKED = 160
LANES = 128
HELD = LANES // FEAT
MIB = 1024 * 1024

F32 = jnp.float32
BF16 = jnp.bfloat16
NN = (((1,), (0,)), ((), ()))
NT = (((1,), (1,)), ((), ()))


def dot(a, b, dims=NN):
    return lax.dot_general(a, b, dims, preferred_element_type=F32)


def feature_tables():
    first = np.zeros((FEAT, PACKED), np.float32)
    second = np.zeros((FEAT, PACKED), np.float32)
    first_bias = np.zeros((PACKED,), np.float32)
    second_bias = np.zeros((PACKED,), np.float32)
    scale = np.zeros((PACKED,), np.float32)
    first_bias[0] = second_bias[0] = scale[0] = 1.0
    place = 1
    for i in range(FEAT):
        first[i, place] = 1.0
        second_bias[place] = 1.0
        scale[place] = 1.0 / 4.0
        place += 1
    for i in range(FEAT):
        for j in range(i, FEAT):
            first[i, place] = 1.0
            second[j, place] = 1.0
            scale[place] = 1.0 / 32.0 if i == j else 1.0 / 16.0
            place += 1
    return first, second, first_bias, second_bias, scale


def placed(table):
    out = np.zeros((HELD, LANES, PACKED), np.float32)
    for place in range(HELD):
        out[place, place * FEAT : (place + 1) * FEAT] = table
    return out


def stacked(table, per_group):
    every = placed(table).transpose(0, 2, 1)
    own = [[p for p in range(HELD) if (p // per_group) % 2 == core] for core in range(2)]
    return np.stack([every[places].reshape(-1, LANES) for places in own])


def project_kernel(at_ref, per_group, layers, gathered, *refs):
    mine, other = refs[:layers], refs[layers : 2 * layers]
    table_ref, bias_ref, wq_ref, wk_ref, own_ref = refs[2 * layers : 2 * layers + 5]
    rest = refs[2 * layers + 5 :]
    weights, rest = rest[:-10], rest[-10:]
    q_ref, k_ref, v_ref, early_ref, total_ref, row_ref, narrow_ref, w_ref, phi_ref, sems = rest
    core, layer, slab = at_ref[0], at_ref[1], at_ref[2]
    both, width = other[0].shape
    rows = both // 2
    model = row_ref.shape[1]
    part = weights[0].shape[-2]
    block = v_ref.shape[2] // layers
    narrow = wq_ref.shape[1]
    copies = []

    def fetch(slot, source, to):
        copies.append((slot, pltpu.make_async_copy(source, to, sems.at[len(copies)])))
        copies[-1][1].start()

    fetch(-1, wq_ref, narrow_ref.at[:, pl.ds(0, narrow)])
    fetch(-1, wk_ref, narrow_ref.at[:, pl.ds(narrow, narrow)])
    fetch(0, own_ref, w_ref.at[0, :, pl.ds(0, block)])
    for d in range(1, layers):
        for m in range(model // part):
            if gathered:
                source, start = weights[0].at[m, d - 1], m * part
            else:
                source, start = weights[m].at[d - 1], pl.multiple_of((slab ^ m) * part, part)
            fetch(d, source, w_ref.at[d // 2, pl.ds(start, part), pl.ds((d % 2) * block, block)])

    def arrived(slots):
        for slot, copy in copies:
            if slot in slots:
                copy.wait()

    for d in range(layers):
        z = lax.rem(layer + layers - d, layers)
        here = pl.multiple_of((2 * z + core) * width, width)
        there = pl.multiple_of((2 * z + 1 - core) * width, width)
        row_ref[:, pl.ds(here, width)] = mine[d][0] if d == 0 else mine[d][...]
        row_ref[:, pl.ds(there, width)] = other[d][...]
    arrived((-1,))
    half = table_ref.shape[1] // 2
    both_narrow = dot(row_ref[...], narrow_ref[...]).astype(BF16)
    for chunk in range(2):
        at = slice(chunk * rows, (chunk + 1) * rows)
        q_ref[chunk] = both_narrow[at, :narrow]
        k_ref[chunk] = both_narrow[at, narrow:]
        for lanes in range(0, narrow, LANES):
            product = dot(table_ref[0], both_narrow[at, narrow + lanes : narrow + lanes + LANES], NT)
            left = product[:half] + bias_ref[:, 0:1]
            right = product[half:] + bias_ref[:, 1:2]
            to = (lanes // LANES) * half
            phi_ref[chunk, to : to + half, :] = (left * right).astype(BF16)

    for pair in range(layers // 2):
        arrived((2 * pair, 2 * pair + 1))
        value = dot(row_ref[...], w_ref[pair]).astype(BF16)
        for d in (2 * pair, 2 * pair + 1):
            z = lax.rem(layer + d, layers)
            side = (d % 2) * block
            lanes = pl.multiple_of(z * block, block)
            for chunk in range(2):
                at = slice(chunk * rows, (chunk + 1) * rows)
                v_ref[chunk, :, pl.ds(lanes, block)] = value[at, side : side + block]
            for i in range(per_group):
                head = z * per_group + i
                place = pl.multiple_of(head * PACKED, PACKED)
                column = side + i * HEAD_DIM
                early = dot(phi_ref[0, pl.ds(place, PACKED), :], value[:rows, column : column + HEAD_DIM])
                late = dot(phi_ref[1, pl.ds(place, PACKED), :], value[rows:, column : column + HEAD_DIM])
                early_ref[head] = early.astype(BF16)
                total_ref[head] = (early + late).astype(BF16)


def local_kernel(at_ref, per_group, offset, q_ref, k_ref, v_ref, early_ref, table_ref, bias_ref, num_ref, phi_ref):
    rows = q_ref.shape[1]
    cut = LANES * -(-rows // (2 * LANES))
    wide = table_ref.shape[2] // 2
    local_head = pl.program_id(0) + offset
    head = (2 * (local_head // per_group) + at_ref[0]) * per_group + lax.rem(local_head, per_group)
    lanes = pl.multiple_of((head // HELD) * LANES, LANES)
    place = lax.rem(head, HELD)
    lane = lax.broadcasted_iota(jnp.int32, (rows, LANES), 1) // FEAT
    for chunk in range(2):
        query = q_ref[chunk, :, pl.ds(lanes, LANES)]
        key = k_ref[chunk, :, pl.ds(lanes, LANES)]
        sides = dot(query, table_ref[place]) + bias_ref[...]
        phi = (sides[:, :PACKED] * sides[:, wide : wide + PACKED]).astype(BF16)
        phi_ref[chunk, 0] = phi
        mine = jnp.where(lane == place, query * jnp.asarray(0.25, BF16), jnp.zeros_like(query))
        for low, high in ((0, cut), (cut, rows)):
            span = high - low
            s = dot(mine[low:high], key[low:high], NT)
            t_at = lax.broadcasted_iota(jnp.int32, (span, span), 0)
            j_at = lax.broadcasted_iota(jnp.int32, (span, span), 1)
            weight = jnp.where(t_at >= j_at, (0.5 * s + 1.0) * s + 1.0, 0.0).astype(BF16)
            num = dot(weight, v_ref[chunk, low:high, :])
            if low > 0:
                s = dot(mine[low:high], key[:low], NT)
                weight = ((0.5 * s + 1.0) * s + 1.0).astype(BF16)
                num = num + dot(weight, v_ref[chunk, :low, :])
            if chunk > 0:
                num = num + dot(phi[low:high], early_ref[0])
            num_ref[chunk, low:high, :] = num


def prefix_kernel(at_ref, line_ref, *refs):
    layers = line_ref.shape[0]
    totals, outs, sum_ref = refs[: -layers - 1], refs[-layers - 1 : -1], refs[-1]
    layer, slab = at_ref[1], at_ref[2]
    run = jnp.zeros(line_ref.shape[1:], F32)
    for m, total in enumerate(totals, 1):
        run = run + total[...].astype(F32) * jnp.where((slab ^ m) < slab, 1.0, 0.0)
    for z in range(layers):
        sum_ref[z] = run.astype(BF16)
        run = run + line_ref[z].astype(F32)
    for d in range(layers):
        outs[d][...] = sum_ref[lax.rem(layer + layers - d, layers)]


def hidden_kernel(at_ref, layers, gain_ref, *refs):
    pieces, parts, out_ref, state_ref = refs[:layers], refs[layers:-2], refs[-2], refs[-1]
    group = pieces[0].shape[0]
    for d in range(layers):
        state_ref[lax.rem(at_ref[1] + d, layers)] = pieces[d][...]
    head = 0
    for num_ref, phi_ref in zip(parts[0::2], parts[1::2]):
        for i in range(phi_ref.shape[1]):
            columns = slice(head * HEAD_DIM, (head + 1) * HEAD_DIM)
            num = num_ref[0, :, i * HEAD_DIM : (i + 1) * HEAD_DIM]
            num = num + dot(phi_ref[0, i], state_ref[head // group, head % group])
            mean_square = jnp.mean(num * num, axis=1, keepdims=True)
            hidden = num * lax.rsqrt(mean_square + 1e-05) * gain_ref[:, columns]
            out_ref[:, columns] = hidden.astype(BF16)
            head += 1


def output_kernel(at_ref, mine_ref, other_ref, *refs):
    outs = refs[len(refs) * 2 // 3 :]
    weights = [w[...].reshape(mine_ref.shape[1], -1) for w in refs[: 2 * len(outs)]]
    width = weights[0].shape[1]
    part = dot(mine_ref[...], jnp.concatenate(weights[0::2], axis=1))
    part = part + dot(other_ref[...], jnp.concatenate(weights[1::2], axis=1))
    for i, out_ref in enumerate(outs):
        out_ref[...] = part[:, i * width : (i + 1) * width].astype(BF16)


def place_kernel(at_ref, *refs):
    pieces, out_ref, sems = refs[:-2], refs[-2], refs[-1]
    layers = len(pieces) // 2
    copies = []
    for i, piece in enumerate(pieces):
        rows = piece.shape[0]
        z = lax.rem(at_ref[1] + layers - i // 2, layers)
        to = out_ref.at[pl.ds(pl.multiple_of((2 * z + i % 2) * rows, rows), rows)]
        copies.append(pltpu.make_async_copy(piece, to, sems.at[i]))
    for copy in copies:
        copy.start()
    for copy in copies:
        copy.wait()


def whole(shape):
    return pl.BlockSpec(shape, lambda *_: (0,) * len(shape))


def params(mib):
    return pltpu.CompilerParams(vmem_limit_bytes=mib * MIB)


def call(kernel, scalar, grid, in_specs, out_specs, out_shape, args, flops, scratch=(), mib=60):
    return pl.pallas_call(
        kernel,
        grid_spec=pltpu.PrefetchScalarGridSpec(
            num_scalar_prefetch=1,
            grid=grid,
            in_specs=in_specs,
            out_specs=out_specs,
            scratch_shapes=list(scratch),
        ),
        out_shape=out_shape,
        compiler_params=params(mib),
        cost_estimate=pl.CostEstimate(flops=flops, bytes_accessed=12 * MIB, transcendentals=0),
    )(scalar, *args)


def per_device(tokens, w_query, w_key, w_value, w_out, gain):
    slabs = lax.axis_size("seq")
    layers = lax.axis_size("z")
    groups = 2 * layers
    my_slab = lax.axis_index("seq")
    core = lax.axis_index("core").astype(jnp.int32)
    layer = lax.axis_index("z").astype(jnp.int32)
    which = core.reshape(1)
    width = tokens.shape[1]
    rows = tokens.shape[0] // groups
    model, value_width = w_value.shape
    part = model // slabs
    per_group = HEADS // groups
    heads = HEADS // 2
    narrow = w_query.shape[1]
    swap = [(0, 1), (1, 0)]

    first, second, first_bias, second_bias, scale = feature_tables()
    sides = [stacked(first, per_group), stacked(second, per_group)]
    key_table = jnp.asarray(np.concatenate(sides, axis=1), BF16)
    repeat = HELD // 2
    key_bias = jnp.asarray(np.stack([np.tile(first_bias, repeat), np.tile(second_bias, repeat)], axis=1))
    wide = 2 * LANES
    query_table = np.zeros((HELD, LANES, 2 * wide), np.float32)
    query_bias = np.zeros((1, 2 * wide), np.float32)
    query_table[:, :, :PACKED] = placed(first * scale)
    query_table[:, :, wide : wide + PACKED] = placed(second)
    query_bias[0, :PACKED] = first_bias * scale
    query_bias[0, wide : wide + PACKED] = second_bias
    query_table, query_bias = jnp.asarray(query_table, BF16), jnp.asarray(query_bias)
    gain_mine = lax.dynamic_index_in_dim(gain.reshape(layers, 2, value_width), core, 1, False)
    gain_mine = gain_mine.reshape(1, layers * value_width)

    flip = lambda m: [(s, s ^ m) for s in range(slabs)]
    turn = lambda d: [(z, (z + d) % layers) for z in range(layers)]
    anywhere = pl.BlockSpec(memory_space=pl.ANY)
    vmem = pl.BlockSpec(memory_space=pltpu.VMEM)
    at = jnp.stack([core, layer, my_slab.astype(jnp.int32)])

    value_part = lax.dynamic_slice_in_dim(w_value, my_slab * part, part, 0)
    blocks = tokens.reshape(layers, 2 * rows, width)
    sent = [lax.dynamic_index_in_dim(blocks, lax.rem(layer + d, layers), 0, False) for d in range(layers)]
    stack = jnp.stack([lax.ppermute(value_part, "z", turn(-d)) for d in range(1, layers)])
    stack, sent, at = lax.optimization_barrier((stack, sent, at))
    if slabs == 4:
        weights = [stack] + [lax.ppermute(stack, "seq", flip(m)) for m in range(1, slabs)]
    else:
        weights = [lax.all_gather(stack, "seq", axis=0, tiled=False)]
    far = layers // 2
    mine = {d: lax.ppermute(sent[d], "z", turn(d)) for d in [far] + [d for d in range(1, layers) if d != far]}
    mine = [sent[0]] + [mine[d] for d in range(1, layers)]
    mine[1:], weights[1:] = lax.optimization_barrier((mine[1:], weights[1:]))
    other = [lax.ppermute(piece, "core", swap) for piece in mine]

    query, key, value, early, total = call(
        lambda at_ref, *refs: project_kernel(at_ref, per_group, layers, slabs != 4, *refs),
        at,
        (1,),
        [pl.BlockSpec((1, 2 * rows, width), lambda i, at: (at[1], 0, 0))]
        + [whole((2 * rows, width))] * (2 * layers - 1)
        + [
            pl.BlockSpec((1,) + key_table.shape[1:], lambda i, at: (at[0], 0, 0)),
            whole(key_bias.shape),
        ]
        + [anywhere] * (3 + len(weights)),
        [
            whole((2, rows, narrow)),
            whole((2, rows, narrow)),
            whole((2, rows, layers * value_width)),
            whole((heads, PACKED, HEAD_DIM)),
            whole((heads, PACKED, HEAD_DIM)),
        ],
        [
            jax.ShapeDtypeStruct((2, rows, narrow), BF16),
            jax.ShapeDtypeStruct((2, rows, narrow), BF16),
            jax.ShapeDtypeStruct((2, rows, layers * value_width), BF16),
            jax.ShapeDtypeStruct((heads, PACKED, HEAD_DIM), BF16),
            jax.ShapeDtypeStruct((heads, PACKED, HEAD_DIM), BF16),
        ],
        (blocks, *mine[1:], *other, key_table, key_bias, w_query, w_key, w_value, *weights),
        4 * rows * model * (model // 2 + 2 * narrow),
        [
            pltpu.VMEM((2 * rows, model), BF16),
            pltpu.VMEM((model, 2 * narrow), BF16),
            pltpu.VMEM((layers // 2, model, 2 * value_width), BF16),
            pltpu.VMEM((2, heads * PACKED, rows), BF16),
            pltpu.SemaphoreType.DMA((3 + (layers - 1) * slabs,)),
        ],
    )

    def local(offset, count):
        return call(
            lambda core_ref, *refs: local_kernel(core_ref, per_group, offset, *refs),
            at,
            (count,),
            [
                whole((2, rows, narrow)),
                whole((2, rows, narrow)),
                pl.BlockSpec((2, rows, HEAD_DIM), lambda i, _: (0, 0, i + offset)),
                pl.BlockSpec((1, PACKED, HEAD_DIM), lambda i, _: (i + offset, 0, 0)),
                whole(query_table.shape),
                whole(query_bias.shape),
            ],
            [
                pl.BlockSpec((2, rows, HEAD_DIM), lambda i, _: (0, 0, i)),
                pl.BlockSpec((2, 1, rows, PACKED), lambda i, _: (0, i, 0, 0)),
            ],
            [
                jax.ShapeDtypeStruct((2, rows, count * HEAD_DIM), F32),
                jax.ShapeDtypeStruct((2, count, rows, PACKED), BF16),
            ],
            (query, key, value, early, query_table, query_bias),
            count * rows * rows * 1200,
        )

    own = total.reshape(layers, per_group, PACKED, HEAD_DIM)
    line = lax.all_to_all(own, "z", split_axis=0, concat_axis=0, tiled=True)
    locals_ = [local(0, 3 * heads // 4)]
    line, locals_ = lax.optimization_barrier((line, locals_))
    slab_total = jnp.sum(line.astype(F32), axis=0).astype(BF16)
    totals = [lax.ppermute(slab_total, "seq", flip(m)) for m in range(1, slabs)]
    piece_shape = (per_group, PACKED, HEAD_DIM)
    prefix = pl.pallas_call(
        prefix_kernel,
        in_specs=[pl.BlockSpec(memory_space=pltpu.SMEM)] + [vmem] * slabs,
        out_specs=[vmem] * layers,
        out_shape=[jax.ShapeDtypeStruct(piece_shape, BF16)] * layers,
        scratch_shapes=[pltpu.VMEM((layers,) + piece_shape, BF16)],
    )(at, line, *totals)
    prefix = [prefix[0]] + [lax.ppermute(prefix[d], "z", turn(-d)) for d in range(1, layers)]
    locals_ = locals_ + [local(3 * heads // 4, heads // 4)]

    def hidden(chunk):
        some = rows // 2
        specs, arrays = [], []
        for num, phi in locals_:
            count = phi.shape[1]
            specs.append(pl.BlockSpec((1, some, count * HEAD_DIM), lambda i, _: (chunk, i, 0)))
            specs.append(pl.BlockSpec((1, count, some, PACKED), lambda i, _: (chunk, 0, i, 0)))
            arrays += [num, phi]
        return call(
            lambda at_ref, *refs: hidden_kernel(at_ref, layers, *refs),
            at,
            (2,),
            [whole((1, heads * HEAD_DIM))] + [whole(piece_shape)] * layers + specs,
            pl.BlockSpec((some, heads * HEAD_DIM), lambda i, _: (i, 0)),
            jax.ShapeDtypeStruct((rows, heads * HEAD_DIM), BF16),
            (gain_mine, *prefix, *arrays),
            rows * heads * HEAD_DIM * 600,
            [pltpu.VMEM((layers,) + piece_shape, BF16)],
            mib=16,
        )

    w_rows = w_out.reshape(layers, 2, value_width, model)

    def project_out(kept, received, to):
        block = (layers, 1, value_width, width)
        specs = []
        for d in to:
            columns = lambda at, d=d: 2 * lax.rem(at[1] + d, layers) + at[0]
            specs.append(pl.BlockSpec(block, lambda i, at, columns=columns: (0, at[0], 0, columns(at))))
            specs.append(pl.BlockSpec(block, lambda i, at, columns=columns: (0, 1 - at[0], 0, columns(at))))
        return call(
            output_kernel,
            at,
            (1,),
            [whole((rows, heads * HEAD_DIM))] * 2 + specs,
            [whole((rows, width))] * len(to),
            [jax.ShapeDtypeStruct((rows, width), BF16)] * len(to),
            (kept, received, *[w_rows] * len(specs)),
            2 * rows * model * width * len(to),
            mib=20,
        )

    kept = [hidden(chunk) for chunk in range(2)]
    received = [lax.ppermute(half, "core", swap) for half in kept]
    order = [far] + [d for d in range(1, layers) if d != far] + [0]
    pieces = {}
    for start in range(0, layers, 2):
        to = order[start : start + 2]
        for chunk in range(2):
            for d, piece in zip(to, project_out(kept[chunk], received[chunk], to)):
                pieces[d, chunk] = lax.ppermute(piece, "z", turn(d)) if d else piece
    return call(
        place_kernel,
        at,
        (1,),
        [vmem] * (2 * layers),
        anywhere,
        jax.ShapeDtypeStruct((groups * rows, width), BF16),
        tuple(pieces[d, chunk] for d in range(layers) for chunk in range(2)),
        0,
        [pltpu.SemaphoreType.DMA((2 * layers,))],
        mib=8,
    )


def solution(mesh):
    slabs, groups = mesh.shape["seq"], mesh.shape["chan"]
    split = jax.sharding.Mesh(mesh.devices.reshape(slabs, groups // 2, 2), ("seq", "z", "core"))
    chan = ("z", "core")
    return jax.shard_map(
        per_device,
        mesh=split,
        in_specs=(P("seq", chan), P(), P(), P(None, chan), P(), P()),
        out_specs=P("seq", chan),
        check_vma=False,
    )
```

```python
import jax
import jax.numpy as jnp
import numpy as np
from jax import lax
from jax.experimental import pallas as pl
from jax.experimental.pallas import tpu as pltpu
from jax.sharding import PartitionSpec as P

HEADS = 16
FEAT = 16
HEAD_DIM = 128
PACKED = 160
LANES = 128
HELD = LANES // FEAT
MIB = 1024 * 1024

F32 = jnp.float32
BF16 = jnp.bfloat16
NN = (((1,), (0,)), ((), ()))
NT = (((1,), (1,)), ((), ()))


def dot(a, b, dims=NN):
    return lax.dot_general(a, b, dims, preferred_element_type=F32)


def feature_tables():
    first = np.zeros((FEAT, PACKED), np.float32)
    second = np.zeros((FEAT, PACKED), np.float32)
    first_bias = np.zeros((PACKED,), np.float32)
    second_bias = np.zeros((PACKED,), np.float32)
    scale = np.zeros((PACKED,), np.float32)
    first_bias[0] = second_bias[0] = scale[0] = 1.0
    place = 1
    for i in range(FEAT):
        first[i, place] = 1.0
        second_bias[place] = 1.0
        scale[place] = 1.0 / 4.0
        place += 1
    for i in range(FEAT):
        for j in range(i, FEAT):
            first[i, place] = 1.0
            second[j, place] = 1.0
            scale[place] = 1.0 / 32.0 if i == j else 1.0 / 16.0
            place += 1
    return first, second, first_bias, second_bias, scale


def placed(table):
    out = np.zeros((HELD, LANES, PACKED), np.float32)
    for place in range(HELD):
        out[place, place * FEAT : (place + 1) * FEAT] = table
    return out


def stacked(table, per_group):
    every = placed(table).transpose(0, 2, 1)
    own = [[p for p in range(HELD) if (p // per_group) % 2 == core] for core in range(2)]
    return np.stack([every[places].reshape(-1, LANES) for places in own])


def project_kernel(at_ref, per_group, layers, gathered, *refs):
    mine, other = refs[:layers], refs[layers : 2 * layers]
    table_ref, bias_ref, wq_ref, wk_ref, own_ref = refs[2 * layers : 2 * layers + 5]
    rest = refs[2 * layers + 5 :]
    weights, rest = rest[:-10], rest[-10:]
    q_ref, k_ref, v_ref, early_ref, total_ref, row_ref, narrow_ref, w_ref, phi_ref, sems = rest
    core, layer, slab = at_ref[0], at_ref[1], at_ref[2]
    both, width = other[0].shape
    rows = both // 2
    model = row_ref.shape[1]
    part = weights[0].shape[-2]
    block = v_ref.shape[2] // layers
    narrow = wq_ref.shape[1]
    copies = []

    def fetch(slot, source, to):
        copies.append((slot, pltpu.make_async_copy(source, to, sems.at[len(copies)])))
        copies[-1][1].start()

    fetch(-1, wq_ref, narrow_ref.at[:, pl.ds(0, narrow)])
    fetch(-1, wk_ref, narrow_ref.at[:, pl.ds(narrow, narrow)])
    fetch(0, own_ref, w_ref.at[0, :, pl.ds(0, block)])
    for d in range(1, layers):
        for m in range(model // part):
            if gathered:
                source, start = weights[0].at[m, d - 1], m * part
            else:
                source, start = weights[m].at[d - 1], pl.multiple_of((slab ^ m) * part, part)
            fetch(d, source, w_ref.at[d // 2, pl.ds(start, part), pl.ds((d % 2) * block, block)])

    def arrived(slots):
        for slot, copy in copies:
            if slot in slots:
                copy.wait()

    for d in range(layers):
        z = lax.rem(layer + layers - d, layers)
        here = pl.multiple_of((2 * z + core) * width, width)
        there = pl.multiple_of((2 * z + 1 - core) * width, width)
        row_ref[:, pl.ds(here, width)] = mine[d][0] if d == 0 else mine[d][...]
        row_ref[:, pl.ds(there, width)] = other[d][...]
    arrived((-1,))
    half = table_ref.shape[1] // 2
    both_narrow = dot(row_ref[...], narrow_ref[...]).astype(BF16)
    for chunk in range(2):
        at = slice(chunk * rows, (chunk + 1) * rows)
        q_ref[chunk] = both_narrow[at, :narrow]
        k_ref[chunk] = both_narrow[at, narrow:]
        for lanes in range(0, narrow, LANES):
            product = dot(table_ref[0], both_narrow[at, narrow + lanes : narrow + lanes + LANES], NT)
            left = product[:half] + bias_ref[:, 0:1]
            right = product[half:] + bias_ref[:, 1:2]
            to = (lanes // LANES) * half
            phi_ref[chunk, to : to + half, :] = (left * right).astype(BF16)

    for pair in range(layers // 2):
        arrived((2 * pair, 2 * pair + 1))
        value = dot(row_ref[...], w_ref[pair]).astype(BF16)
        for d in (2 * pair, 2 * pair + 1):
            z = lax.rem(layer + d, layers)
            side = (d % 2) * block
            lanes = pl.multiple_of(z * block, block)
            for chunk in range(2):
                at = slice(chunk * rows, (chunk + 1) * rows)
                v_ref[chunk, :, pl.ds(lanes, block)] = value[at, side : side + block]
            for i in range(per_group):
                head = z * per_group + i
                place = pl.multiple_of(head * PACKED, PACKED)
                column = side + i * HEAD_DIM
                early = dot(phi_ref[0, pl.ds(place, PACKED), :], value[:rows, column : column + HEAD_DIM])
                late = dot(phi_ref[1, pl.ds(place, PACKED), :], value[rows:, column : column + HEAD_DIM])
                early_ref[head] = early.astype(BF16)
                total_ref[head] = (early + late).astype(BF16)


def local_kernel(at_ref, per_group, offset, q_ref, k_ref, v_ref, early_ref, table_ref, bias_ref, num_ref, phi_ref):
    rows = q_ref.shape[1]
    cut = LANES * -(-rows // (2 * LANES))
    wide = table_ref.shape[2] // 2
    local_head = pl.program_id(0) + offset
    head = (2 * (local_head // per_group) + at_ref[0]) * per_group + lax.rem(local_head, per_group)
    lanes = pl.multiple_of((head // HELD) * LANES, LANES)
    place = lax.rem(head, HELD)
    lane = lax.broadcasted_iota(jnp.int32, (rows, LANES), 1) // FEAT
    for chunk in range(2):
        query = q_ref[chunk, :, pl.ds(lanes, LANES)]
        key = k_ref[chunk, :, pl.ds(lanes, LANES)]
        sides = dot(query, table_ref[place]) + bias_ref[...]
        phi = (sides[:, :PACKED] * sides[:, wide : wide + PACKED]).astype(BF16)
        phi_ref[chunk, 0] = phi
        mine = jnp.where(lane == place, query * jnp.asarray(0.25, BF16), jnp.zeros_like(query))
        for low, high in ((0, cut), (cut, rows)):
            span = high - low
            s = dot(mine[low:high], key[low:high], NT)
            t_at = lax.broadcasted_iota(jnp.int32, (span, span), 0)
            j_at = lax.broadcasted_iota(jnp.int32, (span, span), 1)
            weight = jnp.where(t_at >= j_at, (0.5 * s + 1.0) * s + 1.0, 0.0).astype(BF16)
            num = dot(weight, v_ref[chunk, low:high, :])
            if low > 0:
                s = dot(mine[low:high], key[:low], NT)
                weight = ((0.5 * s + 1.0) * s + 1.0).astype(BF16)
                num = num + dot(weight, v_ref[chunk, :low, :])
            if chunk > 0:
                num = num + dot(phi[low:high], early_ref[0])
            num_ref[chunk, low:high, :] = num


def prefix_kernel(at_ref, line_ref, *refs):
    layers = line_ref.shape[0]
    totals, outs, sum_ref = refs[: -layers - 1], refs[-layers - 1 : -1], refs[-1]
    layer, slab = at_ref[1], at_ref[2]
    run = jnp.zeros(line_ref.shape[1:], F32)
    for m, total in enumerate(totals, 1):
        run = run + total[...].astype(F32) * jnp.where((slab ^ m) < slab, 1.0, 0.0)
    for z in range(layers):
        sum_ref[z] = run.astype(BF16)
        run = run + line_ref[z].astype(F32)
    for d in range(layers):
        outs[d][...] = sum_ref[lax.rem(layer + layers - d, layers)]


def hidden_kernel(at_ref, layers, gain_ref, *refs):
    pieces, parts, out_ref, state_ref = refs[:layers], refs[layers:-2], refs[-2], refs[-1]
    group = pieces[0].shape[0]
    for d in range(layers):
        state_ref[lax.rem(at_ref[1] + d, layers)] = pieces[d][...]
    head = 0
    for num_ref, phi_ref in zip(parts[0::2], parts[1::2]):
        for i in range(phi_ref.shape[1]):
            columns = slice(head * HEAD_DIM, (head + 1) * HEAD_DIM)
            num = num_ref[0, :, i * HEAD_DIM : (i + 1) * HEAD_DIM]
            num = num + dot(phi_ref[0, i], state_ref[head // group, head % group])
            mean_square = jnp.mean(num * num, axis=1, keepdims=True)
            hidden = num * lax.rsqrt(mean_square + 1e-05) * gain_ref[:, columns]
            out_ref[:, columns] = hidden.astype(BF16)
            head += 1


def output_kernel(at_ref, mine_ref, other_ref, *refs):
    outs = refs[len(refs) * 2 // 3 :]
    weights = [w[...].reshape(mine_ref.shape[1], -1) for w in refs[: 2 * len(outs)]]
    width = weights[0].shape[1]
    part = dot(mine_ref[...], jnp.concatenate(weights[0::2], axis=1))
    part = part + dot(other_ref[...], jnp.concatenate(weights[1::2], axis=1))
    for i, out_ref in enumerate(outs):
        out_ref[...] = part[:, i * width : (i + 1) * width].astype(BF16)


def place_kernel(at_ref, *refs):
    pieces, out_ref, sems = refs[:-2], refs[-2], refs[-1]
    layers = len(pieces) // 2
    copies = []
    for i, piece in enumerate(pieces):
        rows = piece.shape[0]
        z = lax.rem(at_ref[1] + layers - i // 2, layers)
        to = out_ref.at[pl.ds(pl.multiple_of((2 * z + i % 2) * rows, rows), rows)]
        copies.append(pltpu.make_async_copy(piece, to, sems.at[i]))
    for copy in copies:
        copy.start()
    for copy in copies:
        copy.wait()


def whole(shape):
    return pl.BlockSpec(shape, lambda *_: (0,) * len(shape))


def params(mib):
    return pltpu.CompilerParams(vmem_limit_bytes=mib * MIB)


def call(kernel, scalar, grid, in_specs, out_specs, out_shape, args, flops, scratch=(), mib=60):
    return pl.pallas_call(
        kernel,
        grid_spec=pltpu.PrefetchScalarGridSpec(
            num_scalar_prefetch=1,
            grid=grid,
            in_specs=in_specs,
            out_specs=out_specs,
            scratch_shapes=list(scratch),
        ),
        out_shape=out_shape,
        compiler_params=params(mib),
        cost_estimate=pl.CostEstimate(flops=flops, bytes_accessed=12 * MIB, transcendentals=0),
    )(scalar, *args)


def per_device(tokens, w_query, w_key, w_value, w_out, gain):
    slabs = lax.axis_size("seq")
    layers = lax.axis_size("z")
    groups = 2 * layers
    my_slab = lax.axis_index("seq")
    core = lax.axis_index("core").astype(jnp.int32)
    layer = lax.axis_index("z").astype(jnp.int32)
    which = core.reshape(1)
    width = tokens.shape[1]
    rows = tokens.shape[0] // groups
    model, value_width = w_value.shape
    part = model // slabs
    per_group = HEADS // groups
    heads = HEADS // 2
    narrow = w_query.shape[1]
    swap = [(0, 1), (1, 0)]

    first, second, first_bias, second_bias, scale = feature_tables()
    sides = [stacked(first, per_group), stacked(second, per_group)]
    key_table = jnp.asarray(np.concatenate(sides, axis=1), BF16)
    repeat = HELD // 2
    key_bias = jnp.asarray(np.stack([np.tile(first_bias, repeat), np.tile(second_bias, repeat)], axis=1))
    wide = 2 * LANES
    query_table = np.zeros((HELD, LANES, 2 * wide), np.float32)
    query_bias = np.zeros((1, 2 * wide), np.float32)
    query_table[:, :, :PACKED] = placed(first * scale)
    query_table[:, :, wide : wide + PACKED] = placed(second)
    query_bias[0, :PACKED] = first_bias * scale
    query_bias[0, wide : wide + PACKED] = second_bias
    query_table, query_bias = jnp.asarray(query_table, BF16), jnp.asarray(query_bias)
    gain_mine = lax.dynamic_index_in_dim(gain.reshape(layers, 2, value_width), core, 1, False)
    gain_mine = gain_mine.reshape(1, layers * value_width)

    flip = lambda m: [(s, s ^ m) for s in range(slabs)]
    turn = lambda d: [(z, (z + d) % layers) for z in range(layers)]
    anywhere = pl.BlockSpec(memory_space=pl.ANY)
    vmem = pl.BlockSpec(memory_space=pltpu.VMEM)
    at = jnp.stack([core, layer, my_slab.astype(jnp.int32)])

    value_part = lax.dynamic_slice_in_dim(w_value, my_slab * part, part, 0)
    blocks = tokens.reshape(layers, 2 * rows, width)
    sent = [lax.dynamic_index_in_dim(blocks, lax.rem(layer + d, layers), 0, False) for d in range(layers)]
    stack = jnp.stack([lax.ppermute(value_part, "z", turn(-d)) for d in range(1, layers)])
    stack, sent, at = lax.optimization_barrier((stack, sent, at))
    if slabs == 4:
        weights = [stack] + [lax.ppermute(stack, "seq", flip(m)) for m in range(1, slabs)]
    else:
        weights = [lax.all_gather(stack, "seq", axis=0, tiled=False)]
    far = layers // 2
    mine = {d: lax.ppermute(sent[d], "z", turn(d)) for d in [far] + [d for d in range(1, layers) if d != far]}
    mine = [sent[0]] + [mine[d] for d in range(1, layers)]
    mine[1:], weights[1:] = lax.optimization_barrier((mine[1:], weights[1:]))
    other = [lax.ppermute(piece, "core", swap) for piece in mine]

    query, key, value, early, total = call(
        lambda at_ref, *refs: project_kernel(at_ref, per_group, layers, slabs != 4, *refs),
        at,
        (1,),
        [pl.BlockSpec((1, 2 * rows, width), lambda i, at: (at[1], 0, 0))]
        + [whole((2 * rows, width))] * (2 * layers - 1)
        + [
            pl.BlockSpec((1,) + key_table.shape[1:], lambda i, at: (at[0], 0, 0)),
            whole(key_bias.shape),
        ]
        + [anywhere] * (3 + len(weights)),
        [
            whole((2, rows, narrow)),
            whole((2, rows, narrow)),
            whole((2, rows, layers * value_width)),
            whole((heads, PACKED, HEAD_DIM)),
            whole((heads, PACKED, HEAD_DIM)),
        ],
        [
            jax.ShapeDtypeStruct((2, rows, narrow), BF16),
            jax.ShapeDtypeStruct((2, rows, narrow), BF16),
            jax.ShapeDtypeStruct((2, rows, layers * value_width), BF16),
            jax.ShapeDtypeStruct((heads, PACKED, HEAD_DIM), BF16),
            jax.ShapeDtypeStruct((heads, PACKED, HEAD_DIM), BF16),
        ],
        (blocks, *mine[1:], *other, key_table, key_bias, w_query, w_key, w_value, *weights),
        4 * rows * model * (model // 2 + 2 * narrow),
        [
            pltpu.VMEM((2 * rows, model), BF16),
            pltpu.VMEM((model, 2 * narrow), BF16),
            pltpu.VMEM((layers // 2, model, 2 * value_width), BF16),
            pltpu.VMEM((2, heads * PACKED, rows), BF16),
            pltpu.SemaphoreType.DMA((3 + (layers - 1) * slabs,)),
        ],
    )

    def local(offset, count):
        return call(
            lambda core_ref, *refs: local_kernel(core_ref, per_group, offset, *refs),
            at,
            (count,),
            [
                whole((2, rows, narrow)),
                whole((2, rows, narrow)),
                pl.BlockSpec((2, rows, HEAD_DIM), lambda i, _: (0, 0, i + offset)),
                pl.BlockSpec((1, PACKED, HEAD_DIM), lambda i, _: (i + offset, 0, 0)),
                whole(query_table.shape),
                whole(query_bias.shape),
            ],
            [
                pl.BlockSpec((2, rows, HEAD_DIM), lambda i, _: (0, 0, i)),
                pl.BlockSpec((2, 1, rows, PACKED), lambda i, _: (0, i, 0, 0)),
            ],
            [
                jax.ShapeDtypeStruct((2, rows, count * HEAD_DIM), F32),
                jax.ShapeDtypeStruct((2, count, rows, PACKED), BF16),
            ],
            (query, key, value, early, query_table, query_bias),
            count * rows * rows * 1200,
            mib=44,
        )

    own = total.reshape(layers, per_group, PACKED, HEAD_DIM)
    line = lax.all_to_all(own, "z", split_axis=0, concat_axis=0, tiled=True)
    locals_ = [local(0, 3 * heads // 4)]
    line, locals_ = lax.optimization_barrier((line, locals_))
    slab_total = jnp.sum(line.astype(F32), axis=0).astype(BF16)
    totals = [lax.ppermute(slab_total, "seq", flip(m)) for m in range(1, slabs)]
    piece_shape = (per_group, PACKED, HEAD_DIM)
    prefix = pl.pallas_call(
        prefix_kernel,
        in_specs=[pl.BlockSpec(memory_space=pltpu.SMEM)] + [vmem] * slabs,
        out_specs=[vmem] * layers,
        out_shape=[jax.ShapeDtypeStruct(piece_shape, BF16)] * layers,
        scratch_shapes=[pltpu.VMEM((layers,) + piece_shape, BF16)],
    )(at, line, *totals)
    prefix = [prefix[0]] + [lax.ppermute(prefix[d], "z", turn(-d)) for d in range(1, layers)]
    locals_ = locals_ + [local(3 * heads // 4, heads // 4)]

    def hidden(chunk):
        some = rows // 2
        specs, arrays = [], []
        for num, phi in locals_:
            count = phi.shape[1]
            specs.append(pl.BlockSpec((1, some, count * HEAD_DIM), lambda i, _: (chunk, i, 0)))
            specs.append(pl.BlockSpec((1, count, some, PACKED), lambda i, _: (chunk, 0, i, 0)))
            arrays += [num, phi]
        return call(
            lambda at_ref, *refs: hidden_kernel(at_ref, layers, *refs),
            at,
            (2,),
            [whole((1, heads * HEAD_DIM))] + [whole(piece_shape)] * layers + specs,
            pl.BlockSpec((some, heads * HEAD_DIM), lambda i, _: (i, 0)),
            jax.ShapeDtypeStruct((rows, heads * HEAD_DIM), BF16),
            (gain_mine, *prefix, *arrays),
            rows * heads * HEAD_DIM * 600,
            [pltpu.VMEM((layers,) + piece_shape, BF16)],
            mib=16,
        )

    w_rows = w_out.reshape(layers, 2, value_width, model)

    def project_out(kept, received, to):
        block = (layers, 1, value_width, width)
        specs = []
        for d in to:
            columns = lambda at, d=d: 2 * lax.rem(at[1] + d, layers) + at[0]
            specs.append(pl.BlockSpec(block, lambda i, at, columns=columns: (0, at[0], 0, columns(at))))
            specs.append(pl.BlockSpec(block, lambda i, at, columns=columns: (0, 1 - at[0], 0, columns(at))))
        return call(
            output_kernel,
            at,
            (1,),
            [whole((rows, heads * HEAD_DIM))] * 2 + specs,
            [whole((rows, width))] * len(to),
            [jax.ShapeDtypeStruct((rows, width), BF16)] * len(to),
            (kept, received, *[w_rows] * len(specs)),
            2 * rows * model * width * len(to),
            mib=20,
        )

    kept = [hidden(chunk) for chunk in range(2)]
    received = [lax.ppermute(half, "core", swap) for half in kept]
    order = [far] + [d for d in range(1, layers) if d != far] + [0]
    pieces = {}
    for start in range(0, layers, 2):
        to = order[start : start + 2]
        for chunk in range(2):
            for d, piece in zip(to, project_out(kept[chunk], received[chunk], to)):
                pieces[d, chunk] = lax.ppermute(piece, "z", turn(d)) if d else piece
    return call(
        place_kernel,
        at,
        (1,),
        [vmem] * (2 * layers),
        anywhere,
        jax.ShapeDtypeStruct((groups * rows, width), BF16),
        tuple(pieces[d, chunk] for d in range(layers) for chunk in range(2)),
        0,
        [pltpu.SemaphoreType.DMA((2 * layers,))],
        mib=8,
    )


def solution(mesh):
    slabs, groups = mesh.shape["seq"], mesh.shape["chan"]
    split = jax.sharding.Mesh(mesh.devices.reshape(slabs, groups // 2, 2), ("seq", "z", "core"))
    chan = ("z", "core")
    return jax.shard_map(
        per_device,
        mesh=split,
        in_specs=(P("seq", chan), P(), P(), P(None, chan), P(), P()),
        out_specs=P("seq", chan),
        check_vma=False,
    )
```
